32 devices in a mesh: batch: 16 (over z, x, core), hid: 2 (over y).
Axes of the slice: x: 2, y: 2, z: 4, core: 2. Of those that a mesh axis runs over, the one named last changes fastest.
Arguments:
- tokens: bfloat16 [4096, 2048], P(('batch', 'hid')), may hold values from -6 to 6
- lengths: int32 [32, 4], P(('batch', 'hid')), may hold values from 0 to 128, as said below
- attention_gain: bfloat16 [2048], P('batch'), may hold values from 0.5 to 1.5
- query_down: bfloat16 [2048, 1024], P('batch'), may hold values from -0.125 to 0.125
- query_gain: bfloat16 [1024], P('batch'), may hold values from 0.5 to 1.5
- query_up: bfloat16 [1024, 4096], P('batch'), may hold values from -0.1875 to 0.1875
- key_value: bfloat16 [2048, 512], P('batch'), may hold values from -0.125 to 0.125
- output_weight: bfloat16 [2048, 4096], P('batch'), may hold values from -0.75 to 0.75
- feed_gain: bfloat16 [2048], P('batch'), may hold values from 0.5 to 1.5
- gate_weight: bfloat16 [2048, 5632], P('batch', 'hid'), may hold values from -0.125 to 0.125
- up_weight: bfloat16 [2048, 5632], P('batch', 'hid'), may hold values from -0.125 to 0.125
- down_weight: bfloat16 [2048, 5632], P('batch', 'hid'), may hold values from -0.078125 to 0.078125
- cotangent: bfloat16 [4096, 2048], P(('batch', 'hid')), may hold values from -6 to 6
Outputs:
- output: bfloat16 [4096, 2048], P(('batch', 'hid'))
- grad_tokens: bfloat16 [4096, 2048], P(('batch', 'hid'))
- grad_attention_gain: float32 [2048], P('batch')
- grad_query_down: float32 [2048, 1024], P('batch')
- grad_query_gain: float32 [1024], P('batch')
- grad_query_up: float32 [1024, 4096], P('batch')
- grad_key_value: float32 [2048, 512], P('batch')
- grad_output_weight: float32 [2048, 4096], P('batch')
- grad_feed_gain: float32 [2048], P('batch')
- grad_gate: float32 [2048, 5632], P('batch', 'hid')
- grad_up: float32 [2048, 5632], P('batch', 'hid')
- grad_down: float32 [2048, 5632], P('batch', 'hid')
The draws below stay inside these ranges and needn't reach their ends.
Inputs may be any that keep to these rules, and one draw needn't show every extreme that they name: Row g holds the lengths of the sequences of device group g in order; used slots hold 32 or more and come first, the rest hold 0; a row sums to 32 to 128; in every draw some row holds one sequence of 128 tokens.
All inputs are finite; a program needn't handle non-finite values.
Results may differ from the reference program's by a relative error of at most 0.017.
Values may be sent and summed in bfloat16 or wider, within the bound.
A program may use at most 320 MiB of HBM per device.

```python
import jax
import jax.numpy as jnp
from jax import lax

D = 2048
QR = 1024
HEADS = 16
HEAD_DIM = 256
FF = 5632
SLOTS = 4
TOK_DEV = 128
LEN_MIN = 32
SHARDS = 32
TOKENS = 4096
N_BATCH = 16
N_HID = 2


def draw_lengths(key, part):
    key = jax.random.fold_in(key, 7)
    keys = jax.random.split(key, 4)
    groups = SHARDS
    totals = jax.random.randint(keys[0], (groups,), LEN_MIN, TOK_DEV + 1)
    full_group = jax.random.randint(keys[1], (), 0, groups)
    is_full = jnp.arange(groups) == full_group
    totals = jnp.where(is_full, TOK_DEV, totals)
    most_count = jnp.minimum(SLOTS, totals // LEN_MIN)
    counts = jax.random.randint(keys[2], (groups,), 1, most_count + 1)
    counts = jnp.where(is_full, 1, counts)
    spare = totals - counts * LEN_MIN
    cuts = jax.random.randint(keys[3], (groups, SLOTS - 1), 0, spare[:, None] + 1)
    slot_index = jnp.arange(SLOTS - 1)
    cuts = jnp.where(slot_index[None, :] >= counts[:, None] - 1, spare[:, None], cuts)
    cuts = jnp.sort(cuts, axis=1)
    bounds = jnp.concatenate([jnp.zeros((groups, 1), jnp.int32), cuts.astype(jnp.int32), spare[:, None].astype(jnp.int32)], axis=1)
    pieces = bounds[:, 1:] - bounds[:, :-1]
    used = jnp.arange(SLOTS)[None, :] < counts[:, None]
    return (pieces + jnp.where(used, LEN_MIN, 0)).astype(jnp.int32)


def levels(own_key, dims, cuts, least, top_value):
    def one(dim, shards_of):
        draws = jax.random.uniform(jax.random.fold_in(jax.random.fold_in(own_key, 6), dim), (shards_of,), jnp.float32, least / len(cuts), top_value / len(cuts))
        return jnp.repeat(jnp.exp(draws), dims[dim] // shards_of).reshape((-1,) + (1,) * (len(dims) - dim - 1))

    level = one(*cuts[0])
    for cut in cuts[1:]:
        level = level * one(*cut)
    return level


def gaussian(key, shape, scale, limit, cuts=(), kind=jnp.bfloat16):
    array = jax.random.normal(key, shape, jnp.float32) * scale
    if len(cuts) > 0:
        array = levels(key, shape, cuts, -0.22, 0.18) * array
    return jnp.clip(array, min=-limit, max=limit).astype(kind)


def setup_inputs(seed: int = 0) -> dict:
    key_list = jax.random.split(jax.random.key(seed), 14)
    tokens = gaussian(key_list[0], (TOKENS, D), 1.0, 6.0, ((0, 32),))
    lengths = draw_lengths(jax.random.fold_in(key_list[13], 71), 0)
    attention_gain = jnp.clip(1.0 + 0.1 * jax.random.normal(key_list[2], (D,), jnp.float32), 0.5, 1.5).astype(jnp.bfloat16)
    query_down = gaussian(key_list[3], (D, QR), D ** -0.5, 0.125, ((0, 16),))
    query_gain = jnp.clip(1.0 + 0.1 * jax.random.normal(key_list[4], (QR,), jnp.float32), 0.5, 1.5).astype(jnp.bfloat16)
    query_up = gaussian(key_list[5], (QR, HEADS * HEAD_DIM), QR ** -0.5, 0.1875, ((0, 16),))
    key_value = gaussian(key_list[6], (D, 2 * HEAD_DIM), D ** -0.5, 0.125, ((0, 16),))
    output_weight = gaussian(key_list[7], (D, HEADS * HEAD_DIM), (max(HEADS * HEAD_DIM // 64, 16)) ** -0.5, 0.75, ((0, 16),))
    feed_gain = jnp.clip(1.0 + 0.1 * jax.random.normal(key_list[8], (D,), jnp.float32), 0.5, 1.5).astype(jnp.bfloat16)
    gate_weight = gaussian(key_list[9], (D, FF), D ** -0.5, 0.125, ((0, 16), (1, 2)))
    up_weight = gaussian(key_list[10], (D, FF), D ** -0.5, 0.125, ((0, 16), (1, 2)))
    down_weight = gaussian(key_list[11], (D, FF), FF ** -0.5, 0.078125, ((0, 16), (1, 2)))
    cotangent = gaussian(key_list[12], (TOKENS, D), 1.0, 6.0, ((0, 32),))
    return dict(tokens=tokens, lengths=lengths, attention_gain=attention_gain, query_down=query_down, query_gain=query_gain, query_up=query_up, key_value=key_value, output_weight=output_weight, feed_gain=feed_gain, gate_weight=gate_weight, up_weight=up_weight, down_weight=down_weight, cotangent=cotangent)


EPS = 1e-05
ROPE_BASE = 10000.0
NEGATIVE = -1e+30
HIGH = lax.Precision.HIGHEST

@jax.custom_vjp
def low(v):
    return lax.optimization_barrier(v.astype(jnp.bfloat16)).astype(jnp.float32)

@jax.custom_vjp
def low_back(v):
    return v

def low_keep(v):
    return (low(v), None)

def low_pass(kept, grad):
    return (grad,)

def back_keep(v):
    return (v, None)

def back_low(kept, grad):
    return (low(grad),)
low.defvjp(low_keep, low_pass)
low_back.defvjp(back_keep, back_low)

def product(spec, left, right):
    return jnp.einsum(spec, left, right, precision=HIGH)

def norm_rows(values, gain):
    return values * lax.rsqrt(lax.optimization_barrier(jnp.mean(values * values, axis=-1, keepdims=True)) + EPS) * gain

def rotate(values, cosine, sine):
    half = values.shape[-1] // 2
    first = values[..., :half]
    second = values[..., half:]
    return jnp.concatenate([first * cosine - second * sine, second * cosine + first * sine], axis=-1)

def layout(row_lengths, count_rows):
    ends = jnp.cumsum(row_lengths).astype(jnp.int32)
    starts = (ends - row_lengths).astype(jnp.int32)
    places = jnp.arange(count_rows, dtype=jnp.int32)
    segment = lax.optimization_barrier(jnp.sum((places[:, None] >= ends[None, :]).astype(jnp.int32), axis=1))
    begins = jnp.concatenate([starts, ends[-1:]]).astype(jnp.int32)
    labels = jnp.arange(begins.shape[0], dtype=jnp.int32)
    firsts = lax.optimization_barrier(jnp.sum(jnp.where(segment[:, None] == labels[None, :], begins[None, :], 0), axis=1)).astype(jnp.int32)
    position = places - firsts
    valid = places < ends[-1]
    allowed = (segment[:, None] == segment[None, :]) & (places[None, :] <= places[:, None])
    return (position, valid, allowed)

def angles_of(position, head_size):
    half = head_size // 2
    freqs = ROPE_BASE ** (-(jnp.arange(half, dtype=jnp.float32) * 2.0) / head_size)
    angle = position.astype(jnp.float32)[:, None] * freqs[None, :]
    return (jnp.cos(angle), jnp.sin(angle))

def block(params, x_rows, row_lengths):
    attention_gain, query_down, query_gain, query_up, key_value, output_weight, feed_gain, gate_weight, up_weight, down_weight = params
    count_rows = x_rows.shape[0]
    position, valid, allowed = angles_input = layout(row_lengths, count_rows)
    cosine, sine = angles_of(position, HEAD_DIM)
    normed = low(norm_rows(x_rows, attention_gain))
    latent = low_back(product('rd,dc->rc', normed, query_down))
    latent_normed = low(norm_rows(latent, query_gain))
    queries = low_back(product('rc,cf->rf', latent_normed, query_up)).reshape(count_rows, HEADS, HEAD_DIM)
    keyvals = low_back(product('rd,de->re', normed, key_value))
    query_rot = low(rotate(queries, cosine[:, None, :], sine[:, None, :]))
    key_rot = low(rotate(keyvals[:, :HEAD_DIM], cosine, sine))
    value_rows = low(keyvals[:, HEAD_DIM:])
    scores = product('qhd,kd->hqk', query_rot, key_rot) * HEAD_DIM ** (-0.5)
    scores = low_back(jnp.where(allowed[None], scores, NEGATIVE))
    highest = lax.optimization_barrier(jnp.max(scores, axis=-1, keepdims=True))
    raised = jnp.exp(scores - highest)
    probs = low(raised / lax.optimization_barrier(jnp.sum(raised, axis=-1, keepdims=True)))
    mixed = product('hqk,kd->qhd', probs, value_rows).reshape(count_rows, HEADS * HEAD_DIM)
    mixed = low(low_back(mixed))
    branch = low_back(product('rf,df->rd', mixed, output_weight))
    middle = x_rows + branch
    normed_ffn = low(norm_rows(middle, feed_gain))
    gate = low_back(product('rd,df->rf', normed_ffn, gate_weight))
    up = low_back(product('rd,df->rf', normed_ffn, up_weight))
    hidden = low(jax.nn.silu(gate) * up)
    feed = low_back(product('rf,df->rd', hidden, down_weight))
    return jnp.where(valid[:, None], middle + feed, x_rows)

def reference(tokens, lengths, attention_gain, query_down, query_gain, query_up, key_value, output_weight, feed_gain, gate_weight, up_weight, down_weight, cotangent):
    params = tuple((weight.astype(jnp.float32) for weight in (attention_gain, query_down, query_gain, query_up, key_value, output_weight, feed_gain, gate_weight, up_weight, down_weight)))
    groups = N_BATCH * N_HID
    inputs = tokens.astype(jnp.float32).reshape(groups, TOK_DEV, D)
    saved_block = jax.checkpoint(block)

    def forward(weights, rows_all):
        return lax.map(lambda pieces: saved_block(weights, pieces[0], pieces[1]), (rows_all, lengths))
    result, pull = jax.vjp(forward, params, inputs)
    grads, grad_rows = pull(cotangent.astype(jnp.float32).reshape(groups, TOK_DEV, D))
    output = result.reshape(TOKENS, D).astype(jnp.bfloat16)
    grad_tokens = grad_rows.reshape(TOKENS, D).astype(jnp.bfloat16)
    return (output, grad_tokens, grads[0], grads[1], grads[2], grads[3], grads[4], grads[5], grads[6], grads[7], grads[8], grads[9])
```

```python
import jax
import jax.numpy as jnp
from jax import lax
from jax.sharding import PartitionSpec as P

HEADS = 16
HEAD_DIM = 256


EPS = 1e-05
ROPE_BASE = 10000.0
NEGATIVE = -1e30


def matmul(spec, left, right):
    return jnp.einsum(spec, left, right, preferred_element_type=jnp.float32)


def norm_rows(values, gain):
    return values * lax.rsqrt(jnp.mean(values * values, axis=-1, keepdims=True) + EPS) * gain


def rotate(values, cosine, sine):
    half = values.shape[-1] // 2
    first = values[..., :half]
    second = values[..., half:]
    return jnp.concatenate(
        [first * cosine - second * sine, second * cosine + first * sine], axis=-1
    )


def layout(row_lengths, count_rows):
    slots = jnp.arange(row_lengths.shape[0], dtype=jnp.int32)
    ends = jnp.sum(jnp.where(slots[None, :] <= slots[:, None], row_lengths[None, :], 0), axis=1)
    starts = ends - row_lengths
    places = jnp.arange(count_rows, dtype=jnp.int32)
    segment = jnp.sum((places[:, None] >= ends[None, :]).astype(jnp.int32), axis=1)
    begins = jnp.concatenate([starts, ends[-1:]])
    labels = jnp.arange(begins.shape[0], dtype=jnp.int32)
    firsts = jnp.sum(jnp.where(segment[:, None] == labels[None, :], begins[None, :], 0), axis=1)
    position = places - firsts
    valid = places < ends[-1]
    allowed = (segment[:, None] == segment[None, :]) & (places[None, :] <= places[:, None])
    return (position, valid, allowed)


def angles_of(position, head_size):
    half = head_size // 2
    freqs = ROPE_BASE ** (-(jnp.arange(half, dtype=jnp.float32) * 2.0) / head_size)
    angle = position.astype(jnp.float32)[:, None] * freqs[None, :]
    return (jnp.cos(angle), jnp.sin(angle))


def masked_scores(query_rot, key_rot, allowed, scale):
    raw = matmul("qhd,kd->hqk", query_rot, key_rot) * scale
    return jnp.where(allowed[None], raw, NEGATIVE)


def per_device(
    tokens,
    lengths,
    attention_gain,
    query_down,
    query_gain,
    query_up,
    key_value,
    output_weight,
    feed_gain,
    gate_weight,
    up_weight,
    down_weight,
    cotangent,
):
    count_rows = tokens.shape[0]
    scale = HEAD_DIM ** (-0.5)
    norm_gain, latent_weight, latent_gain, query_weight, pair_weight, out_weight, ffn_gain = (
        lax.all_gather(attention_gain, "batch", axis=0, tiled=True),
        lax.all_gather(query_down, "batch", axis=0, tiled=True),
        lax.all_gather(query_gain, "batch", axis=0, tiled=True),
        lax.all_gather(query_up, "batch", axis=0, tiled=True),
        lax.all_gather(key_value, "batch", axis=0, tiled=True),
        lax.all_gather(output_weight, "batch", axis=0, tiled=True),
        lax.all_gather(feed_gain, "batch", axis=0, tiled=True),
    )
    gate_full, up_full, down_full = (
        lax.all_gather(gate_weight, "batch", axis=0, tiled=True),
        lax.all_gather(up_weight, "batch", axis=0, tiled=True),
        lax.all_gather(down_weight, "batch", axis=0, tiled=True),
    )
    inputs = tokens.astype(jnp.float32)
    position, valid, allowed = layout(lengths[0], count_rows)
    cosine, sine = angles_of(position, HEAD_DIM)
    first_gain = norm_gain.astype(jnp.float32)
    second_gain = latent_gain.astype(jnp.float32)
    third_gain = ffn_gain.astype(jnp.float32)
    normed = norm_rows(inputs, first_gain).astype(jnp.bfloat16)
    latent = matmul("rd,dc->rc", normed, latent_weight)
    latent_normed = norm_rows(latent, second_gain).astype(jnp.bfloat16)
    queries = matmul("rc,cf->rf", latent_normed, query_weight).reshape(count_rows, HEADS, HEAD_DIM)
    keyvals = matmul("rd,de->re", normed, pair_weight)
    query_rot = rotate(queries, cosine[:, None, :], sine[:, None, :]).astype(jnp.bfloat16)
    key_rot = rotate(keyvals[:, :HEAD_DIM], cosine, sine).astype(jnp.bfloat16)
    value_rows = keyvals[:, HEAD_DIM:].astype(jnp.bfloat16)
    scores = masked_scores(query_rot, key_rot, allowed, scale)
    highest = jnp.max(scores, axis=-1, keepdims=True)
    raised = jnp.exp(scores - highest)
    totals = jnp.sum(raised, axis=-1, keepdims=True)
    probs = (raised / totals).astype(jnp.bfloat16)
    logsum = highest + jnp.log(totals)
    mixed = (
        matmul("hqk,kd->qhd", probs, value_rows)
        .reshape(count_rows, HEADS * HEAD_DIM)
        .astype(jnp.bfloat16)
    )
    branch = matmul("rf,df->rd", mixed, out_weight)
    middle = inputs + branch
    normed_ffn = norm_rows(middle, third_gain).astype(jnp.bfloat16)
    pair_rows = lax.all_gather(normed_ffn, "hid", axis=0, tiled=True)
    gate = matmul("rd,df->rf", pair_rows, gate_full)
    up = matmul("rd,df->rf", pair_rows, up_full)
    sigma = jax.nn.sigmoid(gate)
    activated = gate * sigma
    slope = sigma * (1.0 + gate * (1.0 - sigma))
    hidden = (activated * up).astype(jnp.bfloat16)
    feed = lax.psum_scatter(
        matmul("rf,df->rd", hidden, down_full).astype(jnp.bfloat16),
        "hid",
        scatter_dimension=0,
        tiled=True,
    ).astype(jnp.float32)
    output = jnp.where(valid[:, None], middle + feed, inputs).astype(jnp.bfloat16)
    upstream = cotangent.astype(jnp.float32)
    kept = jnp.where(valid[:, None], upstream, 0.0)
    pair_grad = lax.all_gather(kept.astype(jnp.bfloat16), "hid", axis=0, tiled=True)
    gate_back, up_back, down_back = (
        lax.all_gather(gate_weight, "batch", axis=0, tiled=True),
        lax.all_gather(up_weight, "batch", axis=0, tiled=True),
        lax.all_gather(down_weight, "batch", axis=0, tiled=True),
    )
    (
        gain_back,
        latent_back_weight,
        latent_gain_back,
        query_back,
        pair_back,
        out_back,
        ffn_gain_back,
    ) = (
        lax.all_gather(attention_gain, "batch", axis=0, tiled=True),
        lax.all_gather(query_down, "batch", axis=0, tiled=True),
        lax.all_gather(query_gain, "batch", axis=0, tiled=True),
        lax.all_gather(query_up, "batch", axis=0, tiled=True),
        lax.all_gather(key_value, "batch", axis=0, tiled=True),
        lax.all_gather(output_weight, "batch", axis=0, tiled=True),
        lax.all_gather(feed_gain, "batch", axis=0, tiled=True),
    )
    hidden_grad = matmul("rd,df->rf", pair_grad, down_back)
    gate_grad = (hidden_grad * up * slope).astype(jnp.bfloat16)
    up_grad = (hidden_grad * activated).astype(jnp.bfloat16)
    grad_down = matmul("rd,rf->df", pair_grad, hidden)
    grad_gate = matmul("rd,rf->df", pair_rows, gate_grad)
    grad_up = matmul("rd,rf->df", pair_rows, up_grad)
    ffn_shares = (
        lax.psum_scatter(grad_gate, "batch", scatter_dimension=0, tiled=True),
        lax.psum_scatter(grad_up, "batch", scatter_dimension=0, tiled=True),
        lax.psum_scatter(grad_down, "batch", scatter_dimension=0, tiled=True),
    )
    ffn_grad = lax.psum_scatter(
        matmul("rf,df->rd", gate_grad, gate_back) + matmul("rf,df->rd", up_grad, up_back),
        "hid",
        scatter_dimension=0,
        tiled=True,
    )
    unused_third, third_pull = jax.vjp(norm_rows, middle, ffn_gain_back.astype(jnp.float32))
    middle_norm_grad, feed_gain_grad = third_pull(ffn_grad)
    middle_grad = kept + middle_norm_grad
    branch_grad = middle_grad.astype(jnp.bfloat16)
    grad_out = matmul("rd,rf->df", branch_grad, mixed)
    mixed_grad = (
        matmul("rd,df->rf", branch_grad, out_back)
        .astype(jnp.bfloat16)
        .reshape(count_rows, HEADS, HEAD_DIM)
    )
    scores_back = masked_scores(query_rot, key_rot, allowed, scale)
    probs_back = jnp.exp(scores_back - logsum)
    prob_grad = matmul("qhd,kd->hqk", mixed_grad, value_rows)
    score_grad = (
        probs_back * (prob_grad - jnp.sum(probs_back * prob_grad, axis=-1, keepdims=True))
    ).astype(jnp.bfloat16)
    value_grad = matmul("hqk,qhd->kd", probs, mixed_grad)
    query_rot_grad = matmul("hqk,kd->qhd", score_grad, key_rot) * scale
    key_rot_grad = matmul("hqk,qhd->kd", score_grad, query_rot) * scale
    query_grad = (
        rotate(query_rot_grad, cosine[:, None, :], -sine[:, None, :])
        .reshape(count_rows, HEADS * HEAD_DIM)
        .astype(jnp.bfloat16)
    )
    key_grad = rotate(key_rot_grad, cosine, -sine)
    keyval_grad = jnp.concatenate([key_grad, value_grad], axis=1).astype(jnp.bfloat16)
    grad_query = matmul("rc,rf->cf", latent_normed, query_grad)
    grad_pair = matmul("rd,re->de", normed, keyval_grad)
    latent_normed_grad = matmul("rf,cf->rc", query_grad, query_back)
    unused_second, second_pull = jax.vjp(norm_rows, latent, latent_gain_back.astype(jnp.float32))
    latent_back, latent_gain_grad = second_pull(latent_normed_grad)
    latent_grad = latent_back.astype(jnp.bfloat16)
    grad_latent = matmul("rd,rc->dc", normed, latent_grad)
    normed_grad = matmul("rc,dc->rd", latent_grad, latent_back_weight) + matmul(
        "re,de->rd", keyval_grad, pair_back
    )
    unused_first, first_pull = jax.vjp(norm_rows, inputs, gain_back.astype(jnp.float32))
    input_norm_grad, norm_gain_grad = first_pull(normed_grad)
    grad_tokens = (middle_grad + input_norm_grad + jnp.where(valid[:, None], 0.0, upstream)).astype(
        jnp.bfloat16
    )
    attention_sums = (
        norm_gain_grad,
        grad_latent,
        latent_gain_grad,
        grad_query,
        grad_pair,
        grad_out,
        feed_gain_grad,
    )
    halves = (
        lax.psum_scatter(attention_sums[0], "batch", scatter_dimension=0, tiled=True),
        lax.psum_scatter(attention_sums[1], "batch", scatter_dimension=0, tiled=True),
        lax.psum_scatter(attention_sums[2], "batch", scatter_dimension=0, tiled=True),
        lax.psum_scatter(attention_sums[3], "batch", scatter_dimension=0, tiled=True),
        lax.psum_scatter(attention_sums[4], "batch", scatter_dimension=0, tiled=True),
        lax.psum_scatter(attention_sums[5], "batch", scatter_dimension=0, tiled=True),
        lax.psum_scatter(attention_sums[6], "batch", scatter_dimension=0, tiled=True),
    )
    shares = (
        lax.psum(halves[0].astype(jnp.bfloat16), "hid").astype(jnp.float32),
        lax.psum(halves[1].astype(jnp.bfloat16), "hid").astype(jnp.float32),
        lax.psum(halves[2].astype(jnp.bfloat16), "hid").astype(jnp.float32),
        lax.psum(halves[3].astype(jnp.bfloat16), "hid").astype(jnp.float32),
        lax.psum(halves[4].astype(jnp.bfloat16), "hid").astype(jnp.float32),
        lax.psum(halves[5].astype(jnp.bfloat16), "hid").astype(jnp.float32),
        lax.psum(halves[6].astype(jnp.bfloat16), "hid").astype(jnp.float32),
    )
    return (
        output,
        grad_tokens,
        shares[0],
        shares[1],
        shares[2],
        shares[3],
        shares[4],
        shares[5],
        shares[6],
        ffn_shares[0],
        ffn_shares[1],
        ffn_shares[2],
    )


def solution(mesh):
    placed = (
        P(("batch", "hid"), None),
        P(("batch", "hid"), None),
        P("batch"),
        P("batch", None),
        P("batch"),
        P("batch", None),
        P("batch", None),
        P("batch", None),
        P("batch"),
        P("batch", "hid"),
        P("batch", "hid"),
        P("batch", "hid"),
        P(("batch", "hid"), None),
    )
    return jax.shard_map(
        per_device,
        mesh=mesh,
        in_specs=placed,
        out_specs=(
            P(("batch", "hid"), None),
            P(("batch", "hid"), None),
            P("batch"),
            P("batch", None),
            P("batch"),
            P("batch", None),
            P("batch", None),
            P("batch", None),
            P("batch"),
            P("batch", "hid"),
            P("batch", "hid"),
            P("batch", "hid"),
        ),
        check_vma=False,
    )
```

```python
import functools

import jax
import jax.numpy as jnp
from jax import lax
from jax.experimental import pallas as pl
from jax.experimental.pallas import tpu as pltpu
from jax.sharding import PartitionSpec as P

HEADS = 16
HEAD_DIM = 256


EPS = 1e-05
ROPE_BASE = 10000.0
NEGATIVE = -1e30

QUAD = 4
PAIR = 2
GROUP = QUAD * PAIR
MESH = pl.DeviceIdType.MESH
BF = jnp.bfloat16
F32 = jnp.float32


def matmul(spec, left, right):
    return jnp.einsum(spec, left, right, preferred_element_type=F32)


def norm_rows(values, gain):
    return values * lax.rsqrt(jnp.mean(values * values, axis=-1, keepdims=True) + EPS) * gain


def rotate(values, cosine, sine):
    half = values.shape[-1] // 2
    first = values[..., :half]
    second = values[..., half:]
    return jnp.concatenate(
        [first * cosine - second * sine, second * cosine + first * sine], axis=-1
    )


def layout(row_lengths, count_rows):
    slots = jnp.arange(row_lengths.shape[0], dtype=jnp.int32)
    ends = jnp.sum(jnp.where(slots[None, :] <= slots[:, None], row_lengths[None, :], 0), axis=1)
    starts = ends - row_lengths
    places = jnp.arange(count_rows, dtype=jnp.int32)
    segment = jnp.sum((places[:, None] >= ends[None, :]).astype(jnp.int32), axis=1)
    begins = jnp.concatenate([starts, ends[-1:]])
    labels = jnp.arange(begins.shape[0], dtype=jnp.int32)
    firsts = jnp.sum(jnp.where(segment[:, None] == labels[None, :], begins[None, :], 0), axis=1)
    position = places - firsts
    valid = places < ends[-1]
    allowed = (segment[:, None] == segment[None, :]) & (places[None, :] <= places[:, None])
    return (position, valid, allowed)


def angles_of(position, head_size):
    half = head_size // 2
    freqs = ROPE_BASE ** (-(jnp.arange(half, dtype=F32) * 2.0) / head_size)
    angle = position.astype(F32)[..., None] * freqs
    return (jnp.cos(angle), jnp.sin(angle))


def place():
    batch = lax.axis_index("batch")
    quad = lax.rem(batch, QUAD)
    return batch - quad, quad, lax.axis_index("hid")


def flip(quad, bits):
    core = lax.rem(quad, 2)
    chip = quad - core
    if bits & 1:
        core = 1 - core
    if bits & 2:
        chip = 2 - chip
    return chip + core


def meet(peers):
    barrier = pltpu.get_barrier_semaphore()
    for peer in peers:
        pl.semaphore_signal(barrier, inc=1, device_id=peer, device_id_type=MESH)
    pl.semaphore_wait(barrier, len(peers))


def gather_kernel(count, put, *refs):
    ins, outs = refs[:count], refs[count : 2 * count]
    local_sem, send_sem, recv_sem = refs[2 * count :]
    base, quad, hid = place()

    def spot(f):
        bits, turn = f
        return (flip(quad, bits), 1 - hid if turn else hid)

    def address(f):
        q, h = spot(f)
        return (base + q, h)

    near = [(2, 1), (2, 0), (0, 1)]
    mate = (1, 0)
    meet([address(f) for f in near + [mate]])

    def mine(f):
        q, h = spot(f)
        return q * PAIR + h

    me = quad * PAIR + hid
    started = []
    for i in range(count):
        for j, f in enumerate(near):
            copy = pltpu.make_async_remote_copy(
                src_ref=ins[i],
                dst_ref=put(outs[i], me),
                send_sem=send_sem.at[i, j],
                recv_sem=recv_sem.at[i, j],
                device_id=address(f),
                device_id_type=MESH,
            )
            copy.start()
            started.append(copy)
        copy = pltpu.make_async_remote_copy(
            src_ref=ins[i],
            dst_ref=put(outs[i], me),
            send_sem=send_sem.at[i, 3],
            recv_sem=recv_sem.at[i, 3],
            device_id=address(mate),
            device_id_type=MESH,
        )
        copy.start()
        started.append(copy)
        copy = pltpu.make_async_copy(ins[i], put(outs[i], me), local_sem.at[i])
        copy.start()
    for i in range(count):
        for j in (1, 2, 0):
            f = near[j]
            where = put(outs[i], mine(f))
            pltpu.make_async_remote_copy(
                src_ref=ins[i],
                dst_ref=where,
                send_sem=send_sem.at[i, j],
                recv_sem=recv_sem.at[i, j],
                device_id=address(f),
                device_id_type=MESH,
            ).wait_recv()
            copy = pltpu.make_async_remote_copy(
                src_ref=where,
                dst_ref=where,
                send_sem=send_sem.at[i, 4 + j],
                recv_sem=recv_sem.at[i, 4 + j],
                device_id=address(mate),
                device_id_type=MESH,
            )
            copy.start()
            started.append(copy)
    for i in range(count):
        pltpu.make_async_copy(ins[i], put(outs[i], me), local_sem.at[i]).wait()
        for j, f in [(3, (1, 0))] + [(4 + j, (near[j][0] ^ 1, near[j][1])) for j in range(3)]:
            where = put(outs[i], mine(f))
            pltpu.make_async_remote_copy(
                src_ref=where,
                dst_ref=where,
                send_sem=send_sem.at[i, j],
                recv_sem=recv_sem.at[i, j],
                device_id=address(mate),
                device_id_type=MESH,
            ).wait_recv()
    for copy in started:
        copy.wait_send()


def gather_layer(arrays, ident, name):
    count = len(arrays)
    moved = sum(a.size * 2 * GROUP for a in arrays)
    return pl.pallas_call(
        functools.partial(gather_kernel, count, lambda ref, i: ref.at[i]),
        out_shape=[jax.ShapeDtypeStruct((GROUP,) + a.shape, a.dtype) for a in arrays],
        in_specs=[pl.BlockSpec(memory_space=pl.ANY)] * count,
        out_specs=[pl.BlockSpec(memory_space=pl.ANY)] * count,
        scratch_shapes=[
            pltpu.SemaphoreType.DMA((count,)),
            pltpu.SemaphoreType.DMA((count, 7)),
            pltpu.SemaphoreType.DMA((count, 7)),
        ],
        compiler_params=pltpu.CompilerParams(collective_id=ident, has_side_effects=True),
        cost_estimate=pl.CostEstimate(flops=0, bytes_accessed=16 * moved, transcendentals=0),
        name=name,
    )(*arrays)


def reduce_kernel(in_ref, out_ref, own, mate_in, sums, far_in, local_sem, send_sem, recv_sem):
    base, quad, hid = place()
    rows = out_ref.shape[0]
    ways = [(2, 1), (2, 0), (0, 1), (0, 0)]
    mate = (base + flip(quad, 1), hid)

    def address(f):
        return (base + flip(quad, f[0]), 1 - hid if f[1] else hid)

    def index(f, other):
        q = flip(quad, f[0] ^ (1 if other else 0))
        return q * PAIR + (1 - hid if f[1] else hid)

    meet([address(f) for f in ways[:3]] + [mate])
    to_mate, locals_, far = [], [], []
    for j, f in enumerate(ways):
        copy = pltpu.make_async_remote_copy(
            src_ref=in_ref.at[index(f, True)],
            dst_ref=mate_in.at[j],
            send_sem=send_sem.at[j],
            recv_sem=recv_sem.at[j],
            device_id=mate,
            device_id_type=MESH,
        )
        copy.start()
        to_mate.append(copy)
        copy = pltpu.make_async_copy(in_ref.at[index(f, False)], own.at[j], local_sem.at[j])
        copy.start()
        locals_.append(copy)
    step = 16
    for j, f in enumerate(ways[:3]):
        locals_[j].wait()
        to_mate[j].wait_recv()

        def add(r, carry, j=j):
            at = pl.ds(pl.multiple_of(r * step, step), step)
            sums[j, at, :] = (
                own[j, at, :].astype(F32) + mate_in[j, at, :].astype(F32)
            ).astype(BF)
            return carry

        lax.fori_loop(0, rows // step, add, 0)
        copy = pltpu.make_async_remote_copy(
            src_ref=sums.at[j],
            dst_ref=far_in.at[j],
            send_sem=send_sem.at[4 + j],
            recv_sem=recv_sem.at[4 + j],
            device_id=address(f),
            device_id_type=MESH,
        )
        copy.start()
        far.append(copy)
    locals_[3].wait()
    to_mate[3].wait_recv()
    for copy in far:
        copy.wait_recv()

    def total(r, carry):
        at = pl.ds(pl.multiple_of(r * step, step), step)
        out_ref[at, :] = (
            own[3, at, :].astype(F32)
            + mate_in[3, at, :].astype(F32)
            + far_in[0, at, :].astype(F32)
            + far_in[1, at, :].astype(F32)
            + far_in[2, at, :].astype(F32)
        )
        return carry

    lax.fori_loop(0, rows // step, total, 0)
    for copy in to_mate + far:
        copy.wait_send()


def reduce_layer(blocks, ident, name):
    rows, columns = blocks.shape[1:]
    return pl.pallas_call(
        reduce_kernel,
        out_shape=jax.ShapeDtypeStruct((rows, columns), F32),
        in_specs=[pl.BlockSpec(memory_space=pl.ANY)],
        out_specs=pl.BlockSpec(memory_space=pltpu.VMEM),
        scratch_shapes=[
            pltpu.VMEM((4, rows, columns), BF),
            pltpu.VMEM((4, rows, columns), BF),
            pltpu.VMEM((3, rows, columns), BF),
            pltpu.VMEM((3, rows, columns), BF),
            pltpu.SemaphoreType.DMA((4,)),
            pltpu.SemaphoreType.DMA((7,)),
            pltpu.SemaphoreType.DMA((7,)),
        ],
        compiler_params=pltpu.CompilerParams(
            collective_id=ident, has_side_effects=True, vmem_limit_bytes=48 * 2**20
        ),
        cost_estimate=pl.CostEstimate(
            flops=0, bytes_accessed=16 * blocks.size * 2, transcendentals=0
        ),
        name=name,
    )(blocks)


def swap_kernel(count, *refs):
    ins, outs = refs[:count], refs[count : 2 * count]
    local_sem, send_sem, recv_sem = refs[2 * count :]
    base, quad, hid = place()
    meet([(base + flip(quad, f), hid) for f in (1, 2, 3)])
    copies = []
    for i in range(count):
        for f in (2, 3, 1):
            copy = pltpu.make_async_remote_copy(
                src_ref=ins[i].at[flip(quad, f)],
                dst_ref=outs[i].at[quad],
                send_sem=send_sem.at[i, f - 1],
                recv_sem=recv_sem.at[i, f - 1],
                device_id=(base + flip(quad, f), hid),
                device_id_type=MESH,
            )
            copy.start()
            copies.append((copy, i, f))
        copy = pltpu.make_async_copy(ins[i].at[quad], outs[i].at[quad], local_sem.at[i])
        copy.start()
    for i in range(count):
        pltpu.make_async_copy(ins[i].at[quad], outs[i].at[quad], local_sem.at[i]).wait()
    for copy, i, f in copies:
        pltpu.make_async_remote_copy(
            src_ref=ins[i].at[flip(quad, f)],
            dst_ref=outs[i].at[flip(quad, f)],
            send_sem=send_sem.at[i, f - 1],
            recv_sem=recv_sem.at[i, f - 1],
            device_id=(base + flip(quad, f), hid),
            device_id_type=MESH,
        ).wait_recv()
    for copy, i, f in copies:
        copy.wait_send()


def swap_quad(arrays, ident, name):
    count = len(arrays)
    moved = sum(a.size * 2 for a in arrays)
    return pl.pallas_call(
        functools.partial(swap_kernel, count),
        out_shape=[jax.ShapeDtypeStruct(a.shape, a.dtype) for a in arrays],
        in_specs=[pl.BlockSpec(memory_space=pl.ANY)] * count,
        out_specs=[pl.BlockSpec(memory_space=pl.ANY)] * count,
        scratch_shapes=[
            pltpu.SemaphoreType.DMA((count,)),
            pltpu.SemaphoreType.DMA((count, 3)),
            pltpu.SemaphoreType.DMA((count, 3)),
        ],
        compiler_params=pltpu.CompilerParams(collective_id=ident, has_side_effects=True),
        cost_estimate=pl.CostEstimate(flops=0, bytes_accessed=32 * moved, transcendentals=0),
        name=name,
    )(*arrays)


def hops(layers, forward, first):
    pairs = []
    for z in range(layers - 1):
        if z < first:
            continue
        a, b = (z, z + 1) if forward else (layers - 1 - z, layers - 2 - z)
        pairs += [(a * QUAD + q, b * QUAD + q) for q in range(QUAD)]
    return pairs


def tail_hops(layers, forward, count):
    pairs = []
    for z in range(count):
        a, b = (z, z + 1) if forward else (layers - 1 - z, layers - 2 - z)
        pairs += [(a * QUAD + q, b * QUAD + q) for q in range(QUAD)]
    return pairs


def gather_chain(unit, layers):
    up, down = [unit], [unit]
    for k in range(1, layers):
        up.append(lax.ppermute(up[-1], "batch", hops(layers, True, k - 1)))
        down.append(lax.ppermute(down[-1], "batch", hops(layers, False, k - 1)))
    return [unit] + [down[k] + up[layers - k] for k in range(1, layers)]


def reduce_chain(slots, layers):
    totals = slots[0].astype(F32)
    for forward in (True, False):
        arrived = None
        for offset in range(layers - 1, 0, -1):
            slot = slots[offset] if forward else slots[layers - offset]
            if arrived is not None:
                slot = (slot.astype(F32) + arrived.astype(F32)).astype(BF)
            arrived = lax.ppermute(slot, "batch", tail_hops(layers, forward, layers - offset))
        if arrived is not None:
            totals = totals + arrived.astype(F32)
    return totals


def turn(values, start):
    return lax.dynamic_slice_in_dim(
        jnp.concatenate([values, values], axis=-1), start, values.shape[-1], axis=-1
    )


def per_device(
    layers,
    tokens,
    lengths,
    attention_gain,
    query_down,
    query_gain,
    query_up,
    key_value,
    output_weight,
    feed_gain,
    gate_weight,
    up_weight,
    down_weight,
    cotangent,
):
    count_rows, model = tokens.shape
    part, rank = query_down.shape
    rank_part = query_up.shape[0]
    half = part // PAIR
    pair_columns = key_value.shape[1]
    wide = rank + pair_columns
    all_rows = GROUP * count_rows
    heads = HEADS // GROUP
    head_columns = heads * HEAD_DIM
    units = gate_weight.shape[1] // QUAD
    scale = HEAD_DIM ** (-0.5)
    base, quad, hid = place()
    layer = base // QUAD
    me = quad * PAIR + hid
    span = QUAD * part
    rank_span = QUAD * rank_part

    first_pack = jnp.concatenate(
        [
            lax.dynamic_slice_in_dim(
                jnp.concatenate([query_down, key_value], axis=1), hid * half, half, axis=0
            ),
            jnp.pad(
                jnp.concatenate(
                    [attention_gain, query_gain, feed_gain, lengths[0].astype(BF)]
                )[None],
                ((0, 15), (0, wide - 2 * part - rank_part - lengths.shape[1])),
            ),
        ],
        axis=0,
    )
    first_slots = jnp.stack(gather_chain(first_pack, layers))
    own_heads = [
        lax.dynamic_slice_in_dim(
            jnp.concatenate([output_weight, query_up], axis=0).reshape(
                part + rank_part, QUAD, PAIR, head_columns
            ),
            hid,
            1,
            axis=2,
        )[:, :, 0]
        .transpose(1, 0, 2)
    ][0]
    feed_pack = jnp.concatenate(
        [w.reshape(part, QUAD, units) for w in (gate_weight, up_weight, down_weight)], axis=2
    ).transpose(1, 0, 2)
    head_unit, feed_unit = swap_quad([own_heads, feed_pack], 1, "swap_weights")
    head_slots = gather_chain(head_unit, layers)
    out_slice = jnp.stack([s[:, :part] for s in head_slots]).reshape(model, head_columns)
    query_slice = jnp.stack([s[:, part:] for s in head_slots]).reshape(rank, head_columns)
    feed_slots = gather_chain(feed_unit, layers)
    feed_all = jnp.stack(feed_slots).reshape(model, 3 * units)
    gate_up = feed_all[:, : 2 * units]
    down = feed_all[:, 2 * units :]

    [first_all] = gather_layer([first_slots], 2, "gather_first")
    first_all = first_all.transpose(1, 0, 2, 3)
    first_weight = first_all[:, :, :half].reshape(model, wide)
    small = first_all[:, :, half, :]
    first_gain = small[:, ::PAIR, :part].reshape(model).astype(F32)
    second_gain = small[:, ::PAIR, part : part + rank_part].reshape(rank).astype(F32)
    third_gain = (
        small[:, ::PAIR, part + rank_part : 2 * part + rank_part].reshape(model).astype(F32)
    )
    begin = 2 * part + rank_part
    all_lengths = small[0, :, begin : begin + lengths.shape[1]].astype(jnp.int32)

    inputs = turn(tokens, layer * span).astype(F32)
    upstream = turn(cotangent, layer * span).astype(F32)
    position, valid, allowed_own = layout(lengths[0], count_rows)
    cosine, sine = angles_of(position, HEAD_DIM)
    normed = norm_rows(inputs, first_gain).astype(BF)
    first = matmul("rd,de->re", normed, first_weight)
    latent = turn(first[:, :rank], layer * rank_span)
    keyvals = first[:, rank:]
    latent_normed = norm_rows(latent, second_gain).astype(BF)
    key_rot = rotate(keyvals[:, :HEAD_DIM], cosine, sine).astype(BF)
    value_rows = keyvals[:, HEAD_DIM:].astype(BF)
    [rows_all] = gather_layer(
        [jnp.concatenate([latent_normed, key_rot, value_rows], axis=1)], 3, "gather_latent"
    )
    latent_all = rows_all[:, :, :rank].reshape(all_rows, rank)
    key_all = rows_all[:, :, rank : rank + HEAD_DIM]
    value_all = rows_all[:, :, rank + HEAD_DIM :]

    positions, valids, allowed = jax.vmap(lambda one: layout(one, count_rows))(all_lengths)
    cosines, sines = angles_of(positions, HEAD_DIM)
    queries = matmul("rc,cf->rf", latent_all, query_slice).reshape(
        GROUP, count_rows, heads, HEAD_DIM
    )
    query_rot = rotate(queries, cosines[:, :, None, :], sines[:, :, None, :]).astype(BF)

    def masked_scores():
        raw = matmul("gqhd,gkd->ghqk", query_rot, key_all) * scale
        return jnp.where(allowed[:, None], raw, NEGATIVE)

    scores = masked_scores()
    highest = jnp.max(scores, axis=-1, keepdims=True)
    raised = jnp.exp(scores - highest)
    totals = jnp.sum(raised, axis=-1, keepdims=True)
    probs = (raised / totals).astype(BF)
    logsum = highest + jnp.log(totals)
    mixed = (
        matmul("ghqk,gkd->gqhd", probs, value_all).reshape(all_rows, head_columns).astype(BF)
    )
    branch_terms = matmul("rf,df->rd", mixed, out_slice).astype(BF)
    branch = reduce_layer(branch_terms.reshape(GROUP, count_rows, model), 4, "reduce_branch")
    middle = inputs + branch
    normed_ffn = norm_rows(middle, third_gain).astype(BF)
    kept = jnp.where(valid[:, None], upstream, 0.0)
    feed_rows, grad_rows, normed_rows = gather_layer(
        [normed_ffn, kept.astype(BF), normed], 5, "gather_feed"
    )
    feed_rows = feed_rows.reshape(all_rows, model)
    grad_rows = grad_rows.reshape(all_rows, model)
    normed_rows = normed_rows.reshape(all_rows, model)

    both = matmul("rd,df->rf", feed_rows, gate_up)
    gate, up = both[:, :units], both[:, units:]
    hidden_grad = matmul("rd,df->rf", grad_rows, down)
    sigma = jax.nn.sigmoid(gate)
    activated = gate * sigma
    slope = sigma * (1.0 + gate * (1.0 - sigma))
    hidden = (activated * up).astype(BF)
    both_grad = jnp.concatenate([hidden_grad * up * slope, hidden_grad * activated], axis=1).astype(
        BF
    )
    feed_terms = matmul("rf,df->rd", hidden, down).astype(BF)
    ffn_terms = matmul("rf,df->rd", both_grad, gate_up).astype(BF)
    sums = reduce_layer(
        jnp.concatenate([ffn_terms, feed_terms], axis=1).reshape(GROUP, count_rows, 2 * model),
        6,
        "reduce_feed",
    )
    ffn_grad, feed = sums[:, :model], sums[:, model:]
    grad_both = matmul("rd,rf->df", feed_rows, both_grad).astype(BF)
    grad_down = matmul("rd,rf->df", grad_rows, hidden).astype(BF)
    feed_grads = jnp.concatenate([grad_both, grad_down], axis=1).reshape(
        layers, QUAD, part, 3 * units
    )
    feed_sum = reduce_chain([feed_grads[k] for k in range(layers)], layers).astype(BF)

    output = turn(
        jnp.where(valid[:, None], middle + feed, inputs).astype(BF),
        lax.rem(model - layer * span, model),
    )
    unused_third, third_pull = jax.vjp(norm_rows, middle, third_gain)
    middle_norm_grad, feed_gain_grad = third_pull(ffn_grad)
    middle_grad = kept + middle_norm_grad
    [branch_rows] = gather_layer([middle_grad.astype(BF)], 7, "gather_branch")
    branch_rows = branch_rows.reshape(all_rows, model)

    grad_out = matmul("rd,rf->df", branch_rows, mixed).astype(BF)
    mixed_grad = (
        matmul("rd,df->rf", branch_rows, out_slice)
        .astype(BF)
        .reshape(GROUP, count_rows, heads, HEAD_DIM)
    )
    probs_back = jnp.exp(masked_scores() - logsum)
    prob_grad = matmul("gqhd,gkd->ghqk", mixed_grad, value_all)
    score_grad = (
        probs_back * (prob_grad - jnp.sum(probs_back * prob_grad, axis=-1, keepdims=True))
    ).astype(BF)
    value_terms = matmul("ghqk,gqhd->gkd", probs, mixed_grad)
    query_rot_grad = matmul("ghqk,gkd->gqhd", score_grad, key_all) * scale
    key_terms = matmul("ghqk,gqhd->gkd", score_grad, query_rot) * scale
    query_grad = (
        rotate(query_rot_grad, cosines[:, :, None, :], -sines[:, :, None, :])
        .reshape(all_rows, head_columns)
        .astype(BF)
    )
    grad_query = matmul("rc,rf->cf", latent_all, query_grad).astype(BF)
    latent_terms = matmul("rf,cf->rc", query_grad, query_slice)
    head_grads = [
        jnp.concatenate(
            [
                grad_out.reshape(layers, QUAD, part, head_columns)[k],
                grad_query.reshape(layers, QUAD, rank_part, head_columns)[k],
            ],
            axis=1,
        )
        for k in range(layers)
    ]
    head_sum = reduce_chain(head_grads, layers).astype(BF)
    back = reduce_layer(
        jnp.concatenate(
            [
                latent_terms.reshape(GROUP, count_rows, rank),
                key_terms,
                value_terms,
            ],
            axis=2,
        ).astype(BF),
        8,
        "reduce_latent",
    )

    latent_normed_grad = back[:, :rank]
    keyval_grad = jnp.concatenate(
        [rotate(back[:, rank : rank + HEAD_DIM], cosine, -sine), back[:, rank + HEAD_DIM :]], axis=1
    ).astype(BF)
    unused_second, second_pull = jax.vjp(norm_rows, latent, second_gain)
    latent_back, latent_gain_grad = second_pull(latent_normed_grad)
    latent_grad = turn(latent_back.astype(BF), lax.rem(rank - layer * rank_span, rank))
    first_grad = jnp.concatenate([latent_grad, keyval_grad], axis=1)
    normed_grad = matmul("re,de->rd", first_grad, first_weight)
    unused_first, first_pull = jax.vjp(norm_rows, inputs, first_gain)
    input_norm_grad, norm_gain_grad = first_pull(normed_grad)
    grad_tokens = turn(
        (middle_grad + input_norm_grad + jnp.where(valid[:, None], 0.0, upstream)).astype(BF),
        lax.rem(model - layer * span, model),
    )
    gains = jnp.concatenate([norm_gain_grad, feed_gain_grad, latent_gain_grad])
    gains = jnp.pad(gains.reshape(-1, rank), ((0, 16 - gains.size // rank), (0, wide - rank)))
    [grad_all] = gather_layer(
        [jnp.concatenate([first_grad, gains.astype(BF)], axis=0)], 9, "gather_last"
    )
    gain_sums = jnp.sum(grad_all[:, count_rows:, :rank].astype(F32), axis=0)
    lines = model // rank
    norm_sums = gain_sums[:lines].reshape(layers, span)
    feed_sums = gain_sums[lines : 2 * lines].reshape(layers, span)
    latent_sums = gain_sums[2 * lines].reshape(layers, rank_span)
    columns = wide // QUAD
    grad_slice = lax.dynamic_slice_in_dim(
        grad_all[:, :count_rows].reshape(all_rows, QUAD, columns), quad, 1, axis=1
    )[:, 0]
    half_rows = lax.dynamic_slice_in_dim(
        normed_rows.reshape(all_rows, layers * QUAD, PAIR, half), hid, 1, axis=2
    ).reshape(all_rows, model // PAIR)
    grad_first = matmul("rd,re->de", half_rows, grad_slice).astype(BF)
    small_sums = jnp.concatenate([norm_sums, feed_sums, latent_sums], axis=1)
    small_width = -(-small_sums.shape[1] // columns) * columns
    small_sums = jnp.pad(
        small_sums, ((0, 0), (0, small_width - small_sums.shape[1]))
    ).reshape(layers, -1, columns)
    small_sums = jnp.pad(small_sums, ((0, 0), (0, -small_sums.shape[1] % 16), (0, 0))).astype(BF)
    last_sum = reduce_chain(
        [
            jnp.concatenate(
                [grad_first.reshape(layers, QUAD * half, columns)[k], small_sums[k]], axis=0
            )
            for k in range(layers)
        ],
        layers,
    )
    first_sum = last_sum[: QUAD * half].reshape(QUAD, half, columns).astype(BF)
    small_sum = last_sum[QUAD * half :].reshape(-1)

    feed_own, head_own, first_own = swap_quad([feed_sum, head_sum, first_sum], 10, "swap_sums")
    feed_own = feed_own.transpose(1, 0, 2).astype(F32)
    grad_gate, grad_up, grad_down = (
        feed_own[:, :, i * units : (i + 1) * units].reshape(part, QUAD * units) for i in range(3)
    )
    head_half = head_own.transpose(1, 0, 2)
    first_half = first_own.transpose(1, 0, 2).reshape(half, wide)
    other_way = [(0, 1), (1, 0)]
    head_other = lax.ppermute(head_half, "hid", other_way)
    first_other = lax.ppermute(first_half, "hid", other_way)

    def sides(own, other, axis):
        low = jnp.where(hid == 0, own, other)
        high = jnp.where(hid == 0, other, own)
        return low, high

    low, high = sides(head_half, head_other, 2)
    head_full = (
        jnp.stack([low, high], axis=2).reshape(part + rank_part, HEADS * HEAD_DIM).astype(F32)
    )
    low, high = sides(first_half, first_other, 0)
    first_full = jnp.concatenate([low, high], axis=0).astype(F32)
    return (
        output,
        grad_tokens,
        lax.dynamic_slice_in_dim(small_sum, quad * part, part),
        first_full[:, :rank],
        lax.dynamic_slice_in_dim(small_sum, 2 * span + quad * rank_part, rank_part),
        head_full[part:],
        first_full[:, rank:],
        head_full[:part],
        lax.dynamic_slice_in_dim(small_sum, span + quad * part, part),
        grad_gate,
        grad_up,
        grad_down,
    )


def solution(mesh):
    placed = (
        P(("batch", "hid"), None),
        P(("batch", "hid"), None),
        P("batch"),
        P("batch", None),
        P("batch"),
        P("batch", None),
        P("batch", None),
        P("batch", None),
        P("batch"),
        P("batch", "hid"),
        P("batch", "hid"),
        P("batch", "hid"),
        P(("batch", "hid"), None),
    )
    return jax.shard_map(
        functools.partial(per_device, mesh.shape["batch"] // QUAD),
        mesh=mesh,
        in_specs=placed,
        out_specs=(
            P(("batch", "hid"), None),
            P(("batch", "hid"), None),
            P("batch"),
            P("batch", None),
            P("batch"),
            P("batch", None),
            P("batch", None),
            P("batch", None),
            P("batch"),
            P("batch", "hid"),
            P("batch", "hid"),
            P("batch", "hid"),
        ),
        check_vma=False,
    )
```

```python
import functools

import jax
import jax.numpy as jnp
from jax import lax
from jax.experimental import pallas as pl
from jax.experimental.pallas import tpu as pltpu
from jax.sharding import PartitionSpec as P

HEADS = 16
HEAD_DIM = 256


EPS = 1e-05
ROPE_BASE = 10000.0
NEGATIVE = -1e30

QUAD = 4
PAIR = 2
GROUP = QUAD * PAIR
EXTRA = 32
MESH = pl.DeviceIdType.MESH
BF = jnp.bfloat16
F32 = jnp.float32


def matmul(spec, left, right):
    return jnp.einsum(spec, left, right, preferred_element_type=F32)


def norm_rows(values, gain):
    return values * lax.rsqrt(jnp.mean(values * values, axis=-1, keepdims=True) + EPS) * gain


def rotate(values, cosine, sine):
    half = values.shape[-1] // 2
    first = values[..., :half]
    second = values[..., half:]
    return jnp.concatenate(
        [first * cosine - second * sine, second * cosine + first * sine], axis=-1
    )


def layout(row_lengths, count_rows):
    slots = jnp.arange(row_lengths.shape[0], dtype=jnp.int32)
    ends = jnp.sum(jnp.where(slots[None, :] <= slots[:, None], row_lengths[None, :], 0), axis=1)
    starts = ends - row_lengths
    places = jnp.arange(count_rows, dtype=jnp.int32)
    segment = jnp.sum((places[:, None] >= ends[None, :]).astype(jnp.int32), axis=1)
    begins = jnp.concatenate([starts, ends[-1:]])
    labels = jnp.arange(begins.shape[0], dtype=jnp.int32)
    firsts = jnp.sum(jnp.where(segment[:, None] == labels[None, :], begins[None, :], 0), axis=1)
    position = places - firsts
    valid = places < ends[-1]
    allowed = (segment[:, None] == segment[None, :]) & (places[None, :] <= places[:, None])
    return (position, valid, allowed)


def angles_of(position, head_size):
    half = head_size // 2
    freqs = ROPE_BASE ** (-(jnp.arange(half, dtype=F32) * 2.0) / head_size)
    angle = position.astype(F32)[..., None] * freqs
    return (jnp.cos(angle), jnp.sin(angle))


def place():
    batch = lax.axis_index("batch")
    quad = lax.rem(batch, QUAD)
    return batch - quad, quad, lax.axis_index("hid")


def flip(quad, bits):
    core = lax.rem(quad, 2)
    chip = quad - core
    if bits & 1:
        core = 1 - core
    if bits & 2:
        chip = 2 - chip
    return chip + core


def after(value, *others):
    return lax.optimization_barrier((value, *others))[0]


def meet(peers):
    barrier = pltpu.get_barrier_semaphore()
    for peer in peers:
        pl.semaphore_signal(barrier, inc=1, device_id=peer, device_id_type=MESH)
    pl.semaphore_wait(barrier, len(peers))


def ways_of(base, quad, hid):
    def spot(bits, turn):
        return (flip(quad, bits), 1 - hid if turn else hid)

    def address(f):
        q, h = spot(*f)
        return (base + q, h)

    def index(f):
        q, h = spot(*f)
        return q * PAIR + h

    return address, index


ACROSS, ALONG, CORNER, MATE, SELF = (2, 0), (0, 1), (2, 1), (1, 0), (0, 0)


def gather_kernel(count, cuts, puts, *refs):
    ins, outs = refs[:count], refs[count : 2 * count]
    local_sem, send_sem, recv_sem = refs[2 * count :]
    base, quad, hid = place()
    address, index = ways_of(base, quad, hid)
    meet([address(f) for f in (ACROSS, ALONG, MATE)])

    def part(ref, i, h):
        cut, size = cuts[i]
        return ref.at[pl.ds(0, cut)] if h == 0 else ref.at[pl.ds(cut, size - cut)]

    def spot(i, f):
        return puts[i](outs[i], index(f))

    def copy(i, j, source, target, f):
        return pltpu.make_async_remote_copy(
            src_ref=source,
            dst_ref=target,
            send_sem=send_sem.at[i, j],
            recv_sem=recv_sem.at[i, j],
            device_id=address(f),
            device_id_type=MESH,
        )

    started = []

    def start(one):
        one.start()
        started.append(one)

    for i in range(count):
        for j, f, h in ((0, ACROSS, 0), (3, ALONG, 1), (1, ACROSS, 1), (2, ALONG, 0)):
            start(copy(i, j, part(ins[i], i, h), part(spot(i, SELF), i, h), f))
        start(copy(i, 6, ins[i], spot(i, SELF), MATE))
        pltpu.make_async_copy(ins[i], spot(i, SELF), local_sem.at[i]).start()

    def arrived(i, j, where, f):
        copy(i, j, where, where, f).wait_recv()

    for i in range(count):
        where = part(spot(i, ACROSS), i, 0)
        arrived(i, 0, where, ACROSS)
        start(copy(i, 4, where, where, ALONG))
        where = part(spot(i, ALONG), i, 1)
        arrived(i, 3, where, ALONG)
        start(copy(i, 5, where, where, ACROSS))
        arrived(i, 1, part(spot(i, ACROSS), i, 1), ACROSS)
        where = spot(i, ACROSS)
        start(copy(i, 7, where, where, MATE))
        arrived(i, 2, part(spot(i, ALONG), i, 0), ALONG)
        where = spot(i, ALONG)
        start(copy(i, 8, where, where, MATE))
    for i in range(count):
        where = part(spot(i, CORNER), i, 0)
        arrived(i, 4, where, ALONG)
        start(copy(i, 9, where, where, MATE))
        where = part(spot(i, CORNER), i, 1)
        arrived(i, 5, where, ACROSS)
        start(copy(i, 10, where, where, MATE))
    for i in range(count):
        pltpu.make_async_copy(ins[i], spot(i, SELF), local_sem.at[i]).wait()
        arrived(i, 6, spot(i, MATE), MATE)
        arrived(i, 7, spot(i, (ACROSS[0] ^ 1, ACROSS[1])), MATE)
        arrived(i, 8, spot(i, (ALONG[0] ^ 1, ALONG[1])), MATE)
        corner = spot(i, (CORNER[0] ^ 1, CORNER[1]))
        arrived(i, 9, part(corner, i, 0), MATE)
        arrived(i, 10, part(corner, i, 1), MATE)
    for one in started:
        one.wait_send()


def stacked(ref, place):
    return ref.at[place]


def inside(ref, place):
    return ref.at[:, place]


def gather_layer(arrays, ident, name, puts=None):
    count = len(arrays)
    puts = puts or [stacked] * count
    shapes = [
        (GROUP,) + a.shape if p is stacked else (a.shape[0], GROUP) + a.shape[1:]
        for a, p in zip(arrays, puts)
    ]
    cuts = [
        (a.shape[0] // 2 if a.ndim > 2 else a.shape[0] // 32 * 16, a.shape[0]) for a in arrays
    ]
    moved = sum(a.size * 2 * GROUP for a in arrays)
    return pl.pallas_call(
        functools.partial(gather_kernel, count, cuts, puts),
        out_shape=[jax.ShapeDtypeStruct(s, a.dtype) for s, a in zip(shapes, arrays)],
        in_specs=[pl.BlockSpec(memory_space=pl.ANY)] * count,
        out_specs=[pl.BlockSpec(memory_space=pl.ANY)] * count,
        scratch_shapes=[
            pltpu.SemaphoreType.DMA((count,)),
            pltpu.SemaphoreType.DMA((count, 11)),
            pltpu.SemaphoreType.DMA((count, 11)),
        ],
        compiler_params=pltpu.CompilerParams(collective_id=ident, has_side_effects=True),
        cost_estimate=pl.CostEstimate(flops=0, bytes_accessed=16 * moved, transcendentals=0),
        name=name,
    )(*arrays)


def reduce_kernel(in_ref, out_ref, own, mate_in, sums, relay, far_in, local_sem, send_sem, recv_sem):
    base, quad, hid = place()
    address, index = ways_of(base, quad, hid)
    rows = out_ref.shape[0]
    half = rows // 2
    step = 16
    ways = [CORNER, ACROSS, ALONG, SELF]
    meet([address(f) for f in (ACROSS, ALONG, MATE)])
    started = []

    def copy(j, source, target, f):
        return pltpu.make_async_remote_copy(
            src_ref=source,
            dst_ref=target,
            send_sem=send_sem.at[j],
            recv_sem=recv_sem.at[j],
            device_id=address(f),
            device_id_type=MESH,
        )

    def start(one):
        one.start()
        started.append(one)
        return one

    to_mate, local = [], []
    for j, f in enumerate(ways):
        to_mate.append(start(copy(j, in_ref.at[index((f[0] ^ 1, f[1]))], mate_in.at[j], MATE)))
        local.append(pltpu.make_async_copy(in_ref.at[index(f)], own.at[j], local_sem.at[j]))
        local[-1].start()

    def ready(j):
        local[j].wait()
        to_mate[j].wait_recv()

    def add(j, first, count, more=None):
        def body(r, carry):
            at = pl.ds(pl.multiple_of(first + r * step, step), step)
            value = own[j, at, :].astype(F32) + mate_in[j, at, :].astype(F32)
            if more is not None:
                value += more[pl.ds(pl.multiple_of(r * step, step), step), :].astype(F32)
            sums[j, at, :] = value.astype(BF)
            return carry

        lax.fori_loop(0, count // step, body, 0)

    low, high = pl.ds(0, half), pl.ds(half, half)
    ready(0)
    add(0, 0, half)
    by_across = start(copy(4, sums.at[0, low], relay.at[0], ACROSS))
    add(0, half, half)
    by_along = start(copy(5, sums.at[0, high], relay.at[1], ALONG))
    ready(1)
    add(1, 0, half)
    across_low = start(copy(6, sums.at[1, low], far_in.at[0, low], ACROSS))
    ready(2)
    add(2, half, half)
    along_high = start(copy(7, sums.at[2, high], far_in.at[1, high], ALONG))
    by_across.wait_recv()
    add(2, 0, half, relay.at[0])
    along_low = start(copy(8, sums.at[2, low], far_in.at[1, low], ALONG))
    by_along.wait_recv()
    add(1, half, half, relay.at[1])
    across_high = start(copy(9, sums.at[1, high], far_in.at[0, high], ACROSS))
    ready(3)
    for one in (across_low, along_high, along_low, across_high):
        one.wait_recv()

    def total(r, carry):
        at = pl.ds(pl.multiple_of(r * step, step), step)
        out_ref[at, :] = (
            own[3, at, :].astype(F32)
            + mate_in[3, at, :].astype(F32)
            + far_in[0, at, :].astype(F32)
            + far_in[1, at, :].astype(F32)
        )
        return carry

    lax.fori_loop(0, rows // step, total, 0)
    for one in started:
        one.wait_send()


def reduce_layer(blocks, ident, name):
    rows, columns = blocks.shape[1:]
    return pl.pallas_call(
        reduce_kernel,
        out_shape=jax.ShapeDtypeStruct((rows, columns), F32),
        in_specs=[pl.BlockSpec(memory_space=pl.ANY)],
        out_specs=pl.BlockSpec(memory_space=pltpu.VMEM),
        scratch_shapes=[
            pltpu.VMEM((4, rows, columns), BF),
            pltpu.VMEM((4, rows, columns), BF),
            pltpu.VMEM((3, rows, columns), BF),
            pltpu.VMEM((2, rows // 2, columns), BF),
            pltpu.VMEM((2, rows, columns), BF),
            pltpu.SemaphoreType.DMA((4,)),
            pltpu.SemaphoreType.DMA((10,)),
            pltpu.SemaphoreType.DMA((10,)),
        ],
        compiler_params=pltpu.CompilerParams(
            collective_id=ident, has_side_effects=True, vmem_limit_bytes=40 * 2**20
        ),
        cost_estimate=pl.CostEstimate(
            flops=0, bytes_accessed=16 * blocks.size * 2, transcendentals=0
        ),
        name=name,
    )(blocks)


def swap_kernel(count, takes, puts, flips, *refs):
    ins, outs = refs[:count], refs[count : 2 * count]
    local_sem, send_sem, recv_sem = refs[2 * count :]
    base, quad, hid = place()
    address, index = ways_of(base, quad, hid)
    meet([address(f) for f in flips])

    def copy(i, j, f, owner):
        return pltpu.make_async_remote_copy(
            src_ref=takes[i](ins[i], index(f)),
            dst_ref=puts[i](outs[i], owner),
            send_sem=send_sem.at[i, j],
            recv_sem=recv_sem.at[i, j],
            device_id=address(f),
            device_id_type=MESH,
        )

    me = index(SELF)
    for i in range(count):
        for j, f in enumerate(flips):
            copy(i, j, f, me).start()
        pltpu.make_async_copy(takes[i](ins[i], me), puts[i](outs[i], me), local_sem.at[i]).start()
    for i in range(count):
        pltpu.make_async_copy(takes[i](ins[i], me), puts[i](outs[i], me), local_sem.at[i]).wait()
        for j, f in enumerate(flips):
            copy(i, j, f, index(f)).wait_recv()
    for i in range(count):
        for j, f in enumerate(flips):
            copy(i, j, f, me).wait_send()


QUAD_FLIPS = ((3, 0), (2, 0), (1, 0))
ALL_FLIPS = ((3, 1), (2, 1), (3, 0), (2, 0), (1, 1), (0, 1), (1, 0))


def swap(arrays, takes, puts, shapes, flips, ident, name):
    count = len(arrays)
    moved = sum(a.size * 2 for a in arrays)
    return pl.pallas_call(
        functools.partial(swap_kernel, count, takes, puts, flips),
        out_shape=[jax.ShapeDtypeStruct(s, a.dtype) for s, a in zip(shapes, arrays)],
        in_specs=[pl.BlockSpec(memory_space=pl.ANY)] * count,
        out_specs=[pl.BlockSpec(memory_space=pl.ANY)] * count,
        scratch_shapes=[
            pltpu.SemaphoreType.DMA((count,)),
            pltpu.SemaphoreType.DMA((count, len(flips))),
            pltpu.SemaphoreType.DMA((count, len(flips))),
        ],
        compiler_params=pltpu.CompilerParams(collective_id=ident, has_side_effects=True),
        cost_estimate=pl.CostEstimate(flops=0, bytes_accessed=32 * moved, transcendentals=0),
        name=name,
    )(*arrays)


def columns_of(width):
    return lambda ref, i: ref.at[:, pl.ds(pl.multiple_of(i * width, width), width)]


def quad_of(ref, i):
    return ref.at[i // PAIR]


def layer_groups(layers):
    return [[z * QUAD + q for z in range(layers)] for q in range(QUAD)]


def gather_layers(unit, layers):
    return lax.all_gather(
        unit, "batch", axis=0, tiled=True, axis_index_groups=layer_groups(layers)
    )


def reduce_layers(blocks, layers):
    return lax.psum_scatter(
        blocks,
        "batch",
        scatter_dimension=0,
        tiled=True,
        axis_index_groups=layer_groups(layers),
    )


def per_device(
    layers,
    tokens,
    lengths,
    attention_gain,
    query_down,
    query_gain,
    query_up,
    key_value,
    output_weight,
    feed_gain,
    gate_weight,
    up_weight,
    down_weight,
    cotangent,
):
    count_rows, model = tokens.shape
    part, rank = query_down.shape
    rank_part = query_up.shape[0]
    half = part // PAIR
    wide = rank + key_value.shape[1]
    all_rows = GROUP * count_rows
    heads = HEADS // GROUP
    head_columns = heads * HEAD_DIM
    units = gate_weight.shape[1] // QUAD
    cut = -(-units // 256) * 128
    chunks = [(0, cut), (cut, units)]
    scale = HEAD_DIM ** (-0.5)
    base, quad, hid = place()
    layer = base // QUAD
    me = quad * PAIR + hid
    span = QUAD * part
    rank_span = QUAD * rank_part

    first_pack = jnp.concatenate(
        [
            lax.dynamic_slice_in_dim(
                jnp.concatenate([query_down, key_value], axis=1), hid * half, half, axis=0
            ),
            jnp.pad(
                jnp.concatenate([attention_gain, query_gain, feed_gain, lengths[0].astype(BF)])[None],
                ((0, EXTRA - 1), (0, wide - 2 * part - rank_part - lengths.shape[1])),
            ),
        ],
        axis=0,
    )
    first_slots = gather_layers(first_pack, layers).reshape(layers, half + EXTRA, wide)
    out_unit, query_unit = swap(
        [output_weight, query_up],
        [columns_of(head_columns)] * 2,
        [quad_of] * 2,
        [(QUAD, part, head_columns), (QUAD, rank_part, head_columns)],
        QUAD_FLIPS,
        1,
        "swap_heads",
    )
    head_all = gather_layers(
        jnp.concatenate(
            [query_unit.reshape(rank_span, head_columns), out_unit.reshape(span, head_columns)]
        ),
        layers,
    ).reshape(layers, rank_span + span, head_columns)
    query_slice = head_all[:, :rank_span].reshape(rank, head_columns)
    out_slice = head_all[:, rank_span:].reshape(model, head_columns)
    packs = [
        jnp.concatenate(
            [
                w.reshape(part, QUAD, units)[:, :, low:high]
                for w in (gate_weight, up_weight, down_weight)
            ],
            axis=2,
        ).transpose(1, 0, 2)
        for low, high in chunks
    ]
    feed_units = swap(
        packs, [quad_of] * 2, [quad_of] * 2, [p.shape for p in packs], QUAD_FLIPS, 2, "swap_feed"
    )

    small_width = -(-(2 * part + rank_part + lengths.shape[1]) // 128) * 128
    first_weight, small = gather_layer(
        [first_slots[:, :half], first_slots[:, half : half + 16, :small_width]],
        3,
        "gather_first",
        [inside, stacked],
    )
    feed_weights = [
        gather_layers(feed_units[0].reshape(span, -1), layers),
        gather_layers(after(feed_units[1], first_weight).reshape(span, -1), layers),
    ]
    first_weight = first_weight.reshape(model, wide)
    small = small[:, :, 0].transpose(1, 0, 2)
    first_gain = small[:, ::PAIR, :part].reshape(model).astype(F32)
    second_gain = small[:, ::PAIR, part : part + rank_part].reshape(rank).astype(F32)
    third_gain = (
        small[:, ::PAIR, part + rank_part : 2 * part + rank_part].reshape(model).astype(F32)
    )
    begin = 2 * part + rank_part
    all_lengths = small[:, :, begin : begin + lengths.shape[1]].astype(jnp.int32)
    all_lengths = lax.dynamic_index_in_dim(all_lengths, layer, 0, keepdims=False)

    inputs = tokens.astype(F32)
    upstream = cotangent.astype(F32)
    position, valid, allowed_own = layout(lengths[0], count_rows)
    cosine, sine = angles_of(position, HEAD_DIM)
    normed = norm_rows(inputs, first_gain).astype(BF)
    first = matmul("rd,de->re", normed, first_weight)
    latent = first[:, :rank]
    keyvals = first[:, rank:]
    latent_normed = norm_rows(latent, second_gain).astype(BF)
    key_rot = rotate(keyvals[:, :HEAD_DIM], cosine, sine).astype(BF)
    value_rows = keyvals[:, HEAD_DIM:].astype(BF)
    [rows_all] = gather_layer(
        [jnp.concatenate([latent_normed, key_rot, value_rows], axis=1)], 4, "gather_latent"
    )
    latent_all = rows_all[:, :, :rank].reshape(all_rows, rank)
    key_all = rows_all[:, :, rank : rank + HEAD_DIM]
    value_all = rows_all[:, :, rank + HEAD_DIM :]

    positions, valids, allowed = jax.vmap(lambda one: layout(one, count_rows))(all_lengths)
    cosines, sines = angles_of(positions, HEAD_DIM)
    queries = matmul("rc,cf->rf", latent_all, query_slice).reshape(
        GROUP, count_rows, heads, HEAD_DIM
    )
    query_rot = rotate(queries, cosines[:, :, None, :], sines[:, :, None, :]).astype(BF)

    def masked_scores():
        raw = matmul("gqhd,gkd->ghqk", query_rot, key_all) * scale
        return jnp.where(allowed[:, None], raw, NEGATIVE)

    scores = masked_scores()
    highest = jnp.max(scores, axis=-1, keepdims=True)
    raised = jnp.exp(scores - highest)
    totals = jnp.sum(raised, axis=-1, keepdims=True)
    probs = (raised / totals).astype(BF)
    logsum = highest + jnp.log(totals)
    mixed = matmul("ghqk,gkd->gqhd", probs, value_all).reshape(all_rows, head_columns).astype(BF)
    branch_terms = matmul("rf,df->rd", mixed, out_slice).astype(BF)
    branch = reduce_layer(branch_terms.reshape(GROUP, count_rows, model), 5, "reduce_branch")
    middle = inputs + branch
    normed_ffn = norm_rows(middle, third_gain).astype(BF)
    kept = jnp.where(valid[:, None], upstream, 0.0)
    feed_rows, grad_rows = gather_layer([normed_ffn, kept.astype(BF)], 6, "gather_feed")
    feed_rows = feed_rows.reshape(all_rows, model)
    grad_rows = grad_rows.reshape(all_rows, model)

    feed_terms = jnp.zeros((all_rows, model), F32)
    ffn_terms = jnp.zeros((all_rows, model), F32)
    feed_sums = []
    for weights, (low, high) in zip(feed_weights, chunks):
        width = high - low
        gate_up, down = weights[:, : 2 * width], weights[:, 2 * width :]
        both = matmul("rd,df->rf", feed_rows, gate_up)
        gate, up = both[:, :width], both[:, width:]
        hidden_grad = matmul("rd,df->rf", grad_rows, down)
        sigma = jax.nn.sigmoid(gate)
        activated = gate * sigma
        slope = sigma * (1.0 + gate * (1.0 - sigma))
        hidden = (activated * up).astype(BF)
        both_grad = jnp.concatenate(
            [hidden_grad * up * slope, hidden_grad * activated], axis=1
        ).astype(BF)
        grad_both = matmul("rd,rf->df", feed_rows, both_grad).astype(BF)
        grad_down = matmul("rd,rf->df", grad_rows, hidden).astype(BF)
        grad_pack = jnp.concatenate([grad_both, grad_down], axis=1)
        feed_sums.append(reduce_layers(grad_pack, layers))
        feed_rows = after(feed_rows, grad_pack)
        both_grad = after(both_grad, grad_pack)
        ffn_terms = ffn_terms + matmul("rf,df->rd", both_grad, gate_up)
        feed_terms = feed_terms + matmul("rf,df->rd", hidden, down)
    ffn_grad = reduce_layer(
        ffn_terms.astype(BF).reshape(GROUP, count_rows, model), 7, "reduce_ffn_grad"
    )
    unused_third, third_pull = jax.vjp(norm_rows, middle, third_gain)
    middle_norm_grad, feed_gain_grad = third_pull(ffn_grad)
    middle_grad = kept + middle_norm_grad
    [branch_rows] = gather_layer([middle_grad.astype(BF)], 8, "gather_branch")
    branch_rows = branch_rows.reshape(all_rows, model)

    grad_out = matmul("rd,rf->df", branch_rows, mixed).astype(BF)
    mixed_grad = (
        matmul("rd,df->rf", branch_rows, out_slice)
        .astype(BF)
        .reshape(GROUP, count_rows, heads, HEAD_DIM)
    )
    probs_back = jnp.exp(masked_scores() - logsum)
    prob_grad = matmul("gqhd,gkd->ghqk", mixed_grad, value_all)
    score_grad = (
        probs_back * (prob_grad - jnp.sum(probs_back * prob_grad, axis=-1, keepdims=True))
    ).astype(BF)
    value_terms = matmul("ghqk,gqhd->gkd", probs, mixed_grad)
    query_rot_grad = matmul("ghqk,gkd->gqhd", score_grad, key_all) * scale
    key_terms = matmul("ghqk,gqhd->gkd", score_grad, query_rot) * scale
    query_grad = (
        rotate(query_rot_grad, cosines[:, :, None, :], -sines[:, :, None, :])
        .reshape(all_rows, head_columns)
        .astype(BF)
    )
    grad_query = matmul("rc,rf->cf", latent_all, query_grad).astype(BF)
    latent_terms = matmul("rf,cf->rc", query_grad, query_slice)
    head_pack = jnp.concatenate(
        [
            grad_query.reshape(layers, rank_span, head_columns),
            grad_out.reshape(layers, span, head_columns),
        ],
        axis=1,
    ).reshape(rank + model, head_columns)
    head_sum = reduce_layers(after(head_pack, *feed_sums), layers)
    query_sum, out_sum = head_sum[:rank_span], head_sum[rank_span:]
    back = reduce_layer(
        jnp.concatenate(
            [latent_terms.reshape(GROUP, count_rows, rank), key_terms, value_terms], axis=2
        ).astype(BF),
        9,
        "reduce_latent",
    )

    latent_normed_grad = back[:, :rank]
    keyval_grad = jnp.concatenate(
        [rotate(back[:, rank : rank + HEAD_DIM], cosine, -sine), back[:, rank + HEAD_DIM :]], axis=1
    ).astype(BF)
    unused_second, second_pull = jax.vjp(norm_rows, latent, second_gain)
    latent_back, latent_gain_grad = second_pull(latent_normed_grad)
    first_grad = jnp.concatenate([latent_back.astype(BF), keyval_grad], axis=1)
    normed_grad = matmul("re,de->rd", first_grad, first_weight)
    unused_first, first_pull = jax.vjp(norm_rows, inputs, first_gain)
    input_norm_grad, norm_gain_grad = first_pull(normed_grad)
    grad_tokens = (
        middle_grad + input_norm_grad + jnp.where(valid[:, None], 0.0, upstream)
    ).astype(BF)
    gains = jnp.concatenate([norm_gain_grad, feed_gain_grad, latent_gain_grad])
    gains = jnp.pad(gains.reshape(-1, rank), ((0, 16 - gains.size // rank), (0, wide - rank)))
    grad_all, normed_rows = gather_layer(
        [jnp.concatenate([first_grad, gains.astype(BF)], axis=0), normed], 10, "gather_last"
    )
    normed_rows = normed_rows.reshape(all_rows, model)
    gain_sums = jnp.sum(grad_all[:, count_rows:, :rank].astype(F32), axis=0)
    lines = model // rank
    columns = wide // QUAD
    grad_slice = lax.dynamic_slice_in_dim(
        grad_all[:, :count_rows].reshape(all_rows, wide), quad * columns, columns, axis=1
    )
    half_rows = lax.dynamic_index_in_dim(
        normed_rows.reshape(all_rows, layers * QUAD, PAIR, half), hid, 2, keepdims=False
    ).reshape(all_rows, model // PAIR)
    grad_first = matmul("rd,re->de", half_rows, grad_slice).astype(BF)
    small_sums = jnp.concatenate(
        [
            gain_sums[:lines].reshape(layers, span),
            gain_sums[lines : 2 * lines].reshape(layers, span),
            gain_sums[2 * lines].reshape(layers, rank_span),
        ],
        axis=1,
    )
    flat = 16 * columns
    small_sums = jnp.pad(small_sums, ((0, 0), (0, flat - small_sums.shape[1])))
    last_sum = reduce_layers(
        jnp.concatenate(
            [
                grad_first.reshape(layers, QUAD * half, columns),
                small_sums.reshape(layers, 16, columns).astype(BF),
            ],
            axis=1,
        ).reshape(layers * (QUAD * half + 16), columns),
        layers,
    )
    first_sum = last_sum[: QUAD * half].reshape(QUAD, half, columns)
    small_sum = last_sum[QUAD * half :].astype(F32).reshape(-1)

    feed_terms, grad_all = lax.optimization_barrier((feed_terms, grad_all))
    feed = reduce_layer(
        feed_terms.astype(BF).reshape(GROUP, count_rows, model), 11, "reduce_feed"
    )
    output = jnp.where(valid[:, None], middle + feed, inputs).astype(BF)

    feed_sums = [f.reshape(QUAD, part, -1) for f in feed_sums]
    feed_own = swap(
        feed_sums,
        [quad_of] * 2,
        [quad_of] * 2,
        [f.shape for f in feed_sums],
        QUAD_FLIPS,
        12,
        "swap_feed_sums",
    )
    out_own, query_own, first_own = swap(
        [
            out_sum.reshape(QUAD, part, head_columns),
            query_sum.reshape(QUAD, rank_part, head_columns),
            first_sum,
        ],
        [quad_of] * 3,
        [
            columns_of(head_columns),
            columns_of(head_columns),
            lambda ref, i: ref.at[
                pl.ds(pl.multiple_of(lax.rem(i, PAIR) * half, half), half),
                pl.ds(pl.multiple_of(i // PAIR * columns, columns), columns),
            ],
        ],
        [(part, HEADS * HEAD_DIM), (rank_part, HEADS * HEAD_DIM), (part, wide)],
        ALL_FLIPS,
        13,
        "swap_sums",
    )
    grads = []
    for i in range(3):
        pieces = [
            f[:, :, i * (high - low) : (i + 1) * (high - low)]
            for f, (low, high) in zip(feed_own, chunks)
        ]
        grads.append(
            jnp.concatenate(pieces, axis=2)
            .transpose(1, 0, 2)
            .reshape(part, QUAD * units)
            .astype(F32)
        )
    return (
        output,
        grad_tokens,
        lax.dynamic_slice_in_dim(small_sum, quad * part, part),
        first_own[:, :rank].astype(F32),
        lax.dynamic_slice_in_dim(small_sum, 2 * span + quad * rank_part, rank_part),
        query_own.astype(F32),
        first_own[:, rank:].astype(F32),
        out_own.astype(F32),
        lax.dynamic_slice_in_dim(small_sum, span + quad * part, part),
        *grads,
    )


def solution(mesh):
    placed = (
        P(("batch", "hid"), None),
        P(("batch", "hid"), None),
        P("batch"),
        P("batch", None),
        P("batch"),
        P("batch", None),
        P("batch", None),
        P("batch", None),
        P("batch"),
        P("batch", "hid"),
        P("batch", "hid"),
        P("batch", "hid"),
        P(("batch", "hid"), None),
    )
    return jax.shard_map(
        functools.partial(per_device, mesh.shape["batch"] // QUAD),
        mesh=mesh,
        in_specs=placed,
        out_specs=(
            P(("batch", "hid"), None),
            P(("batch", "hid"), None),
            P("batch"),
            P("batch", None),
            P("batch"),
            P("batch", None),
            P("batch", None),
            P("batch", None),
            P("batch"),
            P("batch", "hid"),
            P("batch", "hid"),
            P("batch", "hid"),
        ),
        check_vma=False,
    )
```

```python
import functools

import jax
import jax.numpy as jnp
from jax import lax
from jax.experimental import pallas as pl
from jax.experimental.pallas import tpu as pltpu
from jax.sharding import PartitionSpec as P

HEADS = 16
HEAD_DIM = 256


EPS = 1e-05
ROPE_BASE = 10000.0
NEGATIVE = -1e30

QUAD = 4
PAIR = 2
GROUP = QUAD * PAIR
EXTRA = 32
MESH = pl.DeviceIdType.MESH
BF = jnp.bfloat16
F32 = jnp.float32


def matmul(spec, left, right):
    return jnp.einsum(spec, left, right, preferred_element_type=F32)


def norm_rows(values, gain):
    return values * lax.rsqrt(jnp.mean(values * values, axis=-1, keepdims=True) + EPS) * gain


def rotate(values, cosine, sine):
    half = values.shape[-1] // 2
    first = values[..., :half]
    second = values[..., half:]
    return jnp.concatenate(
        [first * cosine - second * sine, second * cosine + first * sine], axis=-1
    )


def layout(row_lengths, count_rows):
    slots = jnp.arange(row_lengths.shape[0], dtype=jnp.int32)
    ends = jnp.sum(jnp.where(slots[None, :] <= slots[:, None], row_lengths[None, :], 0), axis=1)
    starts = ends - row_lengths
    places = jnp.arange(count_rows, dtype=jnp.int32)
    segment = jnp.sum((places[:, None] >= ends[None, :]).astype(jnp.int32), axis=1)
    begins = jnp.concatenate([starts, ends[-1:]])
    labels = jnp.arange(begins.shape[0], dtype=jnp.int32)
    firsts = jnp.sum(jnp.where(segment[:, None] == labels[None, :], begins[None, :], 0), axis=1)
    position = places - firsts
    valid = places < ends[-1]
    allowed = (segment[:, None] == segment[None, :]) & (places[None, :] <= places[:, None])
    return (position, valid, allowed)


def angles_of(position, head_size):
    half = head_size // 2
    freqs = ROPE_BASE ** (-(jnp.arange(half, dtype=F32) * 2.0) / head_size)
    angle = position.astype(F32)[..., None] * freqs
    return (jnp.cos(angle), jnp.sin(angle))


def place():
    batch = lax.axis_index("batch")
    quad = lax.rem(batch, QUAD)
    return batch - quad, quad, lax.axis_index("hid")


def flip(quad, bits):
    core = lax.rem(quad, 2)
    chip = quad - core
    if bits & 1:
        core = 1 - core
    if bits & 2:
        chip = 2 - chip
    return chip + core


def after(value, *others):
    return lax.optimization_barrier((value, *others))[0]


def meet(peers):
    barrier = pltpu.get_barrier_semaphore()
    for peer in peers:
        pl.semaphore_signal(barrier, inc=1, device_id=peer, device_id_type=MESH)
    pl.semaphore_wait(barrier, len(peers))


def ways_of(base, quad, hid):
    def spot(bits, turn):
        return (flip(quad, bits), 1 - hid if turn else hid)

    def address(f):
        q, h = spot(*f)
        return (base + q, h)

    def index(f):
        q, h = spot(*f)
        return q * PAIR + h

    return address, index


ACROSS, ALONG, CORNER, MATE, SELF = (2, 0), (0, 1), (2, 1), (1, 0), (0, 0)


def gather_kernel(count, cuts, puts, *refs):
    ins, outs = refs[:count], refs[count : 2 * count]
    local_sem, send_sem, recv_sem = refs[2 * count :]
    base, quad, hid = place()
    address, index = ways_of(base, quad, hid)
    meet([address(f) for f in (ACROSS, ALONG, MATE)])

    def part(ref, i, h):
        cut, size = cuts[i]
        return ref.at[pl.ds(0, cut)] if h == 0 else ref.at[pl.ds(cut, size - cut)]

    def spot(i, f):
        return puts[i](outs[i], index(f))

    def copy(i, j, source, target, f):
        return pltpu.make_async_remote_copy(
            src_ref=source,
            dst_ref=target,
            send_sem=send_sem.at[i, j],
            recv_sem=recv_sem.at[i, j],
            device_id=address(f),
            device_id_type=MESH,
        )

    started = []

    def start(one):
        one.start()
        started.append(one)

    for i in range(count):
        for j, f, h in ((0, ACROSS, 0), (3, ALONG, 1), (1, ACROSS, 1), (2, ALONG, 0)):
            start(copy(i, j, part(ins[i], i, h), part(spot(i, SELF), i, h), f))
        start(copy(i, 6, ins[i], spot(i, SELF), MATE))
        pltpu.make_async_copy(ins[i], spot(i, SELF), local_sem.at[i]).start()

    def arrived(i, j, where, f):
        copy(i, j, where, where, f).wait_recv()

    for i in range(count):
        where = part(spot(i, ACROSS), i, 0)
        arrived(i, 0, where, ACROSS)
        start(copy(i, 4, where, where, ALONG))
        where = part(spot(i, ALONG), i, 1)
        arrived(i, 3, where, ALONG)
        start(copy(i, 5, where, where, ACROSS))
        arrived(i, 1, part(spot(i, ACROSS), i, 1), ACROSS)
        where = spot(i, ACROSS)
        start(copy(i, 7, where, where, MATE))
        arrived(i, 2, part(spot(i, ALONG), i, 0), ALONG)
        where = spot(i, ALONG)
        start(copy(i, 8, where, where, MATE))
    for i in range(count):
        where = part(spot(i, CORNER), i, 0)
        arrived(i, 4, where, ALONG)
        start(copy(i, 9, where, where, MATE))
        where = part(spot(i, CORNER), i, 1)
        arrived(i, 5, where, ACROSS)
        start(copy(i, 10, where, where, MATE))
    for i in range(count):
        pltpu.make_async_copy(ins[i], spot(i, SELF), local_sem.at[i]).wait()
        arrived(i, 6, spot(i, MATE), MATE)
        arrived(i, 7, spot(i, (ACROSS[0] ^ 1, ACROSS[1])), MATE)
        arrived(i, 8, spot(i, (ALONG[0] ^ 1, ALONG[1])), MATE)
        corner = spot(i, (CORNER[0] ^ 1, CORNER[1]))
        arrived(i, 9, part(corner, i, 0), MATE)
        arrived(i, 10, part(corner, i, 1), MATE)
    for one in started:
        one.wait_send()


def stacked(ref, place):
    return ref.at[place]


def inside(ref, place):
    return ref.at[:, place]


def gather_layer(arrays, ident, name, puts=None):
    count = len(arrays)
    puts = puts or [stacked] * count
    shapes = [
        (GROUP,) + a.shape if p is stacked else (a.shape[0], GROUP) + a.shape[1:]
        for a, p in zip(arrays, puts)
    ]
    cuts = [
        (a.shape[0] // 2 if a.ndim > 2 else a.shape[0] // 32 * 16, a.shape[0]) for a in arrays
    ]
    moved = sum(a.size * 2 * GROUP for a in arrays)
    return pl.pallas_call(
        functools.partial(gather_kernel, count, cuts, puts),
        out_shape=[jax.ShapeDtypeStruct(s, a.dtype) for s, a in zip(shapes, arrays)],
        in_specs=[pl.BlockSpec(memory_space=pl.ANY)] * count,
        out_specs=[pl.BlockSpec(memory_space=pl.ANY)] * count,
        scratch_shapes=[
            pltpu.SemaphoreType.DMA((count,)),
            pltpu.SemaphoreType.DMA((count, 11)),
            pltpu.SemaphoreType.DMA((count, 11)),
        ],
        compiler_params=pltpu.CompilerParams(collective_id=ident, has_side_effects=True),
        cost_estimate=pl.CostEstimate(flops=0, bytes_accessed=16 * moved, transcendentals=0),
        name=name,
    )(*arrays)


def reduce_kernel(in_ref, out_ref, own, mate_in, sums, relay, far_in, local_sem, send_sem, recv_sem):
    base, quad, hid = place()
    address, index = ways_of(base, quad, hid)
    rows = out_ref.shape[0]
    half = rows // 2
    step = 16
    ways = [CORNER, ACROSS, ALONG, SELF]
    meet([address(f) for f in (ACROSS, ALONG, MATE)])
    started = []

    def copy(j, source, target, f):
        return pltpu.make_async_remote_copy(
            src_ref=source,
            dst_ref=target,
            send_sem=send_sem.at[j],
            recv_sem=recv_sem.at[j],
            device_id=address(f),
            device_id_type=MESH,
        )

    def start(one):
        one.start()
        started.append(one)
        return one

    to_mate, local = [], []
    for j, f in enumerate(ways):
        to_mate.append(start(copy(j, in_ref.at[index((f[0] ^ 1, f[1]))], mate_in.at[j], MATE)))
        local.append(pltpu.make_async_copy(in_ref.at[index(f)], own.at[j], local_sem.at[j]))
        local[-1].start()

    def ready(j):
        local[j].wait()
        to_mate[j].wait_recv()

    def add(j, first, count, more=None):
        def body(r, carry):
            at = pl.ds(pl.multiple_of(first + r * step, step), step)
            value = own[j, at, :].astype(F32) + mate_in[j, at, :].astype(F32)
            if more is not None:
                value += more[pl.ds(pl.multiple_of(r * step, step), step), :].astype(F32)
            sums[j, at, :] = value.astype(BF)
            return carry

        lax.fori_loop(0, count // step, body, 0)

    low, high = pl.ds(0, half), pl.ds(half, half)
    ready(0)
    add(0, 0, half)
    by_across = start(copy(4, sums.at[0, low], relay.at[0], ACROSS))
    add(0, half, half)
    by_along = start(copy(5, sums.at[0, high], relay.at[1], ALONG))
    ready(1)
    add(1, 0, half)
    across_low = start(copy(6, sums.at[1, low], far_in.at[0, low], ACROSS))
    ready(2)
    add(2, half, half)
    along_high = start(copy(7, sums.at[2, high], far_in.at[1, high], ALONG))
    by_across.wait_recv()
    add(2, 0, half, relay.at[0])
    along_low = start(copy(8, sums.at[2, low], far_in.at[1, low], ALONG))
    by_along.wait_recv()
    add(1, half, half, relay.at[1])
    across_high = start(copy(9, sums.at[1, high], far_in.at[0, high], ACROSS))
    ready(3)
    for one in (across_low, along_high, along_low, across_high):
        one.wait_recv()

    def total(r, carry):
        at = pl.ds(pl.multiple_of(r * step, step), step)
        out_ref[at, :] = (
            own[3, at, :].astype(F32)
            + mate_in[3, at, :].astype(F32)
            + far_in[0, at, :].astype(F32)
            + far_in[1, at, :].astype(F32)
        )
        return carry

    lax.fori_loop(0, rows // step, total, 0)
    for one in started:
        one.wait_send()


def reduce_layer(blocks, ident, name):
    rows, columns = blocks.shape[1:]
    return pl.pallas_call(
        reduce_kernel,
        out_shape=jax.ShapeDtypeStruct((rows, columns), F32),
        in_specs=[pl.BlockSpec(memory_space=pl.ANY)],
        out_specs=pl.BlockSpec(memory_space=pltpu.VMEM),
        scratch_shapes=[
            pltpu.VMEM((4, rows, columns), BF),
            pltpu.VMEM((4, rows, columns), BF),
            pltpu.VMEM((3, rows, columns), BF),
            pltpu.VMEM((2, rows // 2, columns), BF),
            pltpu.VMEM((2, rows, columns), BF),
            pltpu.SemaphoreType.DMA((4,)),
            pltpu.SemaphoreType.DMA((10,)),
            pltpu.SemaphoreType.DMA((10,)),
        ],
        compiler_params=pltpu.CompilerParams(
            collective_id=ident, has_side_effects=True, vmem_limit_bytes=40 * 2**20
        ),
        cost_estimate=pl.CostEstimate(
            flops=0, bytes_accessed=16 * blocks.size * 2, transcendentals=0
        ),
        name=name,
    )(blocks)


def swap_kernel(count, takes, puts, flips, *refs):
    ins, outs = refs[:count], refs[count : 2 * count]
    local_sem, send_sem, recv_sem = refs[2 * count :]
    base, quad, hid = place()
    address, index = ways_of(base, quad, hid)
    meet([address(f) for f in flips])

    def copy(i, j, f, owner):
        return pltpu.make_async_remote_copy(
            src_ref=takes[i](ins[i], index(f)),
            dst_ref=puts[i](outs[i], owner),
            send_sem=send_sem.at[i, j],
            recv_sem=recv_sem.at[i, j],
            device_id=address(f),
            device_id_type=MESH,
        )

    me = index(SELF)
    for i in range(count):
        for j, f in enumerate(flips):
            copy(i, j, f, me).start()
        pltpu.make_async_copy(takes[i](ins[i], me), puts[i](outs[i], me), local_sem.at[i]).start()
    for i in range(count):
        pltpu.make_async_copy(takes[i](ins[i], me), puts[i](outs[i], me), local_sem.at[i]).wait()
        for j, f in enumerate(flips):
            copy(i, j, f, index(f)).wait_recv()
    for i in range(count):
        for j, f in enumerate(flips):
            copy(i, j, f, me).wait_send()


QUAD_FLIPS = ((3, 0), (2, 0), (1, 0))
ALL_FLIPS = ((3, 1), (2, 1), (3, 0), (2, 0), (1, 1), (0, 1), (1, 0))


def swap(arrays, takes, puts, shapes, flips, ident, name):
    count = len(arrays)
    moved = sum(a.size * 2 for a in arrays)
    return pl.pallas_call(
        functools.partial(swap_kernel, count, takes, puts, flips),
        out_shape=[jax.ShapeDtypeStruct(s, a.dtype) for s, a in zip(shapes, arrays)],
        in_specs=[pl.BlockSpec(memory_space=pl.ANY)] * count,
        out_specs=[pl.BlockSpec(memory_space=pl.ANY)] * count,
        scratch_shapes=[
            pltpu.SemaphoreType.DMA((count,)),
            pltpu.SemaphoreType.DMA((count, len(flips))),
            pltpu.SemaphoreType.DMA((count, len(flips))),
        ],
        compiler_params=pltpu.CompilerParams(collective_id=ident, has_side_effects=True),
        cost_estimate=pl.CostEstimate(flops=0, bytes_accessed=32 * moved, transcendentals=0),
        name=name,
    )(*arrays)


def columns_of(width):
    return lambda ref, i: ref.at[:, pl.ds(pl.multiple_of(i * width, width), width)]


def quad_of(ref, i):
    return ref.at[i // PAIR]


def layer_groups(layers):
    return [[z * QUAD + q for z in range(layers)] for q in range(QUAD)]


def gather_layers(unit, layers):
    return lax.all_gather(
        unit, "batch", axis=0, tiled=True, axis_index_groups=layer_groups(layers)
    )


def reduce_layers(blocks, layers):
    return lax.psum_scatter(
        blocks,
        "batch",
        scatter_dimension=0,
        tiled=True,
        axis_index_groups=layer_groups(layers),
    )


def per_device(
    layers,
    tokens,
    lengths,
    attention_gain,
    query_down,
    query_gain,
    query_up,
    key_value,
    output_weight,
    feed_gain,
    gate_weight,
    up_weight,
    down_weight,
    cotangent,
):
    count_rows, model = tokens.shape
    part, rank = query_down.shape
    rank_part = query_up.shape[0]
    half = part // PAIR
    wide = rank + key_value.shape[1]
    all_rows = GROUP * count_rows
    heads = HEADS // GROUP
    head_columns = heads * HEAD_DIM
    units = gate_weight.shape[1] // QUAD
    cut = -(-units // 256) * 128
    chunks = [(0, cut), (cut, units)]
    scale = HEAD_DIM ** (-0.5)
    base, quad, hid = place()
    layer = base // QUAD
    me = quad * PAIR + hid
    span = QUAD * part
    rank_span = QUAD * rank_part

    first_pack = jnp.concatenate(
        [
            lax.dynamic_slice_in_dim(
                jnp.concatenate([query_down, key_value], axis=1), hid * half, half, axis=0
            ),
            jnp.pad(
                jnp.concatenate([attention_gain, query_gain, feed_gain, lengths[0].astype(BF)])[None],
                ((0, EXTRA - 1), (0, wide - 2 * part - rank_part - lengths.shape[1])),
            ),
        ],
        axis=0,
    )
    first_slots = gather_layers(first_pack, layers).reshape(layers, half + EXTRA, wide)
    out_unit, query_unit = swap(
        [output_weight, query_up],
        [columns_of(head_columns)] * 2,
        [quad_of] * 2,
        [(QUAD, part, head_columns), (QUAD, rank_part, head_columns)],
        QUAD_FLIPS,
        1,
        "swap_heads",
    )
    head_all = gather_layers(
        jnp.concatenate(
            [query_unit.reshape(rank_span, head_columns), out_unit.reshape(span, head_columns)]
        ),
        layers,
    ).reshape(layers, rank_span + span, head_columns)
    query_slice = head_all[:, :rank_span].reshape(rank, head_columns)
    out_slice = head_all[:, rank_span:].reshape(model, head_columns)
    packs = [
        jnp.concatenate(
            [
                w.reshape(part, QUAD, units)[:, :, low:high]
                for w in (gate_weight, up_weight, down_weight)
            ],
            axis=2,
        ).transpose(1, 0, 2)
        for low, high in chunks
    ]
    feed_units = swap(
        packs, [quad_of] * 2, [quad_of] * 2, [p.shape for p in packs], QUAD_FLIPS, 2, "swap_feed"
    )

    small_width = -(-(2 * part + rank_part + lengths.shape[1]) // 128) * 128
    first_weight, small = gather_layer(
        [first_slots[:, :half], first_slots[:, half : half + 16, :small_width]],
        3,
        "gather_first",
        [inside, stacked],
    )
    feed_weights = [
        gather_layers(feed_units[0].reshape(span, -1), layers),
        gather_layers(after(feed_units[1], first_weight).reshape(span, -1), layers),
    ]
    first_weight = first_weight.reshape(model, wide)
    small = small[:, :, 0].transpose(1, 0, 2)
    first_gain = small[:, ::PAIR, :part].reshape(model).astype(F32)
    second_gain = small[:, ::PAIR, part : part + rank_part].reshape(rank).astype(F32)
    third_gain = (
        small[:, ::PAIR, part + rank_part : 2 * part + rank_part].reshape(model).astype(F32)
    )
    begin = 2 * part + rank_part
    all_lengths = small[:, :, begin : begin + lengths.shape[1]].astype(jnp.int32)
    all_lengths = lax.dynamic_index_in_dim(all_lengths, layer, 0, keepdims=False)

    inputs = tokens.astype(F32)
    upstream = cotangent.astype(F32)
    position, valid, allowed_own = layout(lengths[0], count_rows)
    cosine, sine = angles_of(position, HEAD_DIM)
    normed = norm_rows(inputs, first_gain).astype(BF)
    first = matmul("rd,de->re", normed, first_weight)
    latent = first[:, :rank]
    keyvals = first[:, rank:]
    latent_normed = norm_rows(latent, second_gain).astype(BF)
    key_rot = rotate(keyvals[:, :HEAD_DIM], cosine, sine).astype(BF)
    value_rows = keyvals[:, HEAD_DIM:].astype(BF)
    [rows_all] = gather_layer(
        [jnp.concatenate([latent_normed, key_rot, value_rows], axis=1)], 4, "gather_latent"
    )
    latent_all = rows_all[:, :, :rank].reshape(all_rows, rank)
    key_all = rows_all[:, :, rank : rank + HEAD_DIM]
    value_all = rows_all[:, :, rank + HEAD_DIM :]

    positions, valids, allowed = jax.vmap(lambda one: layout(one, count_rows))(all_lengths)
    cosines, sines = angles_of(positions, HEAD_DIM)
    queries = matmul("rc,cf->rf", latent_all, query_slice).reshape(
        GROUP, count_rows, heads, HEAD_DIM
    )
    query_rot = rotate(queries, cosines[:, :, None, :], sines[:, :, None, :]).astype(BF)

    def masked_scores():
        raw = matmul("gqhd,gkd->ghqk", query_rot, key_all) * scale
        return jnp.where(allowed[:, None], raw, NEGATIVE)

    scores = masked_scores()
    highest = jnp.max(scores, axis=-1, keepdims=True)
    raised = jnp.exp(scores - highest)
    totals = jnp.sum(raised, axis=-1, keepdims=True)
    probs = (raised / totals).astype(BF)
    logsum = highest + jnp.log(totals)
    mixed = matmul("ghqk,gkd->gqhd", probs, value_all).reshape(all_rows, head_columns).astype(BF)
    branch_terms = matmul("rf,df->rd", mixed, out_slice).astype(BF)
    branch = reduce_layer(branch_terms.reshape(GROUP, count_rows, model), 5, "reduce_branch")
    middle = inputs + branch
    normed_ffn = norm_rows(middle, third_gain).astype(BF)
    kept = jnp.where(valid[:, None], upstream, 0.0)
    feed_rows, grad_rows = gather_layer([normed_ffn, kept.astype(BF)], 6, "gather_feed")
    feed_rows = feed_rows.reshape(all_rows, model)
    grad_rows = grad_rows.reshape(all_rows, model)

    feed_terms = jnp.zeros((all_rows, model), F32)
    ffn_terms = jnp.zeros((all_rows, model), F32)
    grad_packs = []
    normed_rows = []
    for weights, (low, high) in zip(feed_weights, chunks):
        width = high - low
        gate_up, down = weights[:, : 2 * width], weights[:, 2 * width :]
        both = matmul("rd,df->rf", feed_rows, gate_up)
        gate, up = both[:, :width], both[:, width:]
        hidden_grad = matmul("rd,df->rf", grad_rows, down)
        sigma = jax.nn.sigmoid(gate)
        activated = gate * sigma
        slope = sigma * (1.0 + gate * (1.0 - sigma))
        hidden = (activated * up).astype(BF)
        both_grad = jnp.concatenate(
            [hidden_grad * up * slope, hidden_grad * activated], axis=1
        ).astype(BF)
        grad_both = matmul("rd,rf->df", feed_rows, both_grad).astype(BF)
        grad_down = matmul("rd,rf->df", grad_rows, hidden).astype(BF)
        grad_pack = jnp.concatenate([grad_both, grad_down], axis=1)
        grad_packs.append(grad_pack)
        if not normed_rows:
            normed_rows = gather_layer([after(normed, grad_pack)], 15, "gather_normed")
        feed_rows = after(feed_rows, grad_pack, normed_rows[0])
        both_grad = after(both_grad, grad_pack)
        ffn_terms = ffn_terms + matmul("rf,df->rd", both_grad, gate_up)
        feed_terms = feed_terms + matmul("rf,df->rd", hidden, down)
    ffn_grad = reduce_layer(
        ffn_terms.astype(BF).reshape(GROUP, count_rows, model), 7, "reduce_ffn_grad"
    )
    unused_third, third_pull = jax.vjp(norm_rows, middle, third_gain)
    middle_norm_grad, feed_gain_grad = third_pull(ffn_grad)
    middle_grad = kept + middle_norm_grad
    [branch_rows] = gather_layer([middle_grad.astype(BF)], 8, "gather_branch")
    feed_sums = [reduce_layers(grad_packs[0], layers)]
    branch_rows = branch_rows.reshape(all_rows, model)

    mixed_grad = (
        matmul("rd,df->rf", branch_rows, out_slice)
        .astype(BF)
        .reshape(GROUP, count_rows, heads, HEAD_DIM)
    )
    probs_back = jnp.exp(masked_scores() - logsum)
    prob_grad = matmul("gqhd,gkd->ghqk", mixed_grad, value_all)
    score_grad = (
        probs_back * (prob_grad - jnp.sum(probs_back * prob_grad, axis=-1, keepdims=True))
    ).astype(BF)
    value_terms = matmul("ghqk,gqhd->gkd", probs, mixed_grad)
    query_rot_grad = matmul("ghqk,gkd->gqhd", score_grad, key_all) * scale
    key_terms = matmul("ghqk,gqhd->gkd", score_grad, query_rot) * scale
    query_grad = (
        rotate(query_rot_grad, cosines[:, :, None, :], -sines[:, :, None, :])
        .reshape(all_rows, head_columns)
        .astype(BF)
    )
    latent_terms = matmul("rf,cf->rc", query_grad, query_slice)
    back_terms = jnp.concatenate(
        [latent_terms.reshape(GROUP, count_rows, rank), key_terms, value_terms], axis=2
    ).astype(BF)
    second_pack = after(grad_packs[1], feed_sums[0], back_terms)
    feed_sums.append(reduce_layers(second_pack, layers))
    back = reduce_layer(after(back_terms, second_pack), 9, "reduce_latent")
    grad_query = matmul("rc,rf->cf", latent_all, after(query_grad, back)).astype(BF)
    grad_out = matmul("rd,rf->df", after(branch_rows, back), mixed).astype(BF)
    head_pack = jnp.concatenate(
        [
            grad_query.reshape(layers, rank_span, head_columns),
            grad_out.reshape(layers, span, head_columns),
        ],
        axis=1,
    ).reshape(rank + model, head_columns)

    latent_normed_grad = back[:, :rank]
    keyval_grad = jnp.concatenate(
        [rotate(back[:, rank : rank + HEAD_DIM], cosine, -sine), back[:, rank + HEAD_DIM :]], axis=1
    ).astype(BF)
    unused_second, second_pull = jax.vjp(norm_rows, latent, second_gain)
    latent_back, latent_gain_grad = second_pull(latent_normed_grad)
    first_grad = jnp.concatenate([latent_back.astype(BF), keyval_grad], axis=1)
    normed_grad = matmul("re,de->rd", first_grad, first_weight)
    unused_first, first_pull = jax.vjp(norm_rows, inputs, first_gain)
    input_norm_grad, norm_gain_grad = first_pull(normed_grad)
    grad_tokens = (
        middle_grad + input_norm_grad + jnp.where(valid[:, None], 0.0, upstream)
    ).astype(BF)
    first_grad = after(first_grad, head_pack)
    gains = jnp.concatenate([norm_gain_grad, feed_gain_grad, latent_gain_grad])
    gains = jnp.pad(gains.reshape(-1, rank), ((0, 16 - gains.size // rank), (0, wide - rank)))
    [grad_all] = gather_layer(
        [jnp.concatenate([first_grad, gains.astype(BF)], axis=0)], 10, "gather_last"
    )
    feed_terms = feed_terms.astype(BF)
    feed = reduce_layer(
        feed_terms.reshape(GROUP, count_rows, model), 11, "reduce_feed"
    )
    output = jnp.where(valid[:, None], middle + feed, inputs).astype(BF)

    head_pack = after(head_pack, grad_all, feed_terms)
    head_sum = reduce_layers(after(head_pack, *feed_sums), layers)
    query_sum, out_sum = head_sum[:rank_span], head_sum[rank_span:]
    normed_rows = normed_rows[0].reshape(all_rows, model)
    gain_sums = jnp.sum(grad_all[:, count_rows:, :rank].astype(F32), axis=0)
    lines = model // rank
    columns = wide // QUAD
    grad_slice = lax.dynamic_slice_in_dim(
        grad_all[:, :count_rows].reshape(all_rows, wide), quad * columns, columns, axis=1
    )
    grad_first = matmul("rd,re->de", normed_rows, grad_slice).astype(BF)
    grad_first = lax.dynamic_index_in_dim(
        grad_first.reshape(layers * QUAD, PAIR, half, columns), hid, 1, keepdims=False
    )
    small_sums = jnp.concatenate(
        [
            gain_sums[:lines].reshape(layers, span),
            gain_sums[lines : 2 * lines].reshape(layers, span),
            gain_sums[2 * lines].reshape(layers, rank_span),
        ],
        axis=1,
    )
    flat = 16 * columns
    small_sums = jnp.pad(small_sums, ((0, 0), (0, flat - small_sums.shape[1])))
    feed_sums = [f.reshape(QUAD, part, -1) for f in feed_sums]
    quads = [[z * QUAD + q for q in range(QUAD)] for z in range(layers)]
    feed_own = lax.all_to_all(
        jnp.concatenate(feed_sums, axis=2), "batch", 0, 0, axis_index_groups=quads, tiled=True
    )
    last_pack = jnp.concatenate(
        [
            grad_first.reshape(layers, QUAD * half, columns),
            small_sums.reshape(layers, 16, columns).astype(BF),
        ],
        axis=1,
    ).reshape(layers * (QUAD * half + 16), columns)
    last_sum = reduce_layers(after(after(last_pack, feed, feed_own), head_sum), layers)
    first_sum = last_sum[: QUAD * half].reshape(QUAD, half, columns)
    small_sum = last_sum[QUAD * half :].astype(F32).reshape(-1)

    groups = [[z * GROUP + i for i in range(GROUP)] for z in range(layers)]
    head_own = lax.all_to_all(
        jnp.repeat(
            jnp.concatenate(
                [
                    query_sum.reshape(QUAD, rank_part, head_columns),
                    out_sum.reshape(QUAD, part, head_columns),
                ],
                axis=1,
            ),
            PAIR,
            axis=0,
        ),
        ("batch", "hid"),
        0,
        0,
        axis_index_groups=groups,
        tiled=True,
    )
    head_own = head_own.transpose(1, 0, 2).reshape(rank_part + part, HEADS * HEAD_DIM)
    query_own, out_own = head_own[:rank_part], head_own[rank_part:]
    [first_own] = swap(
        [first_sum],
        [quad_of],
        [
            lambda ref, i: ref.at[
                pl.ds(pl.multiple_of(lax.rem(i, PAIR) * half, half), half),
                pl.ds(pl.multiple_of(i // PAIR * columns, columns), columns),
            ],
        ],
        [(part, wide)],
        ALL_FLIPS,
        14,
        "swap_last_sums",
    )
    grads = []
    for i in range(3):
        pieces = []
        begin = 0
        for low, high in chunks:
            width = high - low
            pieces.append(feed_own[:, :, begin + i * width : begin + (i + 1) * width])
            begin += 3 * width
        grads.append(
            jnp.concatenate(pieces, axis=2)
            .transpose(1, 0, 2)
            .reshape(part, QUAD * units)
            .astype(F32)
        )
    return (
        output,
        grad_tokens,
        lax.dynamic_slice_in_dim(small_sum, quad * part, part),
        first_own[:, :rank].astype(F32),
        lax.dynamic_slice_in_dim(small_sum, 2 * span + quad * rank_part, rank_part),
        query_own.astype(F32),
        first_own[:, rank:].astype(F32),
        out_own.astype(F32),
        lax.dynamic_slice_in_dim(small_sum, span + quad * part, part),
        *grads,
    )


def solution(mesh):
    placed = (
        P(("batch", "hid"), None),
        P(("batch", "hid"), None),
        P("batch"),
        P("batch", None),
        P("batch"),
        P("batch", None),
        P("batch", None),
        P("batch", None),
        P("batch"),
        P("batch", "hid"),
        P("batch", "hid"),
        P("batch", "hid"),
        P(("batch", "hid"), None),
    )
    return jax.shard_map(
        functools.partial(per_device, mesh.shape["batch"] // QUAD),
        mesh=mesh,
        in_specs=placed,
        out_specs=(
            P(("batch", "hid"), None),
            P(("batch", "hid"), None),
            P("batch"),
            P("batch", None),
            P("batch"),
            P("batch", None),
            P("batch", None),
            P("batch", None),
            P("batch"),
            P("batch", "hid"),
            P("batch", "hid"),
            P("batch", "hid"),
        ),
        check_vma=False,
    )
```

```python
import functools

import jax
import jax.numpy as jnp
from jax import lax
from jax.experimental import pallas as pl
from jax.experimental.pallas import tpu as pltpu
from jax.sharding import PartitionSpec as P

HEADS = 16
HEAD_DIM = 256


EPS = 1e-05
ROPE_BASE = 10000.0
NEGATIVE = -1e30

QUAD = 4
PAIR = 2
GROUP = QUAD * PAIR
EXTRA = 24
MESH = pl.DeviceIdType.MESH
BF = jnp.bfloat16
F32 = jnp.float32


def matmul(spec, left, right):
    return jnp.einsum(spec, left, right, preferred_element_type=F32)


def norm_rows(values, gain):
    return values * lax.rsqrt(jnp.mean(values * values, axis=-1, keepdims=True) + EPS) * gain


def rotate(values, cosine, sine):
    half = values.shape[-1] // 2
    first = values[..., :half]
    second = values[..., half:]
    return jnp.concatenate(
        [first * cosine - second * sine, second * cosine + first * sine], axis=-1
    )


def layout(row_lengths, count_rows):
    slots = jnp.arange(row_lengths.shape[0], dtype=jnp.int32)
    ends = jnp.sum(jnp.where(slots[None, :] <= slots[:, None], row_lengths[None, :], 0), axis=1)
    starts = ends - row_lengths
    places = jnp.arange(count_rows, dtype=jnp.int32)
    segment = jnp.sum((places[:, None] >= ends[None, :]).astype(jnp.int32), axis=1)
    begins = jnp.concatenate([starts, ends[-1:]])
    labels = jnp.arange(begins.shape[0], dtype=jnp.int32)
    firsts = jnp.sum(jnp.where(segment[:, None] == labels[None, :], begins[None, :], 0), axis=1)
    position = places - firsts
    valid = places < ends[-1]
    allowed = (segment[:, None] == segment[None, :]) & (places[None, :] <= places[:, None])
    return (position, valid, allowed)


def angles_of(position, head_size):
    half = head_size // 2
    freqs = ROPE_BASE ** (-(jnp.arange(half, dtype=F32) * 2.0) / head_size)
    angle = position.astype(F32)[..., None] * freqs
    return (jnp.cos(angle), jnp.sin(angle))


def place():
    batch = lax.axis_index("batch")
    quad = lax.rem(batch, QUAD)
    return batch - quad, quad, lax.axis_index("hid")


def flip(quad, bits):
    core = lax.rem(quad, 2)
    chip = quad - core
    if bits & 1:
        core = 1 - core
    if bits & 2:
        chip = 2 - chip
    return chip + core


def after(value, *others):
    return lax.optimization_barrier((value, *others))[0]


def meet(peers):
    barrier = pltpu.get_barrier_semaphore()
    for peer in peers:
        pl.semaphore_signal(barrier, inc=1, device_id=peer, device_id_type=MESH)
    pl.semaphore_wait(barrier, len(peers))


def ways_of(base, quad, hid):
    def spot(bits, turn):
        return (flip(quad, bits), 1 - hid if turn else hid)

    def address(f):
        q, h = spot(*f)
        return (base + q, h)

    def index(f):
        q, h = spot(*f)
        return q * PAIR + h

    return address, index


ACROSS, ALONG, CORNER, MATE, SELF = (2, 0), (0, 1), (2, 1), (1, 0), (0, 0)


def gather_kernel(count, cuts, puts, *refs):
    ins, outs = refs[:count], refs[count : 2 * count]
    local_sem, send_sem, recv_sem = refs[2 * count :]
    base, quad, hid = place()
    address, index = ways_of(base, quad, hid)
    meet([address(f) for f in (ACROSS, ALONG, MATE)])

    def part(ref, i, h):
        cut, size = cuts[i]
        return ref.at[pl.ds(0, cut)] if h == 0 else ref.at[pl.ds(cut, size - cut)]

    def spot(i, f):
        return puts[i](outs[i], index(f))

    def copy(i, j, source, target, f):
        return pltpu.make_async_remote_copy(
            src_ref=source,
            dst_ref=target,
            send_sem=send_sem.at[i, j],
            recv_sem=recv_sem.at[i, j],
            device_id=address(f),
            device_id_type=MESH,
        )

    started = []

    def start(one):
        one.start()
        started.append(one)

    for i in range(count):
        for j, f, h in ((0, ACROSS, 0), (3, ALONG, 1), (1, ACROSS, 1), (2, ALONG, 0)):
            start(copy(i, j, part(ins[i], i, h), part(spot(i, SELF), i, h), f))
        start(copy(i, 6, ins[i], spot(i, SELF), MATE))
        pltpu.make_async_copy(ins[i], spot(i, SELF), local_sem.at[i]).start()

    def arrived(i, j, where, f):
        copy(i, j, where, where, f).wait_recv()

    for i in range(count):
        where = part(spot(i, ACROSS), i, 0)
        arrived(i, 0, where, ACROSS)
        start(copy(i, 4, where, where, ALONG))
        where = part(spot(i, ALONG), i, 1)
        arrived(i, 3, where, ALONG)
        start(copy(i, 5, where, where, ACROSS))
        arrived(i, 1, part(spot(i, ACROSS), i, 1), ACROSS)
        where = spot(i, ACROSS)
        start(copy(i, 7, where, where, MATE))
        arrived(i, 2, part(spot(i, ALONG), i, 0), ALONG)
        where = spot(i, ALONG)
        start(copy(i, 8, where, where, MATE))
    for i in range(count):
        where = part(spot(i, CORNER), i, 0)
        arrived(i, 4, where, ALONG)
        start(copy(i, 9, where, where, MATE))
        where = part(spot(i, CORNER), i, 1)
        arrived(i, 5, where, ACROSS)
        start(copy(i, 10, where, where, MATE))
    for i in range(count):
        pltpu.make_async_copy(ins[i], spot(i, SELF), local_sem.at[i]).wait()
        arrived(i, 6, spot(i, MATE), MATE)
        arrived(i, 7, spot(i, (ACROSS[0] ^ 1, ACROSS[1])), MATE)
        arrived(i, 8, spot(i, (ALONG[0] ^ 1, ALONG[1])), MATE)
        corner = spot(i, (CORNER[0] ^ 1, CORNER[1]))
        arrived(i, 9, part(corner, i, 0), MATE)
        arrived(i, 10, part(corner, i, 1), MATE)
    for one in started:
        one.wait_send()


def stacked(ref, place):
    return ref.at[place]


def inside(ref, place):
    return ref.at[:, place]


def gather_layer(arrays, ident, name, puts=None):
    count = len(arrays)
    puts = puts or [stacked] * count
    shapes = [
        (GROUP,) + a.shape if p is stacked else (a.shape[0], GROUP) + a.shape[1:]
        for a, p in zip(arrays, puts)
    ]
    cuts = [
        (a.shape[0] // 2 if a.ndim > 2 else a.shape[0] // 32 * 16, a.shape[0]) for a in arrays
    ]
    moved = sum(a.size * 2 * GROUP for a in arrays)
    return pl.pallas_call(
        functools.partial(gather_kernel, count, cuts, puts),
        out_shape=[jax.ShapeDtypeStruct(s, a.dtype) for s, a in zip(shapes, arrays)],
        in_specs=[pl.BlockSpec(memory_space=pl.ANY)] * count,
        out_specs=[pl.BlockSpec(memory_space=pl.ANY)] * count,
        scratch_shapes=[
            pltpu.SemaphoreType.DMA((count,)),
            pltpu.SemaphoreType.DMA((count, 11)),
            pltpu.SemaphoreType.DMA((count, 11)),
        ],
        compiler_params=pltpu.CompilerParams(collective_id=ident, has_side_effects=True),
        cost_estimate=pl.CostEstimate(flops=0, bytes_accessed=16 * moved, transcendentals=0),
        name=name,
    )(*arrays)


def reduce_kernel(in_ref, out_ref, own, mate_in, sums, relay, far_in, local_sem, send_sem, recv_sem):
    base, quad, hid = place()
    address, index = ways_of(base, quad, hid)
    rows = out_ref.shape[0]
    half = rows // 2
    step = 16
    ways = [CORNER, ACROSS, ALONG, SELF]
    meet([address(f) for f in (ACROSS, ALONG, MATE)])
    started = []

    def copy(j, source, target, f):
        return pltpu.make_async_remote_copy(
            src_ref=source,
            dst_ref=target,
            send_sem=send_sem.at[j],
            recv_sem=recv_sem.at[j],
            device_id=address(f),
            device_id_type=MESH,
        )

    def start(one):
        one.start()
        started.append(one)
        return one

    to_mate, local = [], []
    for j, f in enumerate(ways):
        to_mate.append(start(copy(j, in_ref.at[index((f[0] ^ 1, f[1]))], mate_in.at[j], MATE)))
        local.append(pltpu.make_async_copy(in_ref.at[index(f)], own.at[j], local_sem.at[j]))
        local[-1].start()

    def ready(j):
        local[j].wait()
        to_mate[j].wait_recv()

    def add(j, first, count, more=None):
        def body(r, carry):
            at = pl.ds(pl.multiple_of(first + r * step, step), step)
            value = own[j, at, :].astype(F32) + mate_in[j, at, :].astype(F32)
            if more is not None:
                value += more[pl.ds(pl.multiple_of(r * step, step), step), :].astype(F32)
            sums[j, at, :] = value.astype(BF)
            return carry

        lax.fori_loop(0, count // step, body, 0)

    low, high = pl.ds(0, half), pl.ds(half, half)
    ready(0)
    add(0, 0, half)
    by_across = start(copy(4, sums.at[0, low], relay.at[0], ACROSS))
    add(0, half, half)
    by_along = start(copy(5, sums.at[0, high], relay.at[1], ALONG))
    ready(1)
    add(1, 0, half)
    across_low = start(copy(6, sums.at[1, low], far_in.at[0, low], ACROSS))
    ready(2)
    add(2, half, half)
    along_high = start(copy(7, sums.at[2, high], far_in.at[1, high], ALONG))
    by_across.wait_recv()
    add(2, 0, half, relay.at[0])
    along_low = start(copy(8, sums.at[2, low], far_in.at[1, low], ALONG))
    by_along.wait_recv()
    add(1, half, half, relay.at[1])
    across_high = start(copy(9, sums.at[1, high], far_in.at[0, high], ACROSS))
    ready(3)
    for one in (across_low, along_high, along_low, across_high):
        one.wait_recv()

    def total(r, carry):
        at = pl.ds(pl.multiple_of(r * step, step), step)
        out_ref[at, :] = (
            own[3, at, :].astype(F32)
            + mate_in[3, at, :].astype(F32)
            + far_in[0, at, :].astype(F32)
            + far_in[1, at, :].astype(F32)
        )
        return carry

    lax.fori_loop(0, rows // step, total, 0)
    for one in started:
        one.wait_send()


def reduce_layer(blocks, ident, name):
    rows, columns = blocks.shape[1:]
    return pl.pallas_call(
        reduce_kernel,
        out_shape=jax.ShapeDtypeStruct((rows, columns), F32),
        in_specs=[pl.BlockSpec(memory_space=pl.ANY)],
        out_specs=pl.BlockSpec(memory_space=pltpu.VMEM),
        scratch_shapes=[
            pltpu.VMEM((4, rows, columns), BF),
            pltpu.VMEM((4, rows, columns), BF),
            pltpu.VMEM((3, rows, columns), BF),
            pltpu.VMEM((2, rows // 2, columns), BF),
            pltpu.VMEM((2, rows, columns), BF),
            pltpu.SemaphoreType.DMA((4,)),
            pltpu.SemaphoreType.DMA((10,)),
            pltpu.SemaphoreType.DMA((10,)),
        ],
        compiler_params=pltpu.CompilerParams(
            collective_id=ident, has_side_effects=True, vmem_limit_bytes=40 * 2**20
        ),
        cost_estimate=pl.CostEstimate(
            flops=0, bytes_accessed=16 * blocks.size * 2, transcendentals=0
        ),
        name=name,
    )(blocks)


def swap_kernel(count, takes, puts, flips, *refs):
    ins, outs = refs[:count], refs[count : 2 * count]
    local_sem, send_sem, recv_sem = refs[2 * count :]
    base, quad, hid = place()
    address, index = ways_of(base, quad, hid)
    meet([address(f) for f in flips])

    def copy(i, j, f, owner):
        return pltpu.make_async_remote_copy(
            src_ref=takes[i](ins[i], index(f)),
            dst_ref=puts[i](outs[i], owner),
            send_sem=send_sem.at[i, j],
            recv_sem=recv_sem.at[i, j],
            device_id=address(f),
            device_id_type=MESH,
        )

    me = index(SELF)
    for i in range(count):
        for j, f in enumerate(flips):
            copy(i, j, f, me).start()
        pltpu.make_async_copy(takes[i](ins[i], me), puts[i](outs[i], me), local_sem.at[i]).start()
    for i in range(count):
        pltpu.make_async_copy(takes[i](ins[i], me), puts[i](outs[i], me), local_sem.at[i]).wait()
        for j, f in enumerate(flips):
            copy(i, j, f, index(f)).wait_recv()
    for i in range(count):
        for j, f in enumerate(flips):
            copy(i, j, f, me).wait_send()


QUAD_FLIPS = ((3, 0), (2, 0), (1, 0))
ALL_FLIPS = ((3, 1), (2, 1), (3, 0), (2, 0), (1, 1), (0, 1), (1, 0))


def swap(arrays, takes, puts, shapes, flips, ident, name):
    count = len(arrays)
    moved = sum(a.size * 2 for a in arrays)
    return pl.pallas_call(
        functools.partial(swap_kernel, count, takes, puts, flips),
        out_shape=[jax.ShapeDtypeStruct(s, a.dtype) for s, a in zip(shapes, arrays)],
        in_specs=[pl.BlockSpec(memory_space=pl.ANY)] * count,
        out_specs=[pl.BlockSpec(memory_space=pl.ANY)] * count,
        scratch_shapes=[
            pltpu.SemaphoreType.DMA((count,)),
            pltpu.SemaphoreType.DMA((count, len(flips))),
            pltpu.SemaphoreType.DMA((count, len(flips))),
        ],
        compiler_params=pltpu.CompilerParams(collective_id=ident, has_side_effects=True),
        cost_estimate=pl.CostEstimate(flops=0, bytes_accessed=32 * moved, transcendentals=0),
        name=name,
    )(*arrays)


def spread_kernel(blocks_ref, first_ref, second_ref):
    count = first_ref.shape[0]
    columns = blocks_ref.shape[2]
    for i in range(blocks_ref.shape[0]):
        at = pl.ds(i * columns, columns)
        first_ref[:, at] = blocks_ref[i, :count, :].astype(F32)
        second_ref[:, at] = blocks_ref[i, count:, :].astype(F32)


def spread(blocks, count):
    n, rows, columns = blocks.shape
    return pl.pallas_call(
        spread_kernel,
        grid=(n // 2,),
        in_specs=[pl.BlockSpec((2, rows, columns), lambda i: (i, 0, 0))],
        out_specs=[
            pl.BlockSpec((count, 2 * columns), lambda i: (0, i)),
            pl.BlockSpec((rows - count, 2 * columns), lambda i: (0, i)),
        ],
        out_shape=[
            jax.ShapeDtypeStruct((count, n * columns), F32),
            jax.ShapeDtypeStruct((rows - count, n * columns), F32),
        ],
        cost_estimate=pl.CostEstimate(
            flops=0, bytes_accessed=6 * blocks.size, transcendentals=0
        ),
        name="spread_heads",
    )(blocks)


def columns_of(width):
    return lambda ref, i: ref.at[:, pl.ds(pl.multiple_of(i * width, width), width)]


def quad_of(ref, i):
    return ref.at[i // PAIR]


def layer_groups(layers):
    return [[z * QUAD + q for z in range(layers)] for q in range(QUAD)]


def gather_layers(unit, layers):
    return lax.all_gather(
        unit, "batch", axis=0, tiled=True, axis_index_groups=layer_groups(layers)
    )


def reduce_layers(blocks, layers):
    return lax.psum_scatter(
        blocks,
        "batch",
        scatter_dimension=0,
        tiled=True,
        axis_index_groups=layer_groups(layers),
    )


def per_device(
    layers,
    tokens,
    lengths,
    attention_gain,
    query_down,
    query_gain,
    query_up,
    key_value,
    output_weight,
    feed_gain,
    gate_weight,
    up_weight,
    down_weight,
    cotangent,
):
    count_rows, model = tokens.shape
    part, rank = query_down.shape
    rank_part = query_up.shape[0]
    half = part // PAIR
    wide = rank + key_value.shape[1]
    all_rows = GROUP * count_rows
    heads = HEADS // GROUP
    head_columns = heads * HEAD_DIM
    units = gate_weight.shape[1] // QUAD
    cut = -(-units // 256) * 128
    chunks = [(0, cut), (cut, units)]
    scale = HEAD_DIM ** (-0.5)
    base, quad, hid = place()
    layer = base // QUAD
    me = quad * PAIR + hid
    span = QUAD * part
    rank_span = QUAD * rank_part

    first_pack = jnp.concatenate(
        [
            lax.dynamic_slice_in_dim(
                jnp.concatenate([query_down, key_value], axis=1), hid * half, half, axis=0
            ),
            jnp.pad(
                jnp.concatenate([attention_gain, query_gain, feed_gain, lengths[0].astype(BF)])[None],
                ((0, EXTRA - 1), (0, wide - 2 * part - rank_part - lengths.shape[1])),
            ),
        ],
        axis=0,
    )
    first_slots = gather_layers(first_pack, layers).reshape(layers, half + EXTRA, wide)
    out_unit, query_unit = swap(
        [output_weight, query_up],
        [columns_of(head_columns)] * 2,
        [quad_of] * 2,
        [(QUAD, part, head_columns), (QUAD, rank_part, head_columns)],
        QUAD_FLIPS,
        1,
        "swap_heads",
    )
    head_all = gather_layers(
        jnp.concatenate(
            [query_unit.reshape(rank_span, head_columns), out_unit.reshape(span, head_columns)]
        ),
        layers,
    ).reshape(layers, rank_span + span, head_columns)
    query_slice = head_all[:, :rank_span].reshape(rank, head_columns)
    out_slice = head_all[:, rank_span:].reshape(model, head_columns)
    packs = [
        jnp.concatenate(
            [
                w.reshape(part, QUAD, units)[:, :, low:high]
                for w in (gate_weight, up_weight, down_weight)
            ],
            axis=2,
        ).transpose(1, 0, 2)
        for low, high in chunks
    ]
    feed_units = swap(
        packs, [quad_of] * 2, [quad_of] * 2, [p.shape for p in packs], QUAD_FLIPS, 2, "swap_feed"
    )

    small_width = -(-(2 * part + rank_part + lengths.shape[1]) // 128) * 128
    first_weight, small = gather_layer(
        [first_slots[:, :half], first_slots[:, half : half + 16, :small_width]],
        3,
        "gather_first",
        [inside, stacked],
    )
    feed_weights = [
        gather_layers(feed_units[0].reshape(span, -1), layers),
        gather_layers(after(feed_units[1], first_weight).reshape(span, -1), layers),
    ]
    first_weight = first_weight.reshape(model, wide)
    small = small[:, :, 0].transpose(1, 0, 2)
    first_gain = small[:, ::PAIR, :part].reshape(model).astype(F32)
    second_gain = small[:, ::PAIR, part : part + rank_part].reshape(rank).astype(F32)
    third_gain = (
        small[:, ::PAIR, part + rank_part : 2 * part + rank_part].reshape(model).astype(F32)
    )
    begin = 2 * part + rank_part
    all_lengths = small[:, :, begin : begin + lengths.shape[1]].astype(jnp.int32)
    all_lengths = lax.dynamic_index_in_dim(all_lengths, layer, 0, keepdims=False)

    inputs = tokens.astype(F32)
    upstream = cotangent.astype(F32)
    position, valid, allowed_own = layout(lengths[0], count_rows)
    cosine, sine = angles_of(position, HEAD_DIM)
    normed = norm_rows(inputs, first_gain).astype(BF)
    first = matmul("rd,de->re", normed, first_weight)
    latent = first[:, :rank]
    keyvals = first[:, rank:]
    latent_normed = norm_rows(latent, second_gain).astype(BF)
    key_rot = rotate(keyvals[:, :HEAD_DIM], cosine, sine).astype(BF)
    value_rows = keyvals[:, HEAD_DIM:].astype(BF)
    latent_all, key_all, value_all = gather_layer(
        [latent_normed, key_rot, value_rows], 4, "gather_latent"
    )
    latent_all = latent_all.reshape(all_rows, rank)

    positions, valids, allowed = jax.vmap(lambda one: layout(one, count_rows))(all_lengths)
    cosines, sines = angles_of(positions, HEAD_DIM)
    queries = matmul("rc,cf->rf", latent_all, query_slice).reshape(
        GROUP, count_rows, heads, HEAD_DIM
    )
    query_rot = rotate(queries, cosines[:, :, None, :], sines[:, :, None, :]).astype(BF)

    def masked_scores():
        raw = matmul("gqhd,gkd->ghqk", query_rot, key_all) * scale
        return jnp.where(allowed[:, None], raw, NEGATIVE)

    scores = masked_scores()
    highest = jnp.max(scores, axis=-1, keepdims=True)
    raised = jnp.exp(scores - highest)
    totals = jnp.sum(raised, axis=-1, keepdims=True)
    probs = (raised / totals).astype(BF)
    logsum = highest + jnp.log(totals)
    mixed = matmul("ghqk,gkd->gqhd", probs, value_all).reshape(all_rows, head_columns).astype(BF)
    branch_terms = matmul("rf,df->rd", mixed, out_slice).astype(BF)
    branch = reduce_layer(branch_terms.reshape(GROUP, count_rows, model), 5, "reduce_branch")
    middle = inputs + branch
    normed_ffn = norm_rows(middle, third_gain).astype(BF)
    kept = jnp.where(valid[:, None], upstream, 0.0)
    feed_rows, grad_rows = gather_layer([normed_ffn, kept.astype(BF)], 6, "gather_feed")
    feed_rows = feed_rows.reshape(all_rows, model)
    grad_rows = grad_rows.reshape(all_rows, model)

    hiddens = []
    ffn_terms = jnp.zeros((all_rows, model), F32)
    grad_packs = []
    normed_rows = []
    for weights, (low, high) in zip(feed_weights, chunks):
        width = high - low
        gate_up, down = weights[:, : 2 * width], weights[:, 2 * width :]
        both = matmul("rd,df->rf", feed_rows, gate_up)
        gate, up = both[:, :width], both[:, width:]
        hidden_grad = matmul("rd,df->rf", grad_rows, down)
        sigma = jax.nn.sigmoid(gate)
        activated = gate * sigma
        slope = sigma * (1.0 + gate * (1.0 - sigma))
        hidden = (activated * up).astype(BF)
        both_grad = jnp.concatenate(
            [hidden_grad * up * slope, hidden_grad * activated], axis=1
        ).astype(BF)
        grad_both = matmul("rd,rf->df", feed_rows, both_grad).astype(BF)
        grad_down = matmul("rd,rf->df", grad_rows, hidden).astype(BF)
        grad_pack = jnp.concatenate([grad_both, grad_down], axis=1)
        grad_packs.append(grad_pack)
        if not normed_rows:
            normed_rows = gather_layer([after(normed, grad_pack)], 15, "gather_normed")
        feed_rows = after(feed_rows, grad_pack, normed_rows[0])
        both_grad = after(both_grad, grad_pack)
        ffn_terms = ffn_terms + matmul("rf,df->rd", both_grad, gate_up)
        hiddens.append((hidden, down))
    ffn_grad = reduce_layer(
        ffn_terms.astype(BF).reshape(GROUP, count_rows, model), 7, "reduce_ffn_grad"
    )
    unused_third, third_pull = jax.vjp(norm_rows, middle, third_gain)
    middle_norm_grad, feed_gain_grad = third_pull(ffn_grad)
    middle_grad = kept + middle_norm_grad
    [branch_rows] = gather_layer([middle_grad.astype(BF)], 8, "gather_branch")
    feed_sums = [reduce_layers(grad_packs[0], layers)]
    branch_rows = branch_rows.reshape(all_rows, model)

    mixed_grad = (
        matmul("rd,df->rf", branch_rows, out_slice)
        .astype(BF)
        .reshape(GROUP, count_rows, heads, HEAD_DIM)
    )
    probs_back = jnp.exp(masked_scores() - logsum)
    prob_grad = matmul("gqhd,gkd->ghqk", mixed_grad, value_all)
    score_grad = (
        probs_back * (prob_grad - jnp.sum(probs_back * prob_grad, axis=-1, keepdims=True))
    ).astype(BF)
    value_terms = matmul("ghqk,gqhd->gkd", probs, mixed_grad)
    query_rot_grad = matmul("ghqk,gkd->gqhd", score_grad, key_all) * scale
    key_terms = matmul("ghqk,gqhd->gkd", score_grad, query_rot) * scale
    query_grad = (
        rotate(query_rot_grad, cosines[:, :, None, :], -sines[:, :, None, :])
        .reshape(all_rows, head_columns)
        .astype(BF)
    )
    latent_terms = matmul("rf,cf->rc", query_grad, query_slice)
    back_terms = jnp.concatenate(
        [latent_terms.reshape(GROUP, count_rows, rank), key_terms, value_terms], axis=2
    ).astype(BF)
    second_pack = after(grad_packs[1], feed_sums[0], score_grad)
    feed_sums.append(reduce_layers(second_pack, layers))
    back = reduce_layer(after(back_terms, second_pack), 9, "reduce_latent")
    grad_query = matmul("rc,rf->cf", latent_all, after(query_grad, back)).astype(BF)
    grad_out = matmul("rd,rf->df", after(branch_rows, back), mixed).astype(BF)
    head_pack = jnp.concatenate(
        [
            grad_query.reshape(layers, rank_span, head_columns),
            grad_out.reshape(layers, span, head_columns),
        ],
        axis=1,
    ).reshape(rank + model, head_columns)

    latent_normed_grad = back[:, :rank]
    keyval_grad = jnp.concatenate(
        [rotate(back[:, rank : rank + HEAD_DIM], cosine, -sine), back[:, rank + HEAD_DIM :]], axis=1
    ).astype(BF)
    unused_second, second_pull = jax.vjp(norm_rows, latent, second_gain)
    latent_back, latent_gain_grad = second_pull(latent_normed_grad)
    first_grad = jnp.concatenate([latent_back.astype(BF), keyval_grad], axis=1)
    normed_grad = matmul("re,de->rd", first_grad, first_weight)
    unused_first, first_pull = jax.vjp(norm_rows, inputs, first_gain)
    input_norm_grad, norm_gain_grad = first_pull(normed_grad)
    grad_tokens = (
        middle_grad + input_norm_grad + jnp.where(valid[:, None], 0.0, upstream)
    ).astype(BF)
    quads = [[z * QUAD + q for q in range(QUAD)] for z in range(layers)]

    def swap_quads(sums):
        return lax.all_to_all(
            sums.reshape(QUAD, part, -1), "batch", 0, 0, axis_index_groups=quads, tiled=True
        )

    feed_own = [swap_quads(after(feed_sums[0], back))]
    first_grad = after(first_grad, head_pack, feed_own[0])
    gains = jnp.concatenate([norm_gain_grad, feed_gain_grad, latent_gain_grad])
    gains = jnp.pad(gains.reshape(-1, rank), ((0, 32 - gains.size // rank), (0, 0)))
    grad_all, gains_all = gather_layer([first_grad, gains.astype(BF)], 10, "gather_last")
    feed_terms = sum(
        matmul("rf,df->rd", after(hidden, grad_all), down) for hidden, down in hiddens
    ).astype(BF)
    feed = reduce_layer(
        feed_terms.reshape(GROUP, count_rows, model), 11, "reduce_feed"
    )
    output = jnp.where(valid[:, None], middle + feed, inputs).astype(BF)

    head_pack = after(head_pack, grad_all)
    head_sum = reduce_layers(after(head_pack, *feed_sums), layers)
    query_sum, out_sum = head_sum[:rank_span], head_sum[rank_span:]
    normed_rows = normed_rows[0].reshape(all_rows, model)
    gain_sums = jnp.sum(gains_all.astype(F32), axis=0)
    lines = model // rank
    columns = wide // QUAD
    grad_slice = lax.dynamic_slice_in_dim(
        grad_all.reshape(all_rows, wide), quad * columns, columns, axis=1
    )
    grad_first = matmul("rd,re->de", normed_rows, grad_slice).astype(BF)
    grad_first = lax.dynamic_index_in_dim(
        grad_first.reshape(layers * QUAD, PAIR, half, columns), hid, 1, keepdims=False
    )
    small_sums = jnp.concatenate(
        [
            gain_sums[:lines].reshape(layers, span),
            gain_sums[lines : 2 * lines].reshape(layers, span),
            gain_sums[2 * lines].reshape(layers, rank_span),
        ],
        axis=1,
    )
    flat = 16 * columns
    small_sums = jnp.pad(small_sums, ((0, 0), (0, flat - small_sums.shape[1])))
    feed_own.append(swap_quads(feed_sums[1]))
    last_pack = jnp.concatenate(
        [
            grad_first.reshape(layers, QUAD * half, columns),
            small_sums.reshape(layers, 16, columns).astype(BF),
        ],
        axis=1,
    ).reshape(layers * (QUAD * half + 16), columns)
    last_pack = after(after(last_pack, feed, feed_own[1]), head_sum)
    last_sum = reduce_layers(last_pack, layers)
    first_sum = last_sum[: QUAD * half].reshape(QUAD, half, columns)
    small_sum = last_sum[QUAD * half :].astype(F32).reshape(-1)

    grads = []
    for i in range(3):
        pieces = [
            f[:, :, i * (high - low) : (i + 1) * (high - low)]
            for f, (low, high) in zip(feed_own, chunks)
        ]
        grads.append(
            jnp.concatenate(pieces, axis=2)
            .transpose(1, 0, 2)
            .reshape(part, QUAD * units)
            .astype(F32)
        )
    query_sum = after(query_sum, *grads)
    groups = [[z * GROUP + i for i in range(GROUP)] for z in range(layers)]
    head_own = lax.all_to_all(
        jnp.repeat(
            jnp.concatenate(
                [
                    query_sum.reshape(QUAD, rank_part, head_columns),
                    out_sum.reshape(QUAD, part, head_columns),
                ],
                axis=1,
            ),
            PAIR,
            axis=0,
        ),
        ("batch", "hid"),
        0,
        0,
        axis_index_groups=groups,
        tiled=True,
    )
    [first_own] = swap(
        [first_sum],
        [quad_of],
        [
            lambda ref, i: ref.at[
                pl.ds(pl.multiple_of(lax.rem(i, PAIR) * half, half), half),
                pl.ds(pl.multiple_of(i // PAIR * columns, columns), columns),
            ],
        ],
        [(part, wide)],
        ALL_FLIPS,
        14,
        "swap_last_sums",
    )
    query_own, out_own = spread(after(head_own, first_own), rank_part)
    return (
        output,
        grad_tokens,
        lax.dynamic_slice_in_dim(small_sum, quad * part, part),
        first_own[:, :rank].astype(F32),
        lax.dynamic_slice_in_dim(small_sum, 2 * span + quad * rank_part, rank_part),
        query_own,
        first_own[:, rank:].astype(F32),
        out_own,
        lax.dynamic_slice_in_dim(small_sum, span + quad * part, part),
        *grads,
    )


def solution(mesh):
    placed = (
        P(("batch", "hid"), None),
        P(("batch", "hid"), None),
        P("batch"),
        P("batch", None),
        P("batch"),
        P("batch", None),
        P("batch", None),
        P("batch", None),
        P("batch"),
        P("batch", "hid"),
        P("batch", "hid"),
        P("batch", "hid"),
        P(("batch", "hid"), None),
    )
    return jax.shard_map(
        functools.partial(per_device, mesh.shape["batch"] // QUAD),
        mesh=mesh,
        in_specs=placed,
        out_specs=(
            P(("batch", "hid"), None),
            P(("batch", "hid"), None),
            P("batch"),
            P("batch", None),
            P("batch"),
            P("batch", None),
            P("batch", None),
            P("batch", None),
            P("batch"),
            P("batch", "hid"),
            P("batch", "hid"),
            P("batch", "hid"),
        ),
        check_vma=False,
    )
```

```python
import functools

import jax
import jax.numpy as jnp
from jax import lax
from jax.experimental import pallas as pl
from jax.experimental.pallas import tpu as pltpu
from jax.sharding import PartitionSpec as P

HEADS = 16
HEAD_DIM = 256


EPS = 1e-05
ROPE_BASE = 10000.0
NEGATIVE = -1e30

QUAD = 4
PAIR = 2
GROUP = QUAD * PAIR
EXTRA = 24
MESH = pl.DeviceIdType.MESH
BF = jnp.bfloat16
F32 = jnp.float32


def matmul(spec, left, right):
    return jnp.einsum(spec, left, right, preferred_element_type=F32)


def norm_rows(values, gain):
    return values * lax.rsqrt(jnp.mean(values * values, axis=-1, keepdims=True) + EPS) * gain


def rotate(values, cosine, sine):
    half = values.shape[-1] // 2
    first = values[..., :half]
    second = values[..., half:]
    return jnp.concatenate(
        [first * cosine - second * sine, second * cosine + first * sine], axis=-1
    )


def layout(row_lengths, count_rows):
    slots = jnp.arange(row_lengths.shape[0], dtype=jnp.int32)
    ends = jnp.sum(jnp.where(slots[None, :] <= slots[:, None], row_lengths[None, :], 0), axis=1)
    starts = ends - row_lengths
    places = jnp.arange(count_rows, dtype=jnp.int32)
    segment = jnp.sum((places[:, None] >= ends[None, :]).astype(jnp.int32), axis=1)
    begins = jnp.concatenate([starts, ends[-1:]])
    labels = jnp.arange(begins.shape[0], dtype=jnp.int32)
    firsts = jnp.sum(jnp.where(segment[:, None] == labels[None, :], begins[None, :], 0), axis=1)
    position = places - firsts
    valid = places < ends[-1]
    allowed = (segment[:, None] == segment[None, :]) & (places[None, :] <= places[:, None])
    return (position, valid, allowed)


def angles_of(position, head_size):
    half = head_size // 2
    freqs = ROPE_BASE ** (-(jnp.arange(half, dtype=F32) * 2.0) / head_size)
    angle = position.astype(F32)[..., None] * freqs
    return (jnp.cos(angle), jnp.sin(angle))


def place():
    batch = lax.axis_index("batch")
    quad = lax.rem(batch, QUAD)
    return batch - quad, quad, lax.axis_index("hid")


def flip(quad, bits):
    core = lax.rem(quad, 2)
    chip = quad - core
    if bits & 1:
        core = 1 - core
    if bits & 2:
        chip = 2 - chip
    return chip + core


def after(value, *others):
    return lax.optimization_barrier((value, *others))[0]


def meet(peers):
    barrier = pltpu.get_barrier_semaphore()
    for peer in peers:
        pl.semaphore_signal(barrier, inc=1, device_id=peer, device_id_type=MESH)
    pl.semaphore_wait(barrier, len(peers))


def ways_of(base, quad, hid):
    def spot(bits, turn):
        return (flip(quad, bits), 1 - hid if turn else hid)

    def address(f):
        q, h = spot(*f)
        return (base + q, h)

    def index(f):
        q, h = spot(*f)
        return q * PAIR + h

    return address, index


ACROSS, ALONG, CORNER, MATE, SELF = (2, 0), (0, 1), (2, 1), (1, 0), (0, 0)


def gather_kernel(count, cuts, puts, *refs):
    ins, outs = refs[:count], refs[count : 2 * count]
    local_sem, send_sem, recv_sem = refs[2 * count :]
    base, quad, hid = place()
    address, index = ways_of(base, quad, hid)
    meet([address(f) for f in (ACROSS, ALONG, MATE)])

    def part(ref, i, h):
        cut, size = cuts[i]
        return ref.at[pl.ds(0, cut)] if h == 0 else ref.at[pl.ds(cut, size - cut)]

    def spot(i, f):
        return puts[i](outs[i], index(f))

    def copy(i, j, source, target, f):
        return pltpu.make_async_remote_copy(
            src_ref=source,
            dst_ref=target,
            send_sem=send_sem.at[i, j],
            recv_sem=recv_sem.at[i, j],
            device_id=address(f),
            device_id_type=MESH,
        )

    started = []

    def start(one):
        one.start()
        started.append(one)

    for i in range(count):
        for j, f, h in ((0, ACROSS, 0), (3, ALONG, 1), (1, ACROSS, 1), (2, ALONG, 0)):
            start(copy(i, j, part(ins[i], i, h), part(spot(i, SELF), i, h), f))
        start(copy(i, 6, ins[i], spot(i, SELF), MATE))
        pltpu.make_async_copy(ins[i], spot(i, SELF), local_sem.at[i]).start()

    def arrived(i, j, where, f):
        copy(i, j, where, where, f).wait_recv()

    for i in range(count):
        where = part(spot(i, ACROSS), i, 0)
        arrived(i, 0, where, ACROSS)
        start(copy(i, 4, where, where, ALONG))
        where = part(spot(i, ALONG), i, 1)
        arrived(i, 3, where, ALONG)
        start(copy(i, 5, where, where, ACROSS))
        arrived(i, 1, part(spot(i, ACROSS), i, 1), ACROSS)
        where = spot(i, ACROSS)
        start(copy(i, 7, where, where, MATE))
        arrived(i, 2, part(spot(i, ALONG), i, 0), ALONG)
        where = spot(i, ALONG)
        start(copy(i, 8, where, where, MATE))
    for i in range(count):
        where = part(spot(i, CORNER), i, 0)
        arrived(i, 4, where, ALONG)
        start(copy(i, 9, where, where, MATE))
        where = part(spot(i, CORNER), i, 1)
        arrived(i, 5, where, ACROSS)
        start(copy(i, 10, where, where, MATE))
    for i in range(count):
        pltpu.make_async_copy(ins[i], spot(i, SELF), local_sem.at[i]).wait()
        arrived(i, 6, spot(i, MATE), MATE)
        arrived(i, 7, spot(i, (ACROSS[0] ^ 1, ACROSS[1])), MATE)
        arrived(i, 8, spot(i, (ALONG[0] ^ 1, ALONG[1])), MATE)
        corner = spot(i, (CORNER[0] ^ 1, CORNER[1]))
        arrived(i, 9, part(corner, i, 0), MATE)
        arrived(i, 10, part(corner, i, 1), MATE)
    for one in started:
        one.wait_send()


def stacked(ref, place):
    return ref.at[place]


def inside(ref, place):
    return ref.at[:, place]


def gather_layer(arrays, ident, name, puts=None):
    count = len(arrays)
    puts = puts or [stacked] * count
    shapes = [
        (GROUP,) + a.shape if p is stacked else (a.shape[0], GROUP) + a.shape[1:]
        for a, p in zip(arrays, puts)
    ]
    cuts = [
        (a.shape[0] // 2 if a.ndim > 2 else a.shape[0] // 32 * 16, a.shape[0]) for a in arrays
    ]
    moved = sum(a.size * 2 * GROUP for a in arrays)
    return pl.pallas_call(
        functools.partial(gather_kernel, count, cuts, puts),
        out_shape=[jax.ShapeDtypeStruct(s, a.dtype) for s, a in zip(shapes, arrays)],
        in_specs=[pl.BlockSpec(memory_space=pl.ANY)] * count,
        out_specs=[pl.BlockSpec(memory_space=pl.ANY)] * count,
        scratch_shapes=[
            pltpu.SemaphoreType.DMA((count,)),
            pltpu.SemaphoreType.DMA((count, 11)),
            pltpu.SemaphoreType.DMA((count, 11)),
        ],
        compiler_params=pltpu.CompilerParams(collective_id=ident, has_side_effects=True),
        cost_estimate=pl.CostEstimate(flops=0, bytes_accessed=16 * moved, transcendentals=0),
        name=name,
    )(*arrays)


def reduce_kernel(in_ref, out_ref, own, mate_in, sums, relay, far_in, local_sem, send_sem, recv_sem):
    base, quad, hid = place()
    address, index = ways_of(base, quad, hid)
    rows = out_ref.shape[0]
    half = rows // 2
    step = 16
    ways = [CORNER, ACROSS, ALONG, SELF]
    meet([address(f) for f in (ACROSS, ALONG, MATE)])
    started = []

    def copy(j, source, target, f):
        return pltpu.make_async_remote_copy(
            src_ref=source,
            dst_ref=target,
            send_sem=send_sem.at[j],
            recv_sem=recv_sem.at[j],
            device_id=address(f),
            device_id_type=MESH,
        )

    def start(one):
        one.start()
        started.append(one)
        return one

    to_mate, local = [], []
    for j, f in enumerate(ways):
        to_mate.append(start(copy(j, in_ref.at[index((f[0] ^ 1, f[1]))], mate_in.at[j], MATE)))
        local.append(pltpu.make_async_copy(in_ref.at[index(f)], own.at[j], local_sem.at[j]))
        local[-1].start()

    def ready(j):
        local[j].wait()
        to_mate[j].wait_recv()

    def add(j, first, count, more=None):
        def body(r, carry):
            at = pl.ds(pl.multiple_of(first + r * step, step), step)
            value = own[j, at, :].astype(F32) + mate_in[j, at, :].astype(F32)
            if more is not None:
                value += more[pl.ds(pl.multiple_of(r * step, step), step), :].astype(F32)
            sums[j, at, :] = value.astype(BF)
            return carry

        lax.fori_loop(0, count // step, body, 0)

    low, high = pl.ds(0, half), pl.ds(half, half)
    ready(0)
    add(0, 0, half)
    by_across = start(copy(4, sums.at[0, low], relay.at[0], ACROSS))
    add(0, half, half)
    by_along = start(copy(5, sums.at[0, high], relay.at[1], ALONG))
    ready(1)
    add(1, 0, half)
    across_low = start(copy(6, sums.at[1, low], far_in.at[0, low], ACROSS))
    ready(2)
    add(2, half, half)
    along_high = start(copy(7, sums.at[2, high], far_in.at[1, high], ALONG))
    by_across.wait_recv()
    add(2, 0, half, relay.at[0])
    along_low = start(copy(8, sums.at[2, low], far_in.at[1, low], ALONG))
    by_along.wait_recv()
    add(1, half, half, relay.at[1])
    across_high = start(copy(9, sums.at[1, high], far_in.at[0, high], ACROSS))
    ready(3)
    for one in (across_low, along_high, along_low, across_high):
        one.wait_recv()

    def total(r, carry):
        at = pl.ds(pl.multiple_of(r * step, step), step)
        out_ref[at, :] = (
            own[3, at, :].astype(F32)
            + mate_in[3, at, :].astype(F32)
            + far_in[0, at, :].astype(F32)
            + far_in[1, at, :].astype(F32)
        )
        return carry

    lax.fori_loop(0, rows // step, total, 0)
    for one in started:
        one.wait_send()


def reduce_layer(blocks, ident, name):
    rows, columns = blocks.shape[1:]
    return pl.pallas_call(
        reduce_kernel,
        out_shape=jax.ShapeDtypeStruct((rows, columns), F32),
        in_specs=[pl.BlockSpec(memory_space=pl.ANY)],
        out_specs=pl.BlockSpec(memory_space=pltpu.VMEM),
        scratch_shapes=[
            pltpu.VMEM((4, rows, columns), BF),
            pltpu.VMEM((4, rows, columns), BF),
            pltpu.VMEM((3, rows, columns), BF),
            pltpu.VMEM((2, rows // 2, columns), BF),
            pltpu.VMEM((2, rows, columns), BF),
            pltpu.SemaphoreType.DMA((4,)),
            pltpu.SemaphoreType.DMA((10,)),
            pltpu.SemaphoreType.DMA((10,)),
        ],
        compiler_params=pltpu.CompilerParams(
            collective_id=ident, has_side_effects=True, vmem_limit_bytes=40 * 2**20
        ),
        cost_estimate=pl.CostEstimate(
            flops=0, bytes_accessed=16 * blocks.size * 2, transcendentals=0
        ),
        name=name,
    )(blocks)


def swap_kernel(count, takes, puts, flips, *refs):
    ins, outs = refs[:count], refs[count : 2 * count]
    local_sem, send_sem, recv_sem = refs[2 * count :]
    base, quad, hid = place()
    address, index = ways_of(base, quad, hid)
    meet([address(f) for f in flips])

    def copy(i, j, f, owner):
        return pltpu.make_async_remote_copy(
            src_ref=takes[i](ins[i], index(f)),
            dst_ref=puts[i](outs[i], owner),
            send_sem=send_sem.at[i, j],
            recv_sem=recv_sem.at[i, j],
            device_id=address(f),
            device_id_type=MESH,
        )

    me = index(SELF)
    for i in range(count):
        for j, f in enumerate(flips):
            copy(i, j, f, me).start()
        pltpu.make_async_copy(takes[i](ins[i], me), puts[i](outs[i], me), local_sem.at[i]).start()
    for i in range(count):
        pltpu.make_async_copy(takes[i](ins[i], me), puts[i](outs[i], me), local_sem.at[i]).wait()
        for j, f in enumerate(flips):
            copy(i, j, f, index(f)).wait_recv()
    for i in range(count):
        for j, f in enumerate(flips):
            copy(i, j, f, me).wait_send()


QUAD_FLIPS = ((3, 0), (2, 0), (1, 0))
ALL_FLIPS = ((3, 1), (2, 1), (3, 0), (2, 0), (1, 1), (0, 1), (1, 0))


def swap(arrays, takes, puts, shapes, flips, ident, name):
    count = len(arrays)
    moved = sum(a.size * 2 for a in arrays)
    return pl.pallas_call(
        functools.partial(swap_kernel, count, takes, puts, flips),
        out_shape=[jax.ShapeDtypeStruct(s, a.dtype) for s, a in zip(shapes, arrays)],
        in_specs=[pl.BlockSpec(memory_space=pl.ANY)] * count,
        out_specs=[pl.BlockSpec(memory_space=pl.ANY)] * count,
        scratch_shapes=[
            pltpu.SemaphoreType.DMA((count,)),
            pltpu.SemaphoreType.DMA((count, len(flips))),
            pltpu.SemaphoreType.DMA((count, len(flips))),
        ],
        compiler_params=pltpu.CompilerParams(collective_id=ident, has_side_effects=True),
        cost_estimate=pl.CostEstimate(flops=0, bytes_accessed=32 * moved, transcendentals=0),
        name=name,
    )(*arrays)


def spread_kernel(blocks_ref, first_ref, second_ref):
    count = first_ref.shape[0]
    columns = blocks_ref.shape[2]
    for i in range(blocks_ref.shape[0]):
        at = pl.ds(i * columns, columns)
        first_ref[:, at] = blocks_ref[i, :count, :].astype(F32)
        second_ref[:, at] = blocks_ref[i, count:, :].astype(F32)


def spread(blocks, count):
    n, rows, columns = blocks.shape
    return pl.pallas_call(
        spread_kernel,
        grid=(n // 2,),
        in_specs=[pl.BlockSpec((2, rows, columns), lambda i: (i, 0, 0))],
        out_specs=[
            pl.BlockSpec((count, 2 * columns), lambda i: (0, i)),
            pl.BlockSpec((rows - count, 2 * columns), lambda i: (0, i)),
        ],
        out_shape=[
            jax.ShapeDtypeStruct((count, n * columns), F32),
            jax.ShapeDtypeStruct((rows - count, n * columns), F32),
        ],
        cost_estimate=pl.CostEstimate(
            flops=0, bytes_accessed=6 * blocks.size, transcendentals=0
        ),
        name="spread_heads",
    )(blocks)


def settle_kernel(count, takes, puts, results, *refs):
    ins, outs = refs[:count], refs[count : count + len(results)]
    landed = refs[count + len(results) : 2 * count + len(results)]
    local_sem, send_sem, recv_sem = refs[2 * count + len(results) :]
    base, quad, hid = place()
    address, index = ways_of(base, quad, hid)
    meet([address(f) for f in ALL_FLIPS])

    def copy(i, j, f, owner):
        return pltpu.make_async_remote_copy(
            src_ref=takes[i](ins[i], index(f) // PAIR),
            dst_ref=puts[i](landed[i], owner),
            send_sem=send_sem.at[i, j],
            recv_sem=recv_sem.at[i, j],
            device_id=address(f),
            device_id_type=MESH,
        )

    def local(i):
        return pltpu.make_async_copy(
            takes[i](ins[i], quad), puts[i](landed[i], index(SELF)), local_sem.at[i]
        )

    for i in range(count):
        for j, f in enumerate(ALL_FLIPS):
            copy(i, j, f, index(SELF)).start()
        local(i).start()
    for i in range(count):
        local(i).wait()
        for j, f in enumerate(ALL_FLIPS):
            copy(i, j, f, index(f)).wait_recv()
    step = 16
    for (i, begin, end), out in zip(results, outs):

        def body(r, carry, i=i, begin=begin, end=end, out=out):
            at = pl.ds(pl.multiple_of(r * step, step), step)
            out[at, :] = landed[i][at, begin:end].astype(F32)
            return carry

        lax.fori_loop(0, out.shape[0] // step, body, 0)
    for i in range(count):
        for j, f in enumerate(ALL_FLIPS):
            copy(i, j, f, index(SELF)).wait_send()


def settle(arrays, takes, puts, shapes, results, ident, name):
    count = len(arrays)
    moved = sum(s[0] * s[1] for s in shapes)
    return pl.pallas_call(
        functools.partial(settle_kernel, count, takes, puts, results),
        out_shape=[jax.ShapeDtypeStruct((shapes[i][0], e - b), F32) for i, b, e in results],
        in_specs=[pl.BlockSpec(memory_space=pl.ANY)] * count,
        out_specs=[pl.BlockSpec(memory_space=pltpu.VMEM)] * len(results),
        scratch_shapes=[pltpu.VMEM(s, BF) for s in shapes]
        + [
            pltpu.SemaphoreType.DMA((count,)),
            pltpu.SemaphoreType.DMA((count, len(ALL_FLIPS))),
            pltpu.SemaphoreType.DMA((count, len(ALL_FLIPS))),
        ],
        compiler_params=pltpu.CompilerParams(
            collective_id=ident, has_side_effects=True, vmem_limit_bytes=24 * 2**20
        ),
        cost_estimate=pl.CostEstimate(flops=0, bytes_accessed=64 * moved, transcendentals=0),
        name=name,
    )(*arrays)


def rows_of(begin, count):
    return lambda ref, q: ref.at[pl.ds(pl.multiple_of(begin + q * count, 16), count)]


def join_kernel(widths, blocks_ref, *outs):
    total = sum(widths)
    for i, out in enumerate(outs):
        for q in range(QUAD):
            begin, source = q * total, 0
            for width in widths:
                at = source + i * width
                out[:, begin : begin + width] = blocks_ref[q, :, at : at + width].astype(F32)
                begin += width
                source += 3 * width


def join(blocks, widths):
    rows, columns = blocks.shape[1], QUAD * sum(widths)
    strip = min(rows, 32)
    return pl.pallas_call(
        functools.partial(join_kernel, widths),
        grid=(rows // strip,),
        in_specs=[pl.BlockSpec((QUAD, strip, blocks.shape[2]), lambda i: (0, i, 0))],
        out_specs=[pl.BlockSpec((strip, columns), lambda i: (i, 0))] * 3,
        out_shape=[jax.ShapeDtypeStruct((rows, columns), F32)] * 3,
        cost_estimate=pl.CostEstimate(
            flops=0, bytes_accessed=18 * rows * columns, transcendentals=0
        ),
        name="join_feed",
    )(blocks)


def columns_of(width):
    return lambda ref, i: ref.at[:, pl.ds(pl.multiple_of(i * width, width), width)]


def quad_of(ref, i):
    return ref.at[i // PAIR]


def layer_groups(layers):
    return [[z * QUAD + q for z in range(layers)] for q in range(QUAD)]


def gather_layers(unit, layers):
    return lax.all_gather(
        unit, "batch", axis=0, tiled=True, axis_index_groups=layer_groups(layers)
    )


def reduce_layers(blocks, layers):
    return lax.psum_scatter(
        blocks,
        "batch",
        scatter_dimension=0,
        tiled=True,
        axis_index_groups=layer_groups(layers),
    )


def per_device(
    layers,
    tokens,
    lengths,
    attention_gain,
    query_down,
    query_gain,
    query_up,
    key_value,
    output_weight,
    feed_gain,
    gate_weight,
    up_weight,
    down_weight,
    cotangent,
):
    count_rows, model = tokens.shape
    part, rank = query_down.shape
    rank_part = query_up.shape[0]
    half = part // PAIR
    wide = rank + key_value.shape[1]
    all_rows = GROUP * count_rows
    heads = HEADS // GROUP
    head_columns = heads * HEAD_DIM
    units = gate_weight.shape[1] // QUAD
    cut = -(-units // 256) * 128
    chunks = [(0, cut), (cut, units)]
    scale = HEAD_DIM ** (-0.5)
    base, quad, hid = place()
    layer = base // QUAD
    me = quad * PAIR + hid
    span = QUAD * part
    rank_span = QUAD * rank_part

    first_pack = jnp.concatenate(
        [
            lax.dynamic_slice_in_dim(
                jnp.concatenate([query_down, key_value], axis=1), hid * half, half, axis=0
            ),
            jnp.pad(
                jnp.concatenate([attention_gain, query_gain, feed_gain, lengths[0].astype(BF)])[None],
                ((0, EXTRA - 1), (0, wide - 2 * part - rank_part - lengths.shape[1])),
            ),
        ],
        axis=0,
    )
    first_slots = gather_layers(first_pack, layers).reshape(layers, half + EXTRA, wide)
    out_unit, query_unit = swap(
        [output_weight, query_up],
        [columns_of(head_columns)] * 2,
        [quad_of] * 2,
        [(QUAD, part, head_columns), (QUAD, rank_part, head_columns)],
        QUAD_FLIPS,
        1,
        "swap_heads",
    )
    head_all = gather_layers(
        jnp.concatenate(
            [query_unit.reshape(rank_span, head_columns), out_unit.reshape(span, head_columns)]
        ),
        layers,
    ).reshape(layers, rank_span + span, head_columns)
    query_slice = head_all[:, :rank_span].reshape(rank, head_columns)
    out_slice = head_all[:, rank_span:].reshape(model, head_columns)
    packs = [
        jnp.concatenate(
            [
                w.reshape(part, QUAD, units)[:, :, low:high]
                for w in (gate_weight, up_weight, down_weight)
            ],
            axis=2,
        ).transpose(1, 0, 2)
        for low, high in chunks
    ]
    feed_units = swap(
        packs, [quad_of] * 2, [quad_of] * 2, [p.shape for p in packs], QUAD_FLIPS, 2, "swap_feed"
    )

    small_width = -(-(2 * part + rank_part + lengths.shape[1]) // 128) * 128
    first_weight, small = gather_layer(
        [first_slots[:, :half], first_slots[:, half : half + 16, :small_width]],
        3,
        "gather_first",
        [inside, stacked],
    )
    feed_weights = [
        gather_layers(feed_units[0].reshape(span, -1), layers),
        gather_layers(after(feed_units[1], first_weight).reshape(span, -1), layers),
    ]
    first_weight = first_weight.reshape(model, wide)
    small = small[:, :, 0].transpose(1, 0, 2)
    first_gain = small[:, ::PAIR, :part].reshape(model).astype(F32)
    second_gain = small[:, ::PAIR, part : part + rank_part].reshape(rank).astype(F32)
    third_gain = (
        small[:, ::PAIR, part + rank_part : 2 * part + rank_part].reshape(model).astype(F32)
    )
    begin = 2 * part + rank_part
    all_lengths = small[:, :, begin : begin + lengths.shape[1]].astype(jnp.int32)
    all_lengths = lax.dynamic_index_in_dim(all_lengths, layer, 0, keepdims=False)

    inputs = tokens.astype(F32)
    upstream = cotangent.astype(F32)
    position, valid, allowed_own = layout(lengths[0], count_rows)
    cosine, sine = angles_of(position, HEAD_DIM)
    normed = norm_rows(inputs, first_gain).astype(BF)
    first = matmul("rd,de->re", normed, first_weight)
    latent = first[:, :rank]
    keyvals = first[:, rank:]
    latent_normed = norm_rows(latent, second_gain).astype(BF)
    key_rot = rotate(keyvals[:, :HEAD_DIM], cosine, sine).astype(BF)
    value_rows = keyvals[:, HEAD_DIM:].astype(BF)
    latent_all, key_all, value_all = gather_layer(
        [latent_normed, key_rot, value_rows], 4, "gather_latent"
    )
    latent_all = latent_all.reshape(all_rows, rank)

    positions, valids, allowed = jax.vmap(lambda one: layout(one, count_rows))(all_lengths)
    cosines, sines = angles_of(positions, HEAD_DIM)
    queries = matmul("rc,cf->rf", latent_all, query_slice).reshape(
        GROUP, count_rows, heads, HEAD_DIM
    )
    query_rot = rotate(queries, cosines[:, :, None, :], sines[:, :, None, :]).astype(BF)

    def masked_scores():
        raw = matmul("gqhd,gkd->ghqk", query_rot, key_all) * scale
        return jnp.where(allowed[:, None], raw, NEGATIVE)

    scores = masked_scores()
    highest = jnp.max(scores, axis=-1, keepdims=True)
    raised = jnp.exp(scores - highest)
    totals = jnp.sum(raised, axis=-1, keepdims=True)
    probs = (raised / totals).astype(BF)
    logsum = highest + jnp.log(totals)
    mixed = matmul("ghqk,gkd->gqhd", probs, value_all).reshape(all_rows, head_columns).astype(BF)
    branch_terms = matmul("rf,df->rd", mixed, out_slice).astype(BF)
    branch = reduce_layer(branch_terms.reshape(GROUP, count_rows, model), 5, "reduce_branch")
    middle = inputs + branch
    normed_ffn = norm_rows(middle, third_gain).astype(BF)
    kept = jnp.where(valid[:, None], upstream, 0.0)
    feed_rows, grad_rows = gather_layer([normed_ffn, kept.astype(BF)], 6, "gather_feed")
    feed_rows = feed_rows.reshape(all_rows, model)
    grad_rows = grad_rows.reshape(all_rows, model)

    hiddens = []
    ffn_terms = jnp.zeros((all_rows, model), F32)
    grad_packs = []
    normed_rows = []
    for weights, (low, high) in zip(feed_weights, chunks):
        width = high - low
        gate_up, down = weights[:, : 2 * width], weights[:, 2 * width :]
        both = matmul("rd,df->rf", feed_rows, gate_up)
        gate, up = both[:, :width], both[:, width:]
        hidden_grad = matmul("rd,df->rf", grad_rows, down)
        sigma = jax.nn.sigmoid(gate)
        activated = gate * sigma
        slope = sigma * (1.0 + gate * (1.0 - sigma))
        hidden = (activated * up).astype(BF)
        both_grad = jnp.concatenate(
            [hidden_grad * up * slope, hidden_grad * activated], axis=1
        ).astype(BF)
        grad_both = matmul("rd,rf->df", feed_rows, both_grad).astype(BF)
        grad_down = matmul("rd,rf->df", grad_rows, hidden).astype(BF)
        grad_pack = jnp.concatenate([grad_both, grad_down], axis=1)
        grad_packs.append(grad_pack)
        if not normed_rows:
            normed_rows = gather_layer([after(normed, grad_pack)], 15, "gather_normed")
        feed_rows = after(feed_rows, grad_pack, normed_rows[0])
        both_grad = after(both_grad, grad_pack)
        ffn_terms = ffn_terms + matmul("rf,df->rd", both_grad, gate_up)
        hiddens.append((hidden, down))
    ffn_grad = reduce_layer(
        ffn_terms.astype(BF).reshape(GROUP, count_rows, model), 7, "reduce_ffn_grad"
    )
    unused_third, third_pull = jax.vjp(norm_rows, middle, third_gain)
    middle_norm_grad, feed_gain_grad = third_pull(ffn_grad)
    middle_grad = kept + middle_norm_grad
    [branch_rows] = gather_layer([middle_grad.astype(BF)], 8, "gather_branch")
    feed_sums = [reduce_layers(grad_packs[0], layers)]
    branch_rows = branch_rows.reshape(all_rows, model)

    mixed_grad = (
        matmul("rd,df->rf", branch_rows, out_slice)
        .astype(BF)
        .reshape(GROUP, count_rows, heads, HEAD_DIM)
    )
    probs_back = jnp.exp(masked_scores() - logsum)
    prob_grad = matmul("gqhd,gkd->ghqk", mixed_grad, value_all)
    score_grad = (
        probs_back * (prob_grad - jnp.sum(probs_back * prob_grad, axis=-1, keepdims=True))
    ).astype(BF)
    value_terms = matmul("ghqk,gqhd->gkd", probs, mixed_grad)
    query_rot_grad = matmul("ghqk,gkd->gqhd", score_grad, key_all) * scale
    key_terms = matmul("ghqk,gqhd->gkd", score_grad, query_rot) * scale
    query_grad = (
        rotate(query_rot_grad, cosines[:, :, None, :], -sines[:, :, None, :])
        .reshape(all_rows, head_columns)
        .astype(BF)
    )
    latent_terms = matmul("rf,cf->rc", query_grad, query_slice)
    back_terms = jnp.concatenate(
        [latent_terms.reshape(GROUP, count_rows, rank), key_terms, value_terms], axis=2
    ).astype(BF)
    second_pack = after(grad_packs[1], feed_sums[0], score_grad)
    feed_sums.append(reduce_layers(second_pack, layers))
    back = reduce_layer(after(back_terms, second_pack), 9, "reduce_latent")
    grad_query = matmul("rc,rf->cf", latent_all, after(query_grad, back)).astype(BF)
    grad_out = matmul("rd,rf->df", after(branch_rows, back), mixed).astype(BF)
    head_pack = jnp.concatenate(
        [
            grad_query.reshape(layers, rank_span, head_columns),
            grad_out.reshape(layers, span, head_columns),
        ],
        axis=1,
    ).reshape(rank + model, head_columns)

    latent_normed_grad = back[:, :rank]
    keyval_grad = jnp.concatenate(
        [rotate(back[:, rank : rank + HEAD_DIM], cosine, -sine), back[:, rank + HEAD_DIM :]], axis=1
    ).astype(BF)
    unused_second, second_pull = jax.vjp(norm_rows, latent, second_gain)
    latent_back, latent_gain_grad = second_pull(latent_normed_grad)
    first_grad = jnp.concatenate([latent_back.astype(BF), keyval_grad], axis=1)
    normed_grad = matmul("re,de->rd", first_grad, first_weight)
    unused_first, first_pull = jax.vjp(norm_rows, inputs, first_gain)
    input_norm_grad, norm_gain_grad = first_pull(normed_grad)
    grad_tokens = (
        middle_grad + input_norm_grad + jnp.where(valid[:, None], 0.0, upstream)
    ).astype(BF)
    first_grad = after(first_grad, head_pack)
    gains = jnp.concatenate([norm_gain_grad, feed_gain_grad, latent_gain_grad])
    gains = jnp.pad(gains.reshape(-1, rank), ((0, 32 - gains.size // rank), (0, 0)))
    grad_all, gains_all = gather_layer([first_grad, gains.astype(BF)], 10, "gather_last")
    feed_terms = sum(
        matmul("rf,df->rd", after(hidden, grad_all), down) for hidden, down in hiddens
    ).astype(BF)
    feed = reduce_layer(
        feed_terms.reshape(GROUP, count_rows, model), 11, "reduce_feed"
    )
    output = jnp.where(valid[:, None], middle + feed, inputs).astype(BF)

    head_pack = after(head_pack, grad_all)
    head_sum = reduce_layers(after(head_pack, *feed_sums), layers)
    normed_rows = normed_rows[0].reshape(all_rows, model)
    gain_sums = jnp.sum(gains_all.astype(F32), axis=0)
    lines = model // rank
    columns = wide // QUAD
    grad_slice = lax.dynamic_slice_in_dim(
        grad_all.reshape(all_rows, wide), quad * columns, columns, axis=1
    )
    grad_first = matmul("rd,re->de", normed_rows, grad_slice).astype(BF)
    grad_first = lax.dynamic_index_in_dim(
        grad_first.reshape(layers * QUAD, PAIR, half, columns), hid, 1, keepdims=False
    )
    small_sums = jnp.concatenate(
        [
            gain_sums[:lines].reshape(layers, span),
            gain_sums[lines : 2 * lines].reshape(layers, span),
            gain_sums[2 * lines].reshape(layers, rank_span),
        ],
        axis=1,
    )
    flat = 16 * columns
    small_sums = jnp.pad(small_sums, ((0, 0), (0, flat - small_sums.shape[1])))
    quads = [[z * QUAD + q for q in range(QUAD)] for z in range(layers)]
    feed_own = lax.all_to_all(
        after(jnp.concatenate(feed_sums, axis=1), grad_all).reshape(QUAD, part, -1),
        "batch",
        0,
        0,
        axis_index_groups=quads,
        tiled=True,
    )
    last_pack = jnp.concatenate(
        [
            grad_first.reshape(layers, QUAD * half, columns),
            small_sums.reshape(layers, 16, columns).astype(BF),
        ],
        axis=1,
    ).reshape(layers * (QUAD * half + 16), columns)
    grads = join(feed_own, [high - low for low, high in chunks])
    last_pack = after(after(last_pack, feed), head_sum)
    last_sum = reduce_layers(last_pack, layers)
    small_sum = last_sum[QUAD * half :].astype(F32).reshape(-1)

    query_sum, out_sum = head_sum[:rank_span], head_sum[rank_span:]
    groups = [[z * GROUP + i for i in range(GROUP)] for z in range(layers)]
    head_own = lax.all_to_all(
        jnp.repeat(
            jnp.concatenate(
                [
                    query_sum.reshape(QUAD, rank_part, head_columns),
                    out_sum.reshape(QUAD, part, head_columns),
                ],
                axis=1,
            ),
            PAIR,
            axis=0,
        ),
        ("batch", "hid"),
        0,
        0,
        axis_index_groups=groups,
        tiled=True,
    )
    down_own, pair_own = settle(
        [last_sum],
        [rows_of(0, half)],
        [
            lambda ref, i: ref.at[
                pl.ds(pl.multiple_of(lax.rem(i, PAIR) * half, half), half),
                pl.ds(pl.multiple_of(i // PAIR * columns, columns), columns),
            ],
        ],
        [(part, wide)],
        [(0, 0, rank), (0, rank, wide)],
        14,
        "settle_last",
    )
    query_own, out_own = spread(after(head_own, down_own), rank_part)
    return (
        output,
        grad_tokens,
        lax.dynamic_slice_in_dim(small_sum, quad * part, part),
        down_own,
        lax.dynamic_slice_in_dim(small_sum, 2 * span + quad * rank_part, rank_part),
        query_own,
        pair_own,
        out_own,
        lax.dynamic_slice_in_dim(small_sum, span + quad * part, part),
        *grads,
    )


def solution(mesh):
    placed = (
        P(("batch", "hid"), None),
        P(("batch", "hid"), None),
        P("batch"),
        P("batch", None),
        P("batch"),
        P("batch", None),
        P("batch", None),
        P("batch", None),
        P("batch"),
        P("batch", "hid"),
        P("batch", "hid"),
        P("batch", "hid"),
        P(("batch", "hid"), None),
    )
    return jax.shard_map(
        functools.partial(per_device, mesh.shape["batch"] // QUAD),
        mesh=mesh,
        in_specs=placed,
        out_specs=(
            P(("batch", "hid"), None),
            P(("batch", "hid"), None),
            P("batch"),
            P("batch", None),
            P("batch"),
            P("batch", None),
            P("batch", None),
            P("batch", None),
            P("batch"),
            P("batch", "hid"),
            P("batch", "hid"),
            P("batch", "hid"),
        ),
        check_vma=False,
    )
```

```python
import functools

import jax
import jax.numpy as jnp
from jax import lax
from jax.experimental import pallas as pl
from jax.experimental.pallas import tpu as pltpu
from jax.sharding import PartitionSpec as P

HEADS = 16
HEAD_DIM = 256


EPS = 1e-05
ROPE_BASE = 10000.0
NEGATIVE = -1e30

QUAD = 4
PAIR = 2
GROUP = QUAD * PAIR
EXTRA = 24
MESH = pl.DeviceIdType.MESH
BF = jnp.bfloat16
F32 = jnp.float32


def matmul(spec, left, right):
    return jnp.einsum(spec, left, right, preferred_element_type=F32)


def norm_rows(values, gain):
    return values * lax.rsqrt(jnp.mean(values * values, axis=-1, keepdims=True) + EPS) * gain


def rotate(values, cosine, sine):
    half = values.shape[-1] // 2
    first = values[..., :half]
    second = values[..., half:]
    return jnp.concatenate(
        [first * cosine - second * sine, second * cosine + first * sine], axis=-1
    )


def layout(row_lengths, count_rows):
    slots = jnp.arange(row_lengths.shape[0], dtype=jnp.int32)
    ends = jnp.sum(jnp.where(slots[None, :] <= slots[:, None], row_lengths[None, :], 0), axis=1)
    starts = ends - row_lengths
    places = jnp.arange(count_rows, dtype=jnp.int32)
    segment = jnp.sum((places[:, None] >= ends[None, :]).astype(jnp.int32), axis=1)
    begins = jnp.concatenate([starts, ends[-1:]])
    labels = jnp.arange(begins.shape[0], dtype=jnp.int32)
    firsts = jnp.sum(jnp.where(segment[:, None] == labels[None, :], begins[None, :], 0), axis=1)
    position = places - firsts
    valid = places < ends[-1]
    allowed = (segment[:, None] == segment[None, :]) & (places[None, :] <= places[:, None])
    return (position, valid, allowed)


def angles_of(position, head_size):
    half = head_size // 2
    freqs = ROPE_BASE ** (-(jnp.arange(half, dtype=F32) * 2.0) / head_size)
    angle = position.astype(F32)[..., None] * freqs
    return (jnp.cos(angle), jnp.sin(angle))


def place():
    batch = lax.axis_index("batch")
    quad = lax.rem(batch, QUAD)
    return batch - quad, quad, lax.axis_index("hid")


def flip(quad, bits):
    core = lax.rem(quad, 2)
    chip = quad - core
    if bits & 1:
        core = 1 - core
    if bits & 2:
        chip = 2 - chip
    return chip + core


def after(value, *others):
    return lax.optimization_barrier((value, *others))[0]


def meet(peers):
    barrier = pltpu.get_barrier_semaphore()
    for peer in peers:
        pl.semaphore_signal(barrier, inc=1, device_id=peer, device_id_type=MESH)
    pl.semaphore_wait(barrier, len(peers))


def ways_of(base, quad, hid):
    def spot(bits, turn):
        return (flip(quad, bits), 1 - hid if turn else hid)

    def address(f):
        q, h = spot(*f)
        return (base + q, h)

    def index(f):
        q, h = spot(*f)
        return q * PAIR + h

    return address, index


ACROSS, ALONG, CORNER, MATE, SELF = (2, 0), (0, 1), (2, 1), (1, 0), (0, 0)


def gather_kernel(count, cuts, puts, *refs):
    ins, outs = refs[:count], refs[count : 2 * count]
    local_sem, send_sem, recv_sem = refs[2 * count :]
    base, quad, hid = place()
    address, index = ways_of(base, quad, hid)
    meet([address(f) for f in (ACROSS, ALONG, MATE)])

    def part(ref, i, h):
        cut, size = cuts[i]
        return ref.at[pl.ds(0, cut)] if h == 0 else ref.at[pl.ds(cut, size - cut)]

    def spot(i, f):
        return puts[i](outs[i], index(f))

    def copy(i, j, source, target, f):
        return pltpu.make_async_remote_copy(
            src_ref=source,
            dst_ref=target,
            send_sem=send_sem.at[i, j],
            recv_sem=recv_sem.at[i, j],
            device_id=address(f),
            device_id_type=MESH,
        )

    started = []

    def start(one):
        one.start()
        started.append(one)

    for i in range(count):
        for j, f, h in ((0, ACROSS, 0), (3, ALONG, 1), (1, ACROSS, 1), (2, ALONG, 0)):
            start(copy(i, j, part(ins[i], i, h), part(spot(i, SELF), i, h), f))
        start(copy(i, 6, ins[i], spot(i, SELF), MATE))
        pltpu.make_async_copy(ins[i], spot(i, SELF), local_sem.at[i]).start()

    def arrived(i, j, where, f):
        copy(i, j, where, where, f).wait_recv()

    for i in range(count):
        where = part(spot(i, ACROSS), i, 0)
        arrived(i, 0, where, ACROSS)
        start(copy(i, 4, where, where, ALONG))
        where = part(spot(i, ALONG), i, 1)
        arrived(i, 3, where, ALONG)
        start(copy(i, 5, where, where, ACROSS))
        arrived(i, 1, part(spot(i, ACROSS), i, 1), ACROSS)
        where = spot(i, ACROSS)
        start(copy(i, 7, where, where, MATE))
        arrived(i, 2, part(spot(i, ALONG), i, 0), ALONG)
        where = spot(i, ALONG)
        start(copy(i, 8, where, where, MATE))
    for i in range(count):
        where = part(spot(i, CORNER), i, 0)
        arrived(i, 4, where, ALONG)
        start(copy(i, 9, where, where, MATE))
        where = part(spot(i, CORNER), i, 1)
        arrived(i, 5, where, ACROSS)
        start(copy(i, 10, where, where, MATE))
    for i in range(count):
        pltpu.make_async_copy(ins[i], spot(i, SELF), local_sem.at[i]).wait()
        arrived(i, 6, spot(i, MATE), MATE)
        arrived(i, 7, spot(i, (ACROSS[0] ^ 1, ACROSS[1])), MATE)
        arrived(i, 8, spot(i, (ALONG[0] ^ 1, ALONG[1])), MATE)
        corner = spot(i, (CORNER[0] ^ 1, CORNER[1]))
        arrived(i, 9, part(corner, i, 0), MATE)
        arrived(i, 10, part(corner, i, 1), MATE)
    for one in started:
        one.wait_send()


def stacked(ref, place):
    return ref.at[place]


def inside(ref, place):
    return ref.at[:, place]


def gather_layer(arrays, ident, name, puts=None):
    count = len(arrays)
    puts = puts or [stacked] * count
    shapes = [
        (GROUP,) + a.shape if p is stacked else (a.shape[0], GROUP) + a.shape[1:]
        for a, p in zip(arrays, puts)
    ]
    cuts = [
        (a.shape[0] // 2 if a.ndim > 2 else a.shape[0] // 32 * 16, a.shape[0]) for a in arrays
    ]
    moved = sum(a.size * 2 * GROUP for a in arrays)
    return pl.pallas_call(
        functools.partial(gather_kernel, count, cuts, puts),
        out_shape=[jax.ShapeDtypeStruct(s, a.dtype) for s, a in zip(shapes, arrays)],
        in_specs=[pl.BlockSpec(memory_space=pl.ANY)] * count,
        out_specs=[pl.BlockSpec(memory_space=pl.ANY)] * count,
        scratch_shapes=[
            pltpu.SemaphoreType.DMA((count,)),
            pltpu.SemaphoreType.DMA((count, 11)),
            pltpu.SemaphoreType.DMA((count, 11)),
        ],
        compiler_params=pltpu.CompilerParams(collective_id=ident, has_side_effects=True),
        cost_estimate=pl.CostEstimate(flops=0, bytes_accessed=16 * moved, transcendentals=0),
        name=name,
    )(*arrays)


def reduce_kernel(in_ref, out_ref, own, mate_in, sums, relay, far_in, local_sem, send_sem, recv_sem):
    base, quad, hid = place()
    address, index = ways_of(base, quad, hid)
    rows = out_ref.shape[0]
    half = rows // 2
    step = 16
    ways = [CORNER, ACROSS, ALONG, SELF]
    meet([address(f) for f in (ACROSS, ALONG, MATE)])
    started = []

    def copy(j, source, target, f):
        return pltpu.make_async_remote_copy(
            src_ref=source,
            dst_ref=target,
            send_sem=send_sem.at[j],
            recv_sem=recv_sem.at[j],
            device_id=address(f),
            device_id_type=MESH,
        )

    def start(one):
        one.start()
        started.append(one)
        return one

    to_mate, local = [], []
    for j, f in enumerate(ways):
        to_mate.append(start(copy(j, in_ref.at[index((f[0] ^ 1, f[1]))], mate_in.at[j], MATE)))
        local.append(pltpu.make_async_copy(in_ref.at[index(f)], own.at[j], local_sem.at[j]))
        local[-1].start()

    def ready(j):
        local[j].wait()
        to_mate[j].wait_recv()

    def add(j, first, count, more=None):
        def body(r, carry):
            at = pl.ds(pl.multiple_of(first + r * step, step), step)
            value = own[j, at, :].astype(F32) + mate_in[j, at, :].astype(F32)
            if more is not None:
                value += more[pl.ds(pl.multiple_of(r * step, step), step), :].astype(F32)
            sums[j, at, :] = value.astype(BF)
            return carry

        lax.fori_loop(0, count // step, body, 0)

    low, high = pl.ds(0, half), pl.ds(half, half)
    ready(0)
    add(0, 0, half)
    by_across = start(copy(4, sums.at[0, low], relay.at[0], ACROSS))
    add(0, half, half)
    by_along = start(copy(5, sums.at[0, high], relay.at[1], ALONG))
    ready(1)
    add(1, 0, half)
    across_low = start(copy(6, sums.at[1, low], far_in.at[0, low], ACROSS))
    ready(2)
    add(2, half, half)
    along_high = start(copy(7, sums.at[2, high], far_in.at[1, high], ALONG))
    by_across.wait_recv()
    add(2, 0, half, relay.at[0])
    along_low = start(copy(8, sums.at[2, low], far_in.at[1, low], ALONG))
    by_along.wait_recv()
    add(1, half, half, relay.at[1])
    across_high = start(copy(9, sums.at[1, high], far_in.at[0, high], ACROSS))
    ready(3)
    for one in (across_low, along_high, along_low, across_high):
        one.wait_recv()

    def total(r, carry):
        at = pl.ds(pl.multiple_of(r * step, step), step)
        out_ref[at, :] = (
            own[3, at, :].astype(F32)
            + mate_in[3, at, :].astype(F32)
            + far_in[0, at, :].astype(F32)
            + far_in[1, at, :].astype(F32)
        )
        return carry

    lax.fori_loop(0, rows // step, total, 0)
    for one in started:
        one.wait_send()


def reduce_layer(blocks, ident, name):
    rows, columns = blocks.shape[1:]
    return pl.pallas_call(
        reduce_kernel,
        out_shape=jax.ShapeDtypeStruct((rows, columns), F32),
        in_specs=[pl.BlockSpec(memory_space=pl.ANY)],
        out_specs=pl.BlockSpec(memory_space=pltpu.VMEM),
        scratch_shapes=[
            pltpu.VMEM((4, rows, columns), BF),
            pltpu.VMEM((4, rows, columns), BF),
            pltpu.VMEM((3, rows, columns), BF),
            pltpu.VMEM((2, rows // 2, columns), BF),
            pltpu.VMEM((2, rows, columns), BF),
            pltpu.SemaphoreType.DMA((4,)),
            pltpu.SemaphoreType.DMA((10,)),
            pltpu.SemaphoreType.DMA((10,)),
        ],
        compiler_params=pltpu.CompilerParams(
            collective_id=ident, has_side_effects=True, vmem_limit_bytes=40 * 2**20
        ),
        cost_estimate=pl.CostEstimate(
            flops=0, bytes_accessed=16 * blocks.size * 2, transcendentals=0
        ),
        name=name,
    )(blocks)


def swap_kernel(count, takes, puts, flips, *refs):
    ins, outs = refs[:count], refs[count : 2 * count]
    local_sem, send_sem, recv_sem = refs[2 * count :]
    base, quad, hid = place()
    address, index = ways_of(base, quad, hid)
    meet([address(f) for f in flips])

    def copy(i, j, f, owner):
        return pltpu.make_async_remote_copy(
            src_ref=takes[i](ins[i], index(f)),
            dst_ref=puts[i](outs[i], owner),
            send_sem=send_sem.at[i, j],
            recv_sem=recv_sem.at[i, j],
            device_id=address(f),
            device_id_type=MESH,
        )

    me = index(SELF)
    for i in range(count):
        for j, f in enumerate(flips):
            copy(i, j, f, me).start()
        pltpu.make_async_copy(takes[i](ins[i], me), puts[i](outs[i], me), local_sem.at[i]).start()
    for i in range(count):
        pltpu.make_async_copy(takes[i](ins[i], me), puts[i](outs[i], me), local_sem.at[i]).wait()
        for j, f in enumerate(flips):
            copy(i, j, f, index(f)).wait_recv()
    for i in range(count):
        for j, f in enumerate(flips):
            copy(i, j, f, me).wait_send()


QUAD_FLIPS = ((3, 0), (2, 0), (1, 0))
ALL_FLIPS = ((3, 1), (2, 1), (3, 0), (2, 0), (1, 1), (0, 1), (1, 0))


def swap(arrays, takes, puts, shapes, flips, ident, name):
    count = len(arrays)
    moved = sum(a.size * 2 for a in arrays)
    return pl.pallas_call(
        functools.partial(swap_kernel, count, takes, puts, flips),
        out_shape=[jax.ShapeDtypeStruct(s, a.dtype) for s, a in zip(shapes, arrays)],
        in_specs=[pl.BlockSpec(memory_space=pl.ANY)] * count,
        out_specs=[pl.BlockSpec(memory_space=pl.ANY)] * count,
        scratch_shapes=[
            pltpu.SemaphoreType.DMA((count,)),
            pltpu.SemaphoreType.DMA((count, len(flips))),
            pltpu.SemaphoreType.DMA((count, len(flips))),
        ],
        compiler_params=pltpu.CompilerParams(collective_id=ident, has_side_effects=True),
        cost_estimate=pl.CostEstimate(flops=0, bytes_accessed=32 * moved, transcendentals=0),
        name=name,
    )(*arrays)


def spread_kernel(blocks_ref, first_ref, second_ref):
    count = first_ref.shape[0]
    columns = blocks_ref.shape[2]
    for i in range(blocks_ref.shape[0]):
        at = pl.ds(i * columns, columns)
        first_ref[:, at] = blocks_ref[i, :count, :].astype(F32)
        second_ref[:, at] = blocks_ref[i, count:, :].astype(F32)


def spread(blocks, count):
    n, rows, columns = blocks.shape
    return pl.pallas_call(
        spread_kernel,
        grid=(n // 2,),
        in_specs=[pl.BlockSpec((2, rows, columns), lambda i: (i, 0, 0))],
        out_specs=[
            pl.BlockSpec((count, 2 * columns), lambda i: (0, i)),
            pl.BlockSpec((rows - count, 2 * columns), lambda i: (0, i)),
        ],
        out_shape=[
            jax.ShapeDtypeStruct((count, n * columns), F32),
            jax.ShapeDtypeStruct((rows - count, n * columns), F32),
        ],
        cost_estimate=pl.CostEstimate(
            flops=0, bytes_accessed=6 * blocks.size, transcendentals=0
        ),
        name="spread_heads",
    )(blocks)


def settle_kernel(count, takes, puts, results, *refs):
    ins, outs = refs[:count], refs[count : count + len(results)]
    landed = refs[count + len(results) : 2 * count + len(results)]
    local_sem, send_sem, recv_sem = refs[2 * count + len(results) :]
    base, quad, hid = place()
    address, index = ways_of(base, quad, hid)
    meet([address(f) for f in ALL_FLIPS])

    def copy(i, j, f, owner):
        return pltpu.make_async_remote_copy(
            src_ref=takes[i](ins[i], index(f) // PAIR),
            dst_ref=puts[i](landed[i], owner),
            send_sem=send_sem.at[i, j],
            recv_sem=recv_sem.at[i, j],
            device_id=address(f),
            device_id_type=MESH,
        )

    def local(i):
        return pltpu.make_async_copy(
            takes[i](ins[i], quad), puts[i](landed[i], index(SELF)), local_sem.at[i]
        )

    for i in range(count):
        for j, f in enumerate(ALL_FLIPS):
            copy(i, j, f, index(SELF)).start()
        local(i).start()
    for i in range(count):
        local(i).wait()
        for j, f in enumerate(ALL_FLIPS):
            copy(i, j, f, index(f)).wait_recv()
    step = 16
    for (i, begin, end), out in zip(results, outs):

        def body(r, carry, i=i, begin=begin, end=end, out=out):
            at = pl.ds(pl.multiple_of(r * step, step), step)
            out[at, :] = landed[i][at, begin:end].astype(F32)
            return carry

        lax.fori_loop(0, out.shape[0] // step, body, 0)
    for i in range(count):
        for j, f in enumerate(ALL_FLIPS):
            copy(i, j, f, index(SELF)).wait_send()


def settle(arrays, takes, puts, shapes, results, ident, name):
    count = len(arrays)
    moved = sum(s[0] * s[1] for s in shapes)
    return pl.pallas_call(
        functools.partial(settle_kernel, count, takes, puts, results),
        out_shape=[jax.ShapeDtypeStruct((shapes[i][0], e - b), F32) for i, b, e in results],
        in_specs=[pl.BlockSpec(memory_space=pl.ANY)] * count,
        out_specs=[pl.BlockSpec(memory_space=pltpu.VMEM)] * len(results),
        scratch_shapes=[pltpu.VMEM(s, BF) for s in shapes]
        + [
            pltpu.SemaphoreType.DMA((count,)),
            pltpu.SemaphoreType.DMA((count, len(ALL_FLIPS))),
            pltpu.SemaphoreType.DMA((count, len(ALL_FLIPS))),
        ],
        compiler_params=pltpu.CompilerParams(
            collective_id=ident, has_side_effects=True, vmem_limit_bytes=24 * 2**20
        ),
        cost_estimate=pl.CostEstimate(flops=0, bytes_accessed=64 * moved, transcendentals=0),
        name=name,
    )(*arrays)


def rows_of(begin, count):
    return lambda ref, q: ref.at[pl.ds(pl.multiple_of(begin + q * count, 16), count)]


def join_kernel(widths, blocks_ref, *outs):
    total = sum(widths)
    for i, out in enumerate(outs):
        for q in range(QUAD):
            begin, source = q * total, 0
            for width in widths:
                at = source + i * width
                out[:, begin : begin + width] = blocks_ref[q, :, at : at + width].astype(F32)
                begin += width
                source += 3 * width


def join(blocks, widths):
    rows, columns = blocks.shape[1], QUAD * sum(widths)
    strip = min(rows, 32)
    return pl.pallas_call(
        functools.partial(join_kernel, widths),
        grid=(rows // strip,),
        in_specs=[pl.BlockSpec((QUAD, strip, blocks.shape[2]), lambda i: (0, i, 0))],
        out_specs=[pl.BlockSpec((strip, columns), lambda i: (i, 0))] * 3,
        out_shape=[jax.ShapeDtypeStruct((rows, columns), F32)] * 3,
        cost_estimate=pl.CostEstimate(
            flops=0, bytes_accessed=18 * rows * columns, transcendentals=0
        ),
        name="join_feed",
    )(blocks)


def columns_of(width):
    return lambda ref, i: ref.at[:, pl.ds(pl.multiple_of(i * width, width), width)]


def quad_of(ref, i):
    return ref.at[i // PAIR]


def layer_groups(layers):
    return [[z * QUAD + q for z in range(layers)] for q in range(QUAD)]


def gather_layers(unit, layers):
    return lax.all_gather(
        unit, "batch", axis=0, tiled=True, axis_index_groups=layer_groups(layers)
    )


def reduce_layers(blocks, layers):
    return lax.psum_scatter(
        blocks,
        "batch",
        scatter_dimension=0,
        tiled=True,
        axis_index_groups=layer_groups(layers),
    )


def per_device(
    layers,
    tokens,
    lengths,
    attention_gain,
    query_down,
    query_gain,
    query_up,
    key_value,
    output_weight,
    feed_gain,
    gate_weight,
    up_weight,
    down_weight,
    cotangent,
):
    count_rows, model = tokens.shape
    part, rank = query_down.shape
    rank_part = query_up.shape[0]
    half = part // PAIR
    wide = rank + key_value.shape[1]
    all_rows = GROUP * count_rows
    heads = HEADS // GROUP
    head_columns = heads * HEAD_DIM
    units = gate_weight.shape[1] // QUAD
    cut = -(-units // 256) * 128
    chunks = [(0, cut), (cut, units)]
    scale = HEAD_DIM ** (-0.5)
    base, quad, hid = place()
    layer = base // QUAD
    me = quad * PAIR + hid
    span = QUAD * part
    rank_span = QUAD * rank_part

    first_pack = jnp.concatenate(
        [
            lax.dynamic_slice_in_dim(
                jnp.concatenate([query_down, key_value], axis=1), hid * half, half, axis=0
            ),
            jnp.pad(
                jnp.concatenate([attention_gain, query_gain, feed_gain, lengths[0].astype(BF)])[None],
                ((0, EXTRA - 1), (0, wide - 2 * part - rank_part - lengths.shape[1])),
            ),
        ],
        axis=0,
    )
    first_slots = gather_layers(first_pack, layers).reshape(layers, half + EXTRA, wide)
    packs = [
        jnp.concatenate(
            [
                w.reshape(part, QUAD, units)[:, :, low:high]
                for w in (gate_weight, up_weight, down_weight)
            ],
            axis=2,
        ).transpose(1, 0, 2)
        for low, high in chunks
    ]
    out_unit, query_unit, feed_unit = swap(
        [output_weight, query_up, packs[0]],
        [columns_of(head_columns)] * 2 + [quad_of],
        [quad_of] * 3,
        [(QUAD, part, head_columns), (QUAD, rank_part, head_columns), packs[0].shape],
        QUAD_FLIPS,
        1,
        "swap_heads",
    )
    folds = part // rank_part
    thin = head_columns // folds
    head_all = gather_layers(
        jnp.concatenate(
            [
                out_unit,
                feed_unit,
                query_unit.reshape(QUAD, rank_part, folds, thin)
                .transpose(0, 2, 1, 3)
                .reshape(QUAD, part, thin),
            ],
            axis=2,
        ).reshape(span, -1),
        layers,
    )
    out_slice = head_all[:, :head_columns]
    feed_weights = [head_all[:, head_columns : head_columns + packs[0].shape[2]]]
    query_slice = (
        head_all[:, head_columns + packs[0].shape[2] :]
        .reshape(layers * QUAD, folds, rank_part, thin)
        .transpose(0, 2, 1, 3)
        .reshape(rank, head_columns)
    )
    [feed_unit] = swap(
        [after(packs[1], out_unit)],
        [quad_of],
        [quad_of],
        [packs[1].shape],
        QUAD_FLIPS,
        2,
        "swap_feed",
    )

    small_width = -(-(2 * part + rank_part + lengths.shape[1]) // 128) * 128
    first_weight, small = gather_layer(
        [first_slots[:, :half], first_slots[:, half : half + 16, :small_width]],
        3,
        "gather_first",
        [inside, stacked],
    )
    feed_weights.append(gather_layers(after(feed_unit, first_weight).reshape(span, -1), layers))
    first_weight = first_weight.reshape(model, wide)
    small = small[:, :, 0].transpose(1, 0, 2)
    first_gain = small[:, ::PAIR, :part].reshape(model).astype(F32)
    second_gain = small[:, ::PAIR, part : part + rank_part].reshape(rank).astype(F32)
    third_gain = (
        small[:, ::PAIR, part + rank_part : 2 * part + rank_part].reshape(model).astype(F32)
    )
    begin = 2 * part + rank_part
    all_lengths = small[:, :, begin : begin + lengths.shape[1]].astype(jnp.int32)
    all_lengths = lax.dynamic_index_in_dim(all_lengths, layer, 0, keepdims=False)

    inputs = tokens.astype(F32)
    upstream = cotangent.astype(F32)
    position, valid, allowed_own = layout(lengths[0], count_rows)
    cosine, sine = angles_of(position, HEAD_DIM)
    normed = norm_rows(inputs, first_gain).astype(BF)
    first = matmul("rd,de->re", normed, first_weight)
    latent = first[:, :rank]
    keyvals = first[:, rank:]
    latent_normed = norm_rows(latent, second_gain).astype(BF)
    key_rot = rotate(keyvals[:, :HEAD_DIM], cosine, sine).astype(BF)
    value_rows = keyvals[:, HEAD_DIM:].astype(BF)
    latent_all, key_all, value_all = gather_layer(
        [latent_normed, key_rot, value_rows], 4, "gather_latent"
    )
    kept = jnp.where(valid[:, None], upstream, 0.0)
    grad_rows, normed_rows = gather_layer(
        [after(kept.astype(BF), latent_all), normed], 15, "gather_upstream"
    )
    grad_rows = grad_rows.reshape(all_rows, model)
    query_slice = after(query_slice, grad_rows)
    latent_all = latent_all.reshape(all_rows, rank)

    positions, valids, allowed = jax.vmap(lambda one: layout(one, count_rows))(all_lengths)
    cosines, sines = angles_of(positions, HEAD_DIM)
    queries = matmul("rc,cf->rf", latent_all, query_slice).reshape(
        GROUP, count_rows, heads, HEAD_DIM
    )
    query_rot = rotate(queries, cosines[:, :, None, :], sines[:, :, None, :]).astype(BF)

    def masked_scores():
        raw = matmul("gqhd,gkd->ghqk", query_rot, key_all) * scale
        return jnp.where(allowed[:, None], raw, NEGATIVE)

    scores = masked_scores()
    highest = jnp.max(scores, axis=-1, keepdims=True)
    raised = jnp.exp(scores - highest)
    totals = jnp.sum(raised, axis=-1, keepdims=True)
    probs = (raised / totals).astype(BF)
    logsum = highest + jnp.log(totals)
    mixed = matmul("ghqk,gkd->gqhd", probs, value_all).reshape(all_rows, head_columns).astype(BF)
    branch_terms = matmul("rf,df->rd", mixed, out_slice).astype(BF)
    branch = reduce_layer(branch_terms.reshape(GROUP, count_rows, model), 5, "reduce_branch")
    middle = inputs + branch
    normed_ffn = norm_rows(middle, third_gain).astype(BF)
    [feed_rows] = gather_layer([normed_ffn], 6, "gather_feed")
    feed_rows = feed_rows.reshape(all_rows, model)

    hiddens = []
    ffn_terms = jnp.zeros((all_rows, model), F32)
    grad_packs = []
    for weights, (low, high) in zip(feed_weights, chunks):
        width = high - low
        gate_up, down = weights[:, : 2 * width], weights[:, 2 * width :]
        both = matmul("rd,df->rf", feed_rows, gate_up)
        gate, up = both[:, :width], both[:, width:]
        hidden_grad = matmul("rd,df->rf", grad_rows, down)
        sigma = jax.nn.sigmoid(gate)
        activated = gate * sigma
        slope = sigma * (1.0 + gate * (1.0 - sigma))
        hidden = (activated * up).astype(BF)
        both_grad = jnp.concatenate(
            [hidden_grad * up * slope, hidden_grad * activated], axis=1
        ).astype(BF)
        grad_both = matmul("rd,rf->df", feed_rows, both_grad).astype(BF)
        grad_down = matmul("rd,rf->df", grad_rows, hidden).astype(BF)
        grad_pack = jnp.concatenate([grad_both, grad_down], axis=1)
        grad_packs.append(grad_pack)
        feed_rows = after(feed_rows, grad_pack)
        both_grad = after(both_grad, grad_pack)
        ffn_terms = ffn_terms + matmul("rf,df->rd", both_grad, gate_up)
        hiddens.append((hidden, down))
    ffn_grad = reduce_layer(
        ffn_terms.astype(BF).reshape(GROUP, count_rows, model), 7, "reduce_ffn_grad"
    )
    unused_third, third_pull = jax.vjp(norm_rows, middle, third_gain)
    middle_norm_grad, feed_gain_grad = third_pull(ffn_grad)
    middle_grad = kept + middle_norm_grad
    [branch_rows] = gather_layer([middle_grad.astype(BF)], 8, "gather_branch")
    feed_sums = [reduce_layers(grad_packs[0], layers)]
    branch_rows = branch_rows.reshape(all_rows, model)

    mixed_grad = (
        matmul("rd,df->rf", branch_rows, out_slice)
        .astype(BF)
        .reshape(GROUP, count_rows, heads, HEAD_DIM)
    )
    probs_back = jnp.exp(masked_scores() - logsum)
    prob_grad = matmul("gqhd,gkd->ghqk", mixed_grad, value_all)
    score_grad = (
        probs_back * (prob_grad - jnp.sum(probs_back * prob_grad, axis=-1, keepdims=True))
    ).astype(BF)
    value_terms = matmul("ghqk,gqhd->gkd", probs, mixed_grad)
    query_rot_grad = matmul("ghqk,gkd->gqhd", score_grad, key_all) * scale
    key_terms = matmul("ghqk,gqhd->gkd", score_grad, query_rot) * scale
    query_grad = (
        rotate(query_rot_grad, cosines[:, :, None, :], -sines[:, :, None, :])
        .reshape(all_rows, head_columns)
        .astype(BF)
    )
    latent_terms = matmul("rf,cf->rc", query_grad, query_slice)
    back_terms = jnp.concatenate(
        [latent_terms.reshape(GROUP, count_rows, rank), key_terms, value_terms], axis=2
    ).astype(BF)
    second_pack = after(grad_packs[1], feed_sums[0], score_grad)
    feed_sums.append(reduce_layers(second_pack, layers))
    back = reduce_layer(after(back_terms, second_pack), 9, "reduce_latent")
    grad_query = matmul("rc,rf->cf", latent_all, after(query_grad, back)).astype(BF)
    grad_out = matmul("rd,rf->df", after(branch_rows, back), mixed).astype(BF)
    head_pack = jnp.concatenate(
        [
            grad_query.reshape(layers, rank_span, head_columns),
            grad_out.reshape(layers, span, head_columns),
        ],
        axis=1,
    ).reshape(rank + model, head_columns)

    latent_normed_grad = back[:, :rank]
    keyval_grad = jnp.concatenate(
        [rotate(back[:, rank : rank + HEAD_DIM], cosine, -sine), back[:, rank + HEAD_DIM :]], axis=1
    ).astype(BF)
    unused_second, second_pull = jax.vjp(norm_rows, latent, second_gain)
    latent_back, latent_gain_grad = second_pull(latent_normed_grad)
    first_grad = jnp.concatenate([latent_back.astype(BF), keyval_grad], axis=1)
    normed_grad = matmul("re,de->rd", first_grad, first_weight)
    unused_first, first_pull = jax.vjp(norm_rows, inputs, first_gain)
    input_norm_grad, norm_gain_grad = first_pull(normed_grad)
    grad_tokens = (
        middle_grad + input_norm_grad + jnp.where(valid[:, None], 0.0, upstream)
    ).astype(BF)
    first_grad = after(first_grad, head_pack)
    gains = jnp.concatenate([norm_gain_grad, feed_gain_grad, latent_gain_grad])
    gains = jnp.pad(gains.reshape(-1, rank), ((0, 32 - gains.size // rank), (0, 0)))
    grad_all, gains_all = gather_layer([first_grad, gains.astype(BF)], 10, "gather_last")
    feed_terms = sum(
        matmul("rf,df->rd", after(hidden, grad_all), down) for hidden, down in hiddens
    ).astype(BF)
    feed = reduce_layer(
        feed_terms.reshape(GROUP, count_rows, model), 11, "reduce_feed"
    )
    output = jnp.where(valid[:, None], middle + feed, inputs).astype(BF)

    head_pack = after(head_pack, grad_all)
    head_sum = reduce_layers(after(head_pack, *feed_sums), layers)
    normed_rows = normed_rows.reshape(all_rows, model)
    gain_sums = jnp.sum(gains_all.astype(F32), axis=0)
    lines = model // rank
    columns = wide // QUAD
    grad_slice = lax.dynamic_slice_in_dim(
        grad_all.reshape(all_rows, wide), quad * columns, columns, axis=1
    )
    grad_first = matmul("rd,re->de", normed_rows, grad_slice).astype(BF)
    grad_first = lax.dynamic_index_in_dim(
        grad_first.reshape(layers * QUAD, PAIR, half, columns), hid, 1, keepdims=False
    )
    small_sums = jnp.concatenate(
        [
            gain_sums[:lines].reshape(layers, span),
            gain_sums[lines : 2 * lines].reshape(layers, span),
            gain_sums[2 * lines].reshape(layers, rank_span),
        ],
        axis=1,
    )
    flat = 16 * columns
    small_sums = jnp.pad(small_sums, ((0, 0), (0, flat - small_sums.shape[1])))
    quads = [[z * QUAD + q for q in range(QUAD)] for z in range(layers)]
    feed_own = lax.all_to_all(
        after(jnp.concatenate(feed_sums, axis=1), grad_all).reshape(QUAD, part, -1),
        "batch",
        0,
        0,
        axis_index_groups=quads,
        tiled=True,
    )
    last_pack = jnp.concatenate(
        [
            grad_first.reshape(layers, QUAD * half, columns),
            small_sums.reshape(layers, 16, columns).astype(BF),
        ],
        axis=1,
    ).reshape(layers * (QUAD * half + 16), columns)
    grads = join(feed_own, [high - low for low, high in chunks])
    last_pack = after(after(last_pack, feed), head_sum)
    last_sum = reduce_layers(last_pack, layers)
    small_sum = last_sum[QUAD * half :].astype(F32).reshape(-1)

    query_sum, out_sum = head_sum[:rank_span], head_sum[rank_span:]
    groups = [[z * GROUP + i for i in range(GROUP)] for z in range(layers)]
    head_own = lax.all_to_all(
        jnp.repeat(
            jnp.concatenate(
                [
                    query_sum.reshape(QUAD, rank_part, head_columns),
                    out_sum.reshape(QUAD, part, head_columns),
                ],
                axis=1,
            ),
            PAIR,
            axis=0,
        ),
        ("batch", "hid"),
        0,
        0,
        axis_index_groups=groups,
        tiled=True,
    )
    down_own, pair_own = settle(
        [last_sum],
        [rows_of(0, half)],
        [
            lambda ref, i: ref.at[
                pl.ds(pl.multiple_of(lax.rem(i, PAIR) * half, half), half),
                pl.ds(pl.multiple_of(i // PAIR * columns, columns), columns),
            ],
        ],
        [(part, wide)],
        [(0, 0, rank), (0, rank, wide)],
        14,
        "settle_last",
    )
    query_own, out_own = spread(after(head_own, down_own), rank_part)
    return (
        output,
        grad_tokens,
        lax.dynamic_slice_in_dim(small_sum, quad * part, part),
        down_own,
        lax.dynamic_slice_in_dim(small_sum, 2 * span + quad * rank_part, rank_part),
        query_own,
        pair_own,
        out_own,
        lax.dynamic_slice_in_dim(small_sum, span + quad * part, part),
        *grads,
    )


def solution(mesh):
    placed = (
        P(("batch", "hid"), None),
        P(("batch", "hid"), None),
        P("batch"),
        P("batch", None),
        P("batch"),
        P("batch", None),
        P("batch", None),
        P("batch", None),
        P("batch"),
        P("batch", "hid"),
        P("batch", "hid"),
        P("batch", "hid"),
        P(("batch", "hid"), None),
    )
    return jax.shard_map(
        functools.partial(per_device, mesh.shape["batch"] // QUAD),
        mesh=mesh,
        in_specs=placed,
        out_specs=(
            P(("batch", "hid"), None),
            P(("batch", "hid"), None),
            P("batch"),
            P("batch", None),
            P("batch"),
            P("batch", None),
            P("batch", None),
            P("batch", None),
            P("batch"),
            P("batch", "hid"),
            P("batch", "hid"),
            P("batch", "hid"),
        ),
        check_vma=False,
    )
```

```python
import functools

import jax
import jax.numpy as jnp
from jax import lax
from jax.experimental import pallas as pl
from jax.experimental.pallas import tpu as pltpu
from jax.sharding import PartitionSpec as P

HEADS = 16
HEAD_DIM = 256


EPS = 1e-05
ROPE_BASE = 10000.0
NEGATIVE = -1e30

QUAD = 4
PAIR = 2
GROUP = QUAD * PAIR
EXTRA = 24
MESH = pl.DeviceIdType.MESH
BF = jnp.bfloat16
F32 = jnp.float32


def matmul(spec, left, right):
    return jnp.einsum(spec, left, right, preferred_element_type=F32)


def norm_rows(values, gain):
    return values * lax.rsqrt(jnp.mean(values * values, axis=-1, keepdims=True) + EPS) * gain


def rotate(values, cosine, sine):
    half = values.shape[-1] // 2
    first = values[..., :half]
    second = values[..., half:]
    return jnp.concatenate(
        [first * cosine - second * sine, second * cosine + first * sine], axis=-1
    )


def layout(row_lengths, count_rows):
    slots = jnp.arange(row_lengths.shape[0], dtype=jnp.int32)
    ends = jnp.sum(jnp.where(slots[None, :] <= slots[:, None], row_lengths[None, :], 0), axis=1)
    starts = ends - row_lengths
    places = jnp.arange(count_rows, dtype=jnp.int32)
    segment = jnp.sum((places[:, None] >= ends[None, :]).astype(jnp.int32), axis=1)
    begins = jnp.concatenate([starts, ends[-1:]])
    labels = jnp.arange(begins.shape[0], dtype=jnp.int32)
    firsts = jnp.sum(jnp.where(segment[:, None] == labels[None, :], begins[None, :], 0), axis=1)
    position = places - firsts
    valid = places < ends[-1]
    allowed = (segment[:, None] == segment[None, :]) & (places[None, :] <= places[:, None])
    return (position, valid, allowed)


def angles_of(position, head_size):
    half = head_size // 2
    freqs = ROPE_BASE ** (-(jnp.arange(half, dtype=F32) * 2.0) / head_size)
    angle = position.astype(F32)[..., None] * freqs
    return (jnp.cos(angle), jnp.sin(angle))


def place():
    batch = lax.axis_index("batch")
    quad = lax.rem(batch, QUAD)
    return batch - quad, quad, lax.axis_index("hid")


def flip(quad, bits):
    core = lax.rem(quad, 2)
    chip = quad - core
    if bits & 1:
        core = 1 - core
    if bits & 2:
        chip = 2 - chip
    return chip + core


def after(value, *others):
    return lax.optimization_barrier((value, *others))[0]


def meet(peers):
    barrier = pltpu.get_barrier_semaphore()
    for peer in peers:
        pl.semaphore_signal(barrier, inc=1, device_id=peer, device_id_type=MESH)
    pl.semaphore_wait(barrier, len(peers))


def ways_of(base, quad, hid):
    def spot(bits, turn):
        return (flip(quad, bits), 1 - hid if turn else hid)

    def address(f):
        q, h = spot(*f)
        return (base + q, h)

    def index(f):
        q, h = spot(*f)
        return q * PAIR + h

    return address, index


ACROSS, ALONG, CORNER, MATE, SELF = (2, 0), (0, 1), (2, 1), (1, 0), (0, 0)


def gather_kernel(count, cuts, puts, *refs):
    ins, outs = refs[:count], refs[count : 2 * count]
    local_sem, send_sem, recv_sem = refs[2 * count :]
    base, quad, hid = place()
    address, index = ways_of(base, quad, hid)
    meet([address(f) for f in (ACROSS, ALONG, MATE)])

    def part(ref, i, h):
        cut, size = cuts[i]
        return ref.at[pl.ds(0, cut)] if h == 0 else ref.at[pl.ds(cut, size - cut)]

    def spot(i, f):
        return puts[i](outs[i], index(f))

    def copy(i, j, source, target, f):
        return pltpu.make_async_remote_copy(
            src_ref=source,
            dst_ref=target,
            send_sem=send_sem.at[i, j],
            recv_sem=recv_sem.at[i, j],
            device_id=address(f),
            device_id_type=MESH,
        )

    started = []

    def start(one):
        one.start()
        started.append(one)

    for i in range(count):
        for j, f, h in ((0, ACROSS, 0), (3, ALONG, 1), (1, ACROSS, 1), (2, ALONG, 0)):
            start(copy(i, j, part(ins[i], i, h), part(spot(i, SELF), i, h), f))
        start(copy(i, 6, ins[i], spot(i, SELF), MATE))
        pltpu.make_async_copy(ins[i], spot(i, SELF), local_sem.at[i]).start()

    def arrived(i, j, where, f):
        copy(i, j, where, where, f).wait_recv()

    for i in range(count):
        where = part(spot(i, ACROSS), i, 0)
        arrived(i, 0, where, ACROSS)
        start(copy(i, 4, where, where, ALONG))
        where = part(spot(i, ALONG), i, 1)
        arrived(i, 3, where, ALONG)
        start(copy(i, 5, where, where, ACROSS))
        arrived(i, 1, part(spot(i, ACROSS), i, 1), ACROSS)
        where = spot(i, ACROSS)
        start(copy(i, 7, where, where, MATE))
        arrived(i, 2, part(spot(i, ALONG), i, 0), ALONG)
        where = spot(i, ALONG)
        start(copy(i, 8, where, where, MATE))
    for i in range(count):
        where = part(spot(i, CORNER), i, 0)
        arrived(i, 4, where, ALONG)
        start(copy(i, 9, where, where, MATE))
        where = part(spot(i, CORNER), i, 1)
        arrived(i, 5, where, ACROSS)
        start(copy(i, 10, where, where, MATE))
    for i in range(count):
        pltpu.make_async_copy(ins[i], spot(i, SELF), local_sem.at[i]).wait()
        arrived(i, 6, spot(i, MATE), MATE)
        arrived(i, 7, spot(i, (ACROSS[0] ^ 1, ACROSS[1])), MATE)
        arrived(i, 8, spot(i, (ALONG[0] ^ 1, ALONG[1])), MATE)
        corner = spot(i, (CORNER[0] ^ 1, CORNER[1]))
        arrived(i, 9, part(corner, i, 0), MATE)
        arrived(i, 10, part(corner, i, 1), MATE)
    for one in started:
        one.wait_send()


def stacked(ref, place):
    return ref.at[place]


def inside(ref, place):
    return ref.at[:, place]


def gather_layer(arrays, ident, name, puts=None):
    count = len(arrays)
    puts = puts or [stacked] * count
    shapes = [
        (GROUP,) + a.shape if p is stacked else (a.shape[0], GROUP) + a.shape[1:]
        for a, p in zip(arrays, puts)
    ]
    cuts = [
        (a.shape[0] // 2 if a.ndim > 2 else a.shape[0] // 32 * 16, a.shape[0]) for a in arrays
    ]
    moved = sum(a.size * 2 * GROUP for a in arrays)
    return pl.pallas_call(
        functools.partial(gather_kernel, count, cuts, puts),
        out_shape=[jax.ShapeDtypeStruct(s, a.dtype) for s, a in zip(shapes, arrays)],
        in_specs=[pl.BlockSpec(memory_space=pl.ANY)] * count,
        out_specs=[pl.BlockSpec(memory_space=pl.ANY)] * count,
        scratch_shapes=[
            pltpu.SemaphoreType.DMA((count,)),
            pltpu.SemaphoreType.DMA((count, 11)),
            pltpu.SemaphoreType.DMA((count, 11)),
        ],
        compiler_params=pltpu.CompilerParams(collective_id=ident, has_side_effects=True),
        cost_estimate=pl.CostEstimate(flops=0, bytes_accessed=16 * moved, transcendentals=0),
        name=name,
    )(*arrays)


def reduce_kernel(in_ref, out_ref, own, mate_in, sums, relay, far_in, local_sem, send_sem, recv_sem):
    base, quad, hid = place()
    address, index = ways_of(base, quad, hid)
    rows = out_ref.shape[0]
    half = rows // 2
    step = 16
    ways = [CORNER, ACROSS, ALONG, SELF]
    meet([address(f) for f in (ACROSS, ALONG, MATE)])
    started = []

    def copy(j, source, target, f):
        return pltpu.make_async_remote_copy(
            src_ref=source,
            dst_ref=target,
            send_sem=send_sem.at[j],
            recv_sem=recv_sem.at[j],
            device_id=address(f),
            device_id_type=MESH,
        )

    def start(one):
        one.start()
        started.append(one)
        return one

    to_mate, local = [], []
    for j, f in enumerate(ways):
        to_mate.append(start(copy(j, in_ref.at[index((f[0] ^ 1, f[1]))], mate_in.at[j], MATE)))
        local.append(pltpu.make_async_copy(in_ref.at[index(f)], own.at[j], local_sem.at[j]))
        local[-1].start()

    def ready(j):
        local[j].wait()
        to_mate[j].wait_recv()

    def add(j, first, count, more=None):
        def body(r, carry):
            at = pl.ds(pl.multiple_of(first + r * step, step), step)
            value = own[j, at, :].astype(F32) + mate_in[j, at, :].astype(F32)
            if more is not None:
                value += more[pl.ds(pl.multiple_of(r * step, step), step), :].astype(F32)
            sums[j, at, :] = value.astype(BF)
            return carry

        lax.fori_loop(0, count // step, body, 0)

    low, high = pl.ds(0, half), pl.ds(half, half)
    ready(0)
    add(0, 0, half)
    by_across = start(copy(4, sums.at[0, low], relay.at[0], ACROSS))
    add(0, half, half)
    by_along = start(copy(5, sums.at[0, high], relay.at[1], ALONG))
    ready(1)
    add(1, 0, half)
    across_low = start(copy(6, sums.at[1, low], far_in.at[0, low], ACROSS))
    ready(2)
    add(2, half, half)
    along_high = start(copy(7, sums.at[2, high], far_in.at[1, high], ALONG))
    by_across.wait_recv()
    add(2, 0, half, relay.at[0])
    along_low = start(copy(8, sums.at[2, low], far_in.at[1, low], ALONG))
    by_along.wait_recv()
    add(1, half, half, relay.at[1])
    across_high = start(copy(9, sums.at[1, high], far_in.at[0, high], ACROSS))
    ready(3)
    for one in (across_low, along_high, along_low, across_high):
        one.wait_recv()

    def total(r, carry):
        at = pl.ds(pl.multiple_of(r * step, step), step)
        out_ref[at, :] = (
            own[3, at, :].astype(F32)
            + mate_in[3, at, :].astype(F32)
            + far_in[0, at, :].astype(F32)
            + far_in[1, at, :].astype(F32)
        )
        return carry

    lax.fori_loop(0, rows // step, total, 0)
    for one in started:
        one.wait_send()


def reduce_layer(blocks, ident, name):
    rows, columns = blocks.shape[1:]
    return pl.pallas_call(
        reduce_kernel,
        out_shape=jax.ShapeDtypeStruct((rows, columns), F32),
        in_specs=[pl.BlockSpec(memory_space=pl.ANY)],
        out_specs=pl.BlockSpec(memory_space=pltpu.VMEM),
        scratch_shapes=[
            pltpu.VMEM((4, rows, columns), BF),
            pltpu.VMEM((4, rows, columns), BF),
            pltpu.VMEM((3, rows, columns), BF),
            pltpu.VMEM((2, rows // 2, columns), BF),
            pltpu.VMEM((2, rows, columns), BF),
            pltpu.SemaphoreType.DMA((4,)),
            pltpu.SemaphoreType.DMA((10,)),
            pltpu.SemaphoreType.DMA((10,)),
        ],
        compiler_params=pltpu.CompilerParams(
            collective_id=ident, has_side_effects=True, vmem_limit_bytes=40 * 2**20
        ),
        cost_estimate=pl.CostEstimate(
            flops=0, bytes_accessed=16 * blocks.size * 2, transcendentals=0
        ),
        name=name,
    )(blocks)


def swap_kernel(count, homes, takes, puts, flips, *refs):
    outs = refs[count:-3]
    ins, outs = refs[:count], [outs[home] for home in homes]
    local_sem, send_sem, recv_sem = refs[-3:]
    base, quad, hid = place()
    address, index = ways_of(base, quad, hid)
    meet([address(f) for f in flips])

    def copy(i, j, f, owner):
        return pltpu.make_async_remote_copy(
            src_ref=takes[i](ins[i], index(f)),
            dst_ref=puts[i](outs[i], owner),
            send_sem=send_sem.at[i, j],
            recv_sem=recv_sem.at[i, j],
            device_id=address(f),
            device_id_type=MESH,
        )

    me = index(SELF)
    for i in range(count):
        for j, f in enumerate(flips):
            copy(i, j, f, me).start()
        pltpu.make_async_copy(takes[i](ins[i], me), puts[i](outs[i], me), local_sem.at[i]).start()
    for i in range(count):
        pltpu.make_async_copy(takes[i](ins[i], me), puts[i](outs[i], me), local_sem.at[i]).wait()
        for j, f in enumerate(flips):
            copy(i, j, f, index(f)).wait_recv()
    for i in range(count):
        for j, f in enumerate(flips):
            copy(i, j, f, me).wait_send()


QUAD_FLIPS = ((3, 0), (2, 0), (1, 0))
ALL_FLIPS = ((3, 1), (2, 1), (3, 0), (2, 0), (1, 1), (0, 1), (1, 0))


def swap(arrays, takes, puts, shapes, flips, ident, name, homes=None):
    count = len(arrays)
    homes = homes or range(count)
    moved = sum(a.size * 2 for a in arrays)
    return pl.pallas_call(
        functools.partial(swap_kernel, count, homes, takes, puts, flips),
        out_shape=[jax.ShapeDtypeStruct(s, BF) for s in shapes],
        in_specs=[pl.BlockSpec(memory_space=pl.ANY)] * count,
        out_specs=[pl.BlockSpec(memory_space=pl.ANY)] * len(shapes),
        scratch_shapes=[
            pltpu.SemaphoreType.DMA((count,)),
            pltpu.SemaphoreType.DMA((count, len(flips))),
            pltpu.SemaphoreType.DMA((count, len(flips))),
        ],
        compiler_params=pltpu.CompilerParams(collective_id=ident, has_side_effects=True),
        cost_estimate=pl.CostEstimate(flops=0, bytes_accessed=32 * moved, transcendentals=0),
        name=name,
    )(*arrays)


def spread_kernel(blocks_ref, first_ref, second_ref):
    count = first_ref.shape[0]
    columns = blocks_ref.shape[2]
    for i in range(blocks_ref.shape[0]):
        at = pl.ds(i * columns, columns)
        first_ref[:, at] = blocks_ref[i, :count, :].astype(F32)
        second_ref[:, at] = blocks_ref[i, count:, :].astype(F32)


def spread(blocks, count):
    n, rows, columns = blocks.shape
    return pl.pallas_call(
        spread_kernel,
        grid=(n // 2,),
        in_specs=[pl.BlockSpec((2, rows, columns), lambda i: (i, 0, 0))],
        out_specs=[
            pl.BlockSpec((count, 2 * columns), lambda i: (0, i)),
            pl.BlockSpec((rows - count, 2 * columns), lambda i: (0, i)),
        ],
        out_shape=[
            jax.ShapeDtypeStruct((count, n * columns), F32),
            jax.ShapeDtypeStruct((rows - count, n * columns), F32),
        ],
        cost_estimate=pl.CostEstimate(
            flops=0, bytes_accessed=6 * blocks.size, transcendentals=0
        ),
        name="spread_heads",
    )(blocks)


def settle_kernel(count, takes, puts, results, *refs):
    ins, outs = refs[:count], refs[count : count + len(results)]
    landed = refs[count + len(results) : 2 * count + len(results)]
    local_sem, send_sem, recv_sem = refs[2 * count + len(results) :]
    base, quad, hid = place()
    address, index = ways_of(base, quad, hid)
    meet([address(f) for f in ALL_FLIPS])

    def copy(i, j, f, owner):
        return pltpu.make_async_remote_copy(
            src_ref=takes[i](ins[i], index(f) // PAIR),
            dst_ref=puts[i](landed[i], owner),
            send_sem=send_sem.at[i, j],
            recv_sem=recv_sem.at[i, j],
            device_id=address(f),
            device_id_type=MESH,
        )

    def local(i):
        return pltpu.make_async_copy(
            takes[i](ins[i], quad), puts[i](landed[i], index(SELF)), local_sem.at[i]
        )

    for i in range(count):
        for j, f in enumerate(ALL_FLIPS):
            copy(i, j, f, index(SELF)).start()
        local(i).start()
    for i in range(count):
        local(i).wait()
        for j, f in enumerate(ALL_FLIPS):
            copy(i, j, f, index(f)).wait_recv()
    step = 16
    for (i, begin, end), out in zip(results, outs):

        def body(r, carry, i=i, begin=begin, end=end, out=out):
            at = pl.ds(pl.multiple_of(r * step, step), step)
            out[at, :] = landed[i][at, begin:end].astype(F32)
            return carry

        lax.fori_loop(0, out.shape[0] // step, body, 0)
    for i in range(count):
        for j, f in enumerate(ALL_FLIPS):
            copy(i, j, f, index(SELF)).wait_send()


def settle(arrays, takes, puts, shapes, results, ident, name):
    count = len(arrays)
    moved = sum(s[0] * s[1] for s in shapes)
    return pl.pallas_call(
        functools.partial(settle_kernel, count, takes, puts, results),
        out_shape=[jax.ShapeDtypeStruct((shapes[i][0], e - b), F32) for i, b, e in results],
        in_specs=[pl.BlockSpec(memory_space=pl.ANY)] * count,
        out_specs=[pl.BlockSpec(memory_space=pltpu.VMEM)] * len(results),
        scratch_shapes=[pltpu.VMEM(s, BF) for s in shapes]
        + [
            pltpu.SemaphoreType.DMA((count,)),
            pltpu.SemaphoreType.DMA((count, len(ALL_FLIPS))),
            pltpu.SemaphoreType.DMA((count, len(ALL_FLIPS))),
        ],
        compiler_params=pltpu.CompilerParams(
            collective_id=ident, has_side_effects=True, vmem_limit_bytes=24 * 2**20
        ),
        cost_estimate=pl.CostEstimate(flops=0, bytes_accessed=64 * moved, transcendentals=0),
        name=name,
    )(*arrays)


def rows_of(begin, count):
    return lambda ref, q: ref.at[pl.ds(pl.multiple_of(begin + q * count, 16), count)]


def join_kernel(widths, blocks_ref, *outs):
    total = sum(widths)
    for i, out in enumerate(outs):
        for q in range(QUAD):
            begin, source = q * total, 0
            for width in widths:
                at = source + i * width
                out[:, begin : begin + width] = blocks_ref[q, :, at : at + width].astype(F32)
                begin += width
                source += 3 * width


def join(blocks, widths):
    rows, columns = blocks.shape[1], QUAD * sum(widths)
    strip = min(rows, 32)
    return pl.pallas_call(
        functools.partial(join_kernel, widths),
        grid=(rows // strip,),
        in_specs=[pl.BlockSpec((QUAD, strip, blocks.shape[2]), lambda i: (0, i, 0))],
        out_specs=[pl.BlockSpec((strip, columns), lambda i: (i, 0))] * 3,
        out_shape=[jax.ShapeDtypeStruct((rows, columns), F32)] * 3,
        cost_estimate=pl.CostEstimate(
            flops=0, bytes_accessed=18 * rows * columns, transcendentals=0
        ),
        name="join_feed",
    )(blocks)


def columns_of(width):
    return lambda ref, i: ref.at[:, pl.ds(pl.multiple_of(i * width, width), width)]


def quad_of(ref, i):
    return ref.at[i // PAIR]


def layer_groups(layers):
    return [[z * QUAD + q for z in range(layers)] for q in range(QUAD)]


def gather_layers(unit, layers):
    return lax.all_gather(
        unit, "batch", axis=0, tiled=True, axis_index_groups=layer_groups(layers)
    )


def reduce_layers(blocks, layers):
    return lax.psum_scatter(
        blocks,
        "batch",
        scatter_dimension=0,
        tiled=True,
        axis_index_groups=layer_groups(layers),
    )


def per_device(
    layers,
    tokens,
    lengths,
    attention_gain,
    query_down,
    query_gain,
    query_up,
    key_value,
    output_weight,
    feed_gain,
    gate_weight,
    up_weight,
    down_weight,
    cotangent,
):
    count_rows, model = tokens.shape
    part, rank = query_down.shape
    rank_part = query_up.shape[0]
    half = part // PAIR
    wide = rank + key_value.shape[1]
    all_rows = GROUP * count_rows
    heads = HEADS // GROUP
    head_columns = heads * HEAD_DIM
    units = gate_weight.shape[1] // QUAD
    cut = -(-units // 256) * 128
    chunks = [(0, cut), (cut, units)]
    scale = HEAD_DIM ** (-0.5)
    base, quad, hid = place()
    layer = base // QUAD
    me = quad * PAIR + hid
    span = QUAD * part
    rank_span = QUAD * rank_part

    first_pack = jnp.concatenate(
        [
            lax.dynamic_slice_in_dim(
                jnp.concatenate([query_down, key_value], axis=1), hid * half, half, axis=0
            ),
            jnp.pad(
                jnp.concatenate([attention_gain, query_gain, feed_gain, lengths[0].astype(BF)])[None],
                ((0, EXTRA - 1), (0, wide - 2 * part - rank_part - lengths.shape[1])),
            ),
        ],
        axis=0,
    )
    first_slots = gather_layers(first_pack, layers).reshape(layers, half + EXTRA, wide)
    packs = [
        jnp.concatenate(
            [
                w.reshape(part, QUAD, units)[:, :, low:high]
                for w in (gate_weight, up_weight, down_weight)
            ],
            axis=2,
        ).transpose(1, 0, 2)
        for low, high in chunks
    ]
    folds = part // rank_part
    thin = head_columns // folds
    feed_end = head_columns + packs[0].shape[2]

    def fold_of(fold):
        def take(ref, i):
            begin = pl.multiple_of(i * head_columns, head_columns) + fold * thin
            return ref.at[:, pl.ds(begin, thin)]

        def put(ref, i):
            rows = pl.ds(fold * rank_part, rank_part)
            return ref.at[i // PAIR, rows, pl.ds(feed_end, thin)]

        return take, put

    fold_ways = [fold_of(fold) for fold in range(folds)]
    [head_unit] = swap(
        [output_weight, packs[0]] + [query_up] * folds,
        [columns_of(head_columns), quad_of] + [take for take, put in fold_ways],
        [
            lambda ref, i: ref.at[i // PAIR, :, pl.ds(0, head_columns)],
            lambda ref, i: ref.at[i // PAIR, :, pl.ds(head_columns, feed_end - head_columns)],
        ]
        + [put for take, put in fold_ways],
        [(QUAD, part, feed_end + thin)],
        QUAD_FLIPS,
        1,
        "swap_heads",
        [0] * (2 + folds),
    )
    head_all = gather_layers(head_unit.reshape(span, -1), layers)
    out_slice = head_all[:, :head_columns]
    feed_weights = [head_all[:, head_columns:feed_end]]
    query_slice = (
        head_all[:, feed_end:]
        .reshape(layers * QUAD, folds, rank_part, thin)
        .transpose(0, 2, 1, 3)
        .reshape(rank, head_columns)
    )
    [feed_unit] = swap(
        [after(packs[1], head_unit)],
        [quad_of],
        [quad_of],
        [packs[1].shape],
        QUAD_FLIPS,
        2,
        "swap_feed",
    )

    small_width = -(-(2 * part + rank_part + lengths.shape[1]) // 128) * 128
    first_weight, small = gather_layer(
        [first_slots[:, :half], first_slots[:, half : half + 16, :small_width]],
        3,
        "gather_first",
        [inside, stacked],
    )
    feed_weights.append(gather_layers(after(feed_unit, first_weight).reshape(span, -1), layers))
    first_weight = first_weight.reshape(model, wide)
    small = small[:, :, 0].transpose(1, 0, 2)
    first_gain = small[:, ::PAIR, :part].reshape(model).astype(F32)
    second_gain = small[:, ::PAIR, part : part + rank_part].reshape(rank).astype(F32)
    third_gain = (
        small[:, ::PAIR, part + rank_part : 2 * part + rank_part].reshape(model).astype(F32)
    )
    begin = 2 * part + rank_part
    all_lengths = small[:, :, begin : begin + lengths.shape[1]].astype(jnp.int32)
    all_lengths = lax.dynamic_index_in_dim(all_lengths, layer, 0, keepdims=False)

    inputs = tokens.astype(F32)
    upstream = cotangent.astype(F32)
    position, valid, allowed_own = layout(lengths[0], count_rows)
    cosine, sine = angles_of(position, HEAD_DIM)
    normed = norm_rows(inputs, first_gain).astype(BF)
    first = matmul("rd,de->re", normed, first_weight)
    latent = first[:, :rank]
    keyvals = first[:, rank:]
    latent_normed = norm_rows(latent, second_gain).astype(BF)
    key_rot = rotate(keyvals[:, :HEAD_DIM], cosine, sine).astype(BF)
    value_rows = keyvals[:, HEAD_DIM:].astype(BF)
    latent_all, key_all, value_all = gather_layer(
        [latent_normed, key_rot, value_rows], 4, "gather_latent"
    )
    kept = jnp.where(valid[:, None], upstream, 0.0)
    grad_rows, normed_rows = gather_layer(
        [after(kept.astype(BF), latent_all), normed], 15, "gather_upstream"
    )
    grad_rows = grad_rows.reshape(all_rows, model)
    query_slice = after(query_slice, grad_rows)
    latent_all = latent_all.reshape(all_rows, rank)

    positions, valids, allowed = jax.vmap(lambda one: layout(one, count_rows))(all_lengths)
    cosines, sines = angles_of(positions, HEAD_DIM)
    queries = matmul("rc,cf->rf", latent_all, query_slice).reshape(
        GROUP, count_rows, heads, HEAD_DIM
    )
    query_rot = rotate(queries, cosines[:, :, None, :], sines[:, :, None, :]).astype(BF)

    def masked_scores():
        raw = matmul("gqhd,gkd->ghqk", query_rot, key_all) * scale
        return jnp.where(allowed[:, None], raw, NEGATIVE)

    scores = masked_scores()
    highest = jnp.max(scores, axis=-1, keepdims=True)
    raised = jnp.exp(scores - highest)
    totals = jnp.sum(raised, axis=-1, keepdims=True)
    probs = (raised / totals).astype(BF)
    logsum = highest + jnp.log(totals)
    mixed = matmul("ghqk,gkd->gqhd", probs, value_all).reshape(all_rows, head_columns).astype(BF)
    branch_terms = matmul("rf,df->rd", mixed, out_slice).astype(BF)
    branch = reduce_layer(branch_terms.reshape(GROUP, count_rows, model), 5, "reduce_branch")
    middle = inputs + branch
    normed_ffn = norm_rows(middle, third_gain).astype(BF)
    [feed_rows] = gather_layer([normed_ffn], 6, "gather_feed")
    feed_rows = feed_rows.reshape(all_rows, model)

    hiddens = []
    ffn_terms = jnp.zeros((all_rows, model), F32)
    grad_packs = []
    for weights, (low, high) in zip(feed_weights, chunks):
        width = high - low
        gate_up, down = weights[:, : 2 * width], weights[:, 2 * width :]
        both = matmul("rd,df->rf", feed_rows, gate_up)
        gate, up = both[:, :width], both[:, width:]
        hidden_grad = matmul("rd,df->rf", grad_rows, down)
        sigma = jax.nn.sigmoid(gate)
        activated = gate * sigma
        slope = sigma * (1.0 + gate * (1.0 - sigma))
        hidden = (activated * up).astype(BF)
        both_grad = jnp.concatenate(
            [hidden_grad * up * slope, hidden_grad * activated], axis=1
        ).astype(BF)
        grad_both = matmul("rd,rf->df", feed_rows, both_grad).astype(BF)
        grad_down = matmul("rd,rf->df", grad_rows, hidden).astype(BF)
        grad_pack = jnp.concatenate([grad_both, grad_down], axis=1)
        grad_packs.append(grad_pack)
        feed_rows = after(feed_rows, grad_pack)
        both_grad = after(both_grad, grad_pack)
        ffn_terms = ffn_terms + matmul("rf,df->rd", both_grad, gate_up)
        hiddens.append((hidden, down))
    ffn_grad = reduce_layer(
        ffn_terms.astype(BF).reshape(GROUP, count_rows, model), 7, "reduce_ffn_grad"
    )
    unused_third, third_pull = jax.vjp(norm_rows, middle, third_gain)
    middle_norm_grad, feed_gain_grad = third_pull(ffn_grad)
    middle_grad = kept + middle_norm_grad
    [branch_rows] = gather_layer([middle_grad.astype(BF)], 8, "gather_branch")
    feed_sums = [reduce_layers(grad_packs[0], layers)]
    branch_rows = branch_rows.reshape(all_rows, model)

    mixed_grad = (
        matmul("rd,df->rf", branch_rows, out_slice)
        .astype(BF)
        .reshape(GROUP, count_rows, heads, HEAD_DIM)
    )
    probs_back = jnp.exp(masked_scores() - logsum)
    prob_grad = matmul("gqhd,gkd->ghqk", mixed_grad, value_all)
    score_grad = (
        probs_back * (prob_grad - jnp.sum(probs_back * prob_grad, axis=-1, keepdims=True))
    ).astype(BF)
    value_terms = matmul("ghqk,gqhd->gkd", probs, mixed_grad)
    query_rot_grad = matmul("ghqk,gkd->gqhd", score_grad, key_all) * scale
    key_terms = matmul("ghqk,gqhd->gkd", score_grad, query_rot) * scale
    query_grad = (
        rotate(query_rot_grad, cosines[:, :, None, :], -sines[:, :, None, :])
        .reshape(all_rows, head_columns)
        .astype(BF)
    )
    latent_terms = matmul("rf,cf->rc", query_grad, query_slice)
    back_terms = jnp.concatenate(
        [latent_terms.reshape(GROUP, count_rows, rank), key_terms, value_terms], axis=2
    ).astype(BF)
    second_pack = after(grad_packs[1], feed_sums[0], score_grad)
    feed_sums.append(reduce_layers(second_pack, layers))
    back = reduce_layer(after(back_terms, second_pack), 9, "reduce_latent")
    grad_query = matmul("rc,rf->cf", latent_all, after(query_grad, back)).astype(BF)
    grad_out = matmul("rd,rf->df", after(branch_rows, back), mixed).astype(BF)
    head_pack = jnp.concatenate(
        [
            grad_query.reshape(layers, rank_span, head_columns),
            grad_out.reshape(layers, span, head_columns),
        ],
        axis=1,
    ).reshape(rank + model, head_columns)

    latent_normed_grad = back[:, :rank]
    keyval_grad = jnp.concatenate(
        [rotate(back[:, rank : rank + HEAD_DIM], cosine, -sine), back[:, rank + HEAD_DIM :]], axis=1
    ).astype(BF)
    unused_second, second_pull = jax.vjp(norm_rows, latent, second_gain)
    latent_back, latent_gain_grad = second_pull(latent_normed_grad)
    first_grad = jnp.concatenate([latent_back.astype(BF), keyval_grad], axis=1)
    normed_grad = matmul("re,de->rd", first_grad, first_weight)
    unused_first, first_pull = jax.vjp(norm_rows, inputs, first_gain)
    input_norm_grad, norm_gain_grad = first_pull(normed_grad)
    grad_tokens = (
        middle_grad + input_norm_grad + jnp.where(valid[:, None], 0.0, upstream)
    ).astype(BF)
    first_grad = after(first_grad, head_pack)
    gains = jnp.concatenate([norm_gain_grad, feed_gain_grad, latent_gain_grad])
    gains = jnp.pad(gains.reshape(-1, rank), ((0, 32 - gains.size // rank), (0, 0)))
    grad_all, gains_all = gather_layer([first_grad, gains.astype(BF)], 10, "gather_last")
    feed_terms = sum(
        matmul("rf,df->rd", after(hidden, grad_all), down) for hidden, down in hiddens
    ).astype(BF)
    feed = reduce_layer(
        feed_terms.reshape(GROUP, count_rows, model), 11, "reduce_feed"
    )
    output = jnp.where(valid[:, None], middle + feed, inputs).astype(BF)

    head_pack = after(head_pack, grad_all)
    head_sum = reduce_layers(after(head_pack, *feed_sums), layers)
    normed_rows = normed_rows.reshape(all_rows, model)
    gain_sums = jnp.sum(gains_all.astype(F32), axis=0)
    lines = model // rank
    columns = wide // QUAD
    grad_slice = lax.dynamic_slice_in_dim(
        grad_all.reshape(all_rows, wide), quad * columns, columns, axis=1
    )
    grad_first = matmul("rd,re->de", normed_rows, grad_slice).astype(BF)
    grad_first = lax.dynamic_index_in_dim(
        grad_first.reshape(layers * QUAD, PAIR, half, columns), hid, 1, keepdims=False
    )
    small_sums = jnp.concatenate(
        [
            gain_sums[:lines].reshape(layers, span),
            gain_sums[lines : 2 * lines].reshape(layers, span),
            gain_sums[2 * lines].reshape(layers, rank_span),
        ],
        axis=1,
    )
    flat = 16 * columns
    small_sums = jnp.pad(small_sums, ((0, 0), (0, flat - small_sums.shape[1])))
    quads = [[z * QUAD + q for q in range(QUAD)] for z in range(layers)]
    feed_own = lax.all_to_all(
        after(jnp.concatenate(feed_sums, axis=1), grad_all).reshape(QUAD, part, -1),
        "batch",
        0,
        0,
        axis_index_groups=quads,
        tiled=True,
    )
    last_pack = jnp.concatenate(
        [
            grad_first.reshape(layers, QUAD * half, columns),
            small_sums.reshape(layers, 16, columns).astype(BF),
        ],
        axis=1,
    ).reshape(layers * (QUAD * half + 16), columns)
    grads = join(feed_own, [high - low for low, high in chunks])
    last_pack = after(after(last_pack, feed), head_sum)
    last_sum = reduce_layers(last_pack, layers)
    small_sum = last_sum[QUAD * half :].astype(F32).reshape(-1)

    query_sum, out_sum = head_sum[:rank_span], head_sum[rank_span:]
    groups = [[z * GROUP + i for i in range(GROUP)] for z in range(layers)]
    head_own = lax.all_to_all(
        jnp.repeat(
            jnp.concatenate(
                [
                    query_sum.reshape(QUAD, rank_part, head_columns),
                    out_sum.reshape(QUAD, part, head_columns),
                ],
                axis=1,
            ),
            PAIR,
            axis=0,
        ),
        ("batch", "hid"),
        0,
        0,
        axis_index_groups=groups,
        tiled=True,
    )
    down_own, pair_own = settle(
        [last_sum],
        [rows_of(0, half)],
        [
            lambda ref, i: ref.at[
                pl.ds(pl.multiple_of(lax.rem(i, PAIR) * half, half), half),
                pl.ds(pl.multiple_of(i // PAIR * columns, columns), columns),
            ],
        ],
        [(part, wide)],
        [(0, 0, rank), (0, rank, wide)],
        14,
        "settle_last",
    )
    query_own, out_own = spread(after(head_own, down_own), rank_part)
    return (
        output,
        grad_tokens,
        lax.dynamic_slice_in_dim(small_sum, quad * part, part),
        down_own,
        lax.dynamic_slice_in_dim(small_sum, 2 * span + quad * rank_part, rank_part),
        query_own,
        pair_own,
        out_own,
        lax.dynamic_slice_in_dim(small_sum, span + quad * part, part),
        *grads,
    )


def solution(mesh):
    placed = (
        P(("batch", "hid"), None),
        P(("batch", "hid"), None),
        P("batch"),
        P("batch", None),
        P("batch"),
        P("batch", None),
        P("batch", None),
        P("batch", None),
        P("batch"),
        P("batch", "hid"),
        P("batch", "hid"),
        P("batch", "hid"),
        P(("batch", "hid"), None),
    )
    return jax.shard_map(
        functools.partial(per_device, mesh.shape["batch"] // QUAD),
        mesh=mesh,
        in_specs=placed,
        out_specs=(
            P(("batch", "hid"), None),
            P(("batch", "hid"), None),
            P("batch"),
            P("batch", None),
            P("batch"),
            P("batch", None),
            P("batch", None),
            P("batch", None),
            P("batch"),
            P("batch", "hid"),
            P("batch", "hid"),
            P("batch", "hid"),
        ),
        check_vma=False,
    )
```

```python
import functools

import jax
import jax.numpy as jnp
from jax import lax
from jax.experimental import pallas as pl
from jax.experimental.pallas import tpu as pltpu
from jax.sharding import PartitionSpec as P

HEADS = 16
HEAD_DIM = 256


EPS = 1e-05
ROPE_BASE = 10000.0
NEGATIVE = -1e30

QUAD = 4
PAIR = 2
GROUP = QUAD * PAIR
EXTRA = 24
MESH = pl.DeviceIdType.MESH
BF = jnp.bfloat16
F32 = jnp.float32


def matmul(spec, left, right):
    return jnp.einsum(spec, left, right, preferred_element_type=F32)


def norm_rows(values, gain):
    return values * lax.rsqrt(jnp.mean(values * values, axis=-1, keepdims=True) + EPS) * gain


def rotate(values, cosine, sine):
    half = values.shape[-1] // 2
    first = values[..., :half]
    second = values[..., half:]
    return jnp.concatenate(
        [first * cosine - second * sine, second * cosine + first * sine], axis=-1
    )


def layout(row_lengths, count_rows):
    slots = jnp.arange(row_lengths.shape[0], dtype=jnp.int32)
    ends = jnp.sum(jnp.where(slots[None, :] <= slots[:, None], row_lengths[None, :], 0), axis=1)
    starts = ends - row_lengths
    places = jnp.arange(count_rows, dtype=jnp.int32)
    segment = jnp.sum((places[:, None] >= ends[None, :]).astype(jnp.int32), axis=1)
    begins = jnp.concatenate([starts, ends[-1:]])
    labels = jnp.arange(begins.shape[0], dtype=jnp.int32)
    firsts = jnp.sum(jnp.where(segment[:, None] == labels[None, :], begins[None, :], 0), axis=1)
    position = places - firsts
    valid = places < ends[-1]
    allowed = (segment[:, None] == segment[None, :]) & (places[None, :] <= places[:, None])
    return (position, valid, allowed)


def angles_of(position, head_size):
    half = head_size // 2
    freqs = ROPE_BASE ** (-(jnp.arange(half, dtype=F32) * 2.0) / head_size)
    angle = position.astype(F32)[..., None] * freqs
    return (jnp.cos(angle), jnp.sin(angle))


def place():
    batch = lax.axis_index("batch")
    quad = lax.rem(batch, QUAD)
    return batch - quad, quad, lax.axis_index("hid")


def flip(quad, bits):
    core = lax.rem(quad, 2)
    chip = quad - core
    if bits & 1:
        core = 1 - core
    if bits & 2:
        chip = 2 - chip
    return chip + core


def after(value, *others):
    return lax.optimization_barrier((value, *others))[0]


def meet(peers):
    barrier = pltpu.get_barrier_semaphore()
    for peer in peers:
        pl.semaphore_signal(barrier, inc=1, device_id=peer, device_id_type=MESH)
    pl.semaphore_wait(barrier, len(peers))


def ways_of(base, quad, hid):
    def spot(bits, turn):
        return (flip(quad, bits), 1 - hid if turn else hid)

    def address(f):
        q, h = spot(*f)
        return (base + q, h)

    def index(f):
        q, h = spot(*f)
        return q * PAIR + h

    return address, index


ACROSS, ALONG, CORNER, MATE, SELF = (2, 0), (0, 1), (2, 1), (1, 0), (0, 0)


def gather_kernel(count, cuts, puts, *refs):
    ins, outs = refs[:count], refs[count : 2 * count]
    local_sem, send_sem, recv_sem = refs[2 * count :]
    base, quad, hid = place()
    address, index = ways_of(base, quad, hid)
    meet([address(f) for f in (ACROSS, ALONG, MATE)])

    def part(ref, i, h):
        cut, size = cuts[i]
        return ref.at[pl.ds(0, cut)] if h == 0 else ref.at[pl.ds(cut, size - cut)]

    def spot(i, f):
        return puts[i](outs[i], index(f))

    def copy(i, j, source, target, f):
        return pltpu.make_async_remote_copy(
            src_ref=source,
            dst_ref=target,
            send_sem=send_sem.at[i, j],
            recv_sem=recv_sem.at[i, j],
            device_id=address(f),
            device_id_type=MESH,
        )

    started = []

    def start(one):
        one.start()
        started.append(one)

    for i in range(count):
        for j, f, h in ((0, ACROSS, 0), (3, ALONG, 1), (1, ACROSS, 1), (2, ALONG, 0)):
            start(copy(i, j, part(ins[i], i, h), part(spot(i, SELF), i, h), f))
        start(copy(i, 6, ins[i], spot(i, SELF), MATE))
        pltpu.make_async_copy(ins[i], spot(i, SELF), local_sem.at[i]).start()

    def arrived(i, j, where, f):
        copy(i, j, where, where, f).wait_recv()

    for i in range(count):
        where = part(spot(i, ACROSS), i, 0)
        arrived(i, 0, where, ACROSS)
        start(copy(i, 4, where, where, ALONG))
        where = part(spot(i, ALONG), i, 1)
        arrived(i, 3, where, ALONG)
        start(copy(i, 5, where, where, ACROSS))
        arrived(i, 1, part(spot(i, ACROSS), i, 1), ACROSS)
        where = spot(i, ACROSS)
        start(copy(i, 7, where, where, MATE))
        arrived(i, 2, part(spot(i, ALONG), i, 0), ALONG)
        where = spot(i, ALONG)
        start(copy(i, 8, where, where, MATE))
    for i in range(count):
        where = part(spot(i, CORNER), i, 0)
        arrived(i, 4, where, ALONG)
        start(copy(i, 9, where, where, MATE))
        where = part(spot(i, CORNER), i, 1)
        arrived(i, 5, where, ACROSS)
        start(copy(i, 10, where, where, MATE))
    for i in range(count):
        pltpu.make_async_copy(ins[i], spot(i, SELF), local_sem.at[i]).wait()
        arrived(i, 6, spot(i, MATE), MATE)
        arrived(i, 7, spot(i, (ACROSS[0] ^ 1, ACROSS[1])), MATE)
        arrived(i, 8, spot(i, (ALONG[0] ^ 1, ALONG[1])), MATE)
        corner = spot(i, (CORNER[0] ^ 1, CORNER[1]))
        arrived(i, 9, part(corner, i, 0), MATE)
        arrived(i, 10, part(corner, i, 1), MATE)
    for one in started:
        one.wait_send()


def stacked(ref, place):
    return ref.at[place]


def inside(ref, place):
    return ref.at[:, place]


def gather_layer(arrays, ident, name, puts=None):
    count = len(arrays)
    puts = puts or [stacked] * count
    shapes = [
        (GROUP,) + a.shape if p is stacked else (a.shape[0], GROUP) + a.shape[1:]
        for a, p in zip(arrays, puts)
    ]
    cuts = [
        (a.shape[0] // 2 if a.ndim > 2 else a.shape[0] // 32 * 16, a.shape[0]) for a in arrays
    ]
    moved = sum(a.size * 2 * GROUP for a in arrays)
    return pl.pallas_call(
        functools.partial(gather_kernel, count, cuts, puts),
        out_shape=[jax.ShapeDtypeStruct(s, a.dtype) for s, a in zip(shapes, arrays)],
        in_specs=[pl.BlockSpec(memory_space=pl.ANY)] * count,
        out_specs=[pl.BlockSpec(memory_space=pl.ANY)] * count,
        scratch_shapes=[
            pltpu.SemaphoreType.DMA((count,)),
            pltpu.SemaphoreType.DMA((count, 11)),
            pltpu.SemaphoreType.DMA((count, 11)),
        ],
        compiler_params=pltpu.CompilerParams(collective_id=ident, has_side_effects=True),
        cost_estimate=pl.CostEstimate(flops=0, bytes_accessed=16 * moved, transcendentals=0),
        name=name,
    )(*arrays)


def reduce_kernel(in_ref, out_ref, own, mate_in, sums, relay, far_in, local_sem, send_sem, recv_sem):
    base, quad, hid = place()
    address, index = ways_of(base, quad, hid)
    rows = out_ref.shape[0]
    half = rows // 2
    step = 16
    ways = [CORNER, ACROSS, ALONG, SELF]
    meet([address(f) for f in (ACROSS, ALONG, MATE)])
    started = []

    def copy(j, source, target, f):
        return pltpu.make_async_remote_copy(
            src_ref=source,
            dst_ref=target,
            send_sem=send_sem.at[j],
            recv_sem=recv_sem.at[j],
            device_id=address(f),
            device_id_type=MESH,
        )

    def start(one):
        one.start()
        started.append(one)
        return one

    to_mate, local = [], []
    for j, f in enumerate(ways):
        to_mate.append(start(copy(j, in_ref.at[index((f[0] ^ 1, f[1]))], mate_in.at[j], MATE)))
        local.append(pltpu.make_async_copy(in_ref.at[index(f)], own.at[j], local_sem.at[j]))
        local[-1].start()

    def ready(j):
        local[j].wait()
        to_mate[j].wait_recv()

    def add(j, first, count, more=None):
        def body(r, carry):
            at = pl.ds(pl.multiple_of(first + r * step, step), step)
            value = own[j, at, :].astype(F32) + mate_in[j, at, :].astype(F32)
            if more is not None:
                value += more[pl.ds(pl.multiple_of(r * step, step), step), :].astype(F32)
            sums[j, at, :] = value.astype(BF)
            return carry

        lax.fori_loop(0, count // step, body, 0)

    low, high = pl.ds(0, half), pl.ds(half, half)
    ready(0)
    add(0, 0, half)
    by_across = start(copy(4, sums.at[0, low], relay.at[0], ACROSS))
    add(0, half, half)
    by_along = start(copy(5, sums.at[0, high], relay.at[1], ALONG))
    ready(1)
    add(1, 0, half)
    across_low = start(copy(6, sums.at[1, low], far_in.at[0, low], ACROSS))
    ready(2)
    add(2, half, half)
    along_high = start(copy(7, sums.at[2, high], far_in.at[1, high], ALONG))
    by_across.wait_recv()
    add(2, 0, half, relay.at[0])
    along_low = start(copy(8, sums.at[2, low], far_in.at[1, low], ALONG))
    by_along.wait_recv()
    add(1, half, half, relay.at[1])
    across_high = start(copy(9, sums.at[1, high], far_in.at[0, high], ACROSS))
    ready(3)
    for one in (across_low, along_high, along_low, across_high):
        one.wait_recv()

    def total(r, carry):
        at = pl.ds(pl.multiple_of(r * step, step), step)
        out_ref[at, :] = (
            own[3, at, :].astype(F32)
            + mate_in[3, at, :].astype(F32)
            + far_in[0, at, :].astype(F32)
            + far_in[1, at, :].astype(F32)
        )
        return carry

    lax.fori_loop(0, rows // step, total, 0)
    for one in started:
        one.wait_send()


def reduce_layer(blocks, ident, name):
    rows, columns = blocks.shape[1:]
    return pl.pallas_call(
        reduce_kernel,
        out_shape=jax.ShapeDtypeStruct((rows, columns), F32),
        in_specs=[pl.BlockSpec(memory_space=pl.ANY)],
        out_specs=pl.BlockSpec(memory_space=pltpu.VMEM),
        scratch_shapes=[
            pltpu.VMEM((4, rows, columns), BF),
            pltpu.VMEM((4, rows, columns), BF),
            pltpu.VMEM((3, rows, columns), BF),
            pltpu.VMEM((2, rows // 2, columns), BF),
            pltpu.VMEM((2, rows, columns), BF),
            pltpu.SemaphoreType.DMA((4,)),
            pltpu.SemaphoreType.DMA((10,)),
            pltpu.SemaphoreType.DMA((10,)),
        ],
        compiler_params=pltpu.CompilerParams(
            collective_id=ident, has_side_effects=True, vmem_limit_bytes=40 * 2**20
        ),
        cost_estimate=pl.CostEstimate(
            flops=0, bytes_accessed=16 * blocks.size * 2, transcendentals=0
        ),
        name=name,
    )(blocks)


def swap_kernel(count, homes, takes, puts, flips, *refs):
    outs = refs[count:-3]
    ins, outs = refs[:count], [outs[home] for home in homes]
    local_sem, send_sem, recv_sem = refs[-3:]
    base, quad, hid = place()
    address, index = ways_of(base, quad, hid)
    meet([address(f) for f in flips])

    def copy(i, j, f, owner):
        return pltpu.make_async_remote_copy(
            src_ref=takes[i](ins[i], index(f)),
            dst_ref=puts[i](outs[i], owner),
            send_sem=send_sem.at[i, j],
            recv_sem=recv_sem.at[i, j],
            device_id=address(f),
            device_id_type=MESH,
        )

    me = index(SELF)
    for i in range(count):
        for j, f in enumerate(flips):
            copy(i, j, f, me).start()
        pltpu.make_async_copy(takes[i](ins[i], me), puts[i](outs[i], me), local_sem.at[i]).start()
    for i in range(count):
        pltpu.make_async_copy(takes[i](ins[i], me), puts[i](outs[i], me), local_sem.at[i]).wait()
        for j, f in enumerate(flips):
            copy(i, j, f, index(f)).wait_recv()
    for i in range(count):
        for j, f in enumerate(flips):
            copy(i, j, f, me).wait_send()


QUAD_FLIPS = ((3, 0), (2, 0), (1, 0))
ALL_FLIPS = ((3, 1), (2, 1), (3, 0), (2, 0), (1, 1), (0, 1), (1, 0))


def swap(arrays, takes, puts, shapes, flips, ident, name, homes=None):
    count = len(arrays)
    homes = homes or range(count)
    moved = sum(a.size * 2 for a in arrays)
    return pl.pallas_call(
        functools.partial(swap_kernel, count, homes, takes, puts, flips),
        out_shape=[jax.ShapeDtypeStruct(s, BF) for s in shapes],
        in_specs=[pl.BlockSpec(memory_space=pl.ANY)] * count,
        out_specs=[pl.BlockSpec(memory_space=pl.ANY)] * len(shapes),
        scratch_shapes=[
            pltpu.SemaphoreType.DMA((count,)),
            pltpu.SemaphoreType.DMA((count, len(flips))),
            pltpu.SemaphoreType.DMA((count, len(flips))),
        ],
        compiler_params=pltpu.CompilerParams(collective_id=ident, has_side_effects=True),
        cost_estimate=pl.CostEstimate(flops=0, bytes_accessed=32 * moved, transcendentals=0),
        name=name,
    )(*arrays)


def spread_kernel(blocks_ref, first_ref, second_ref):
    count = first_ref.shape[0]
    columns = blocks_ref.shape[2]
    for i in range(blocks_ref.shape[0]):
        at = pl.ds(i * columns, columns)
        first_ref[:, at] = blocks_ref[i, :count, :].astype(F32)
        second_ref[:, at] = blocks_ref[i, count:, :].astype(F32)


def spread(blocks, count):
    n, rows, columns = blocks.shape
    return pl.pallas_call(
        spread_kernel,
        grid=(n // 2,),
        in_specs=[pl.BlockSpec((2, rows, columns), lambda i: (i, 0, 0))],
        out_specs=[
            pl.BlockSpec((count, 2 * columns), lambda i: (0, i)),
            pl.BlockSpec((rows - count, 2 * columns), lambda i: (0, i)),
        ],
        out_shape=[
            jax.ShapeDtypeStruct((count, n * columns), F32),
            jax.ShapeDtypeStruct((rows - count, n * columns), F32),
        ],
        cost_estimate=pl.CostEstimate(
            flops=0, bytes_accessed=6 * blocks.size, transcendentals=0
        ),
        name="spread_heads",
    )(blocks)


def settle_kernel(count, takes, puts, results, *refs):
    ins, outs = refs[:count], refs[count : count + len(results)]
    landed = refs[count + len(results) : 2 * count + len(results)]
    local_sem, send_sem, recv_sem = refs[2 * count + len(results) :]
    base, quad, hid = place()
    address, index = ways_of(base, quad, hid)
    meet([address(f) for f in ALL_FLIPS])

    def copy(i, j, f, owner):
        return pltpu.make_async_remote_copy(
            src_ref=takes[i](ins[i], index(f) // PAIR),
            dst_ref=puts[i](landed[i], owner),
            send_sem=send_sem.at[i, j],
            recv_sem=recv_sem.at[i, j],
            device_id=address(f),
            device_id_type=MESH,
        )

    def local(i):
        return pltpu.make_async_copy(
            takes[i](ins[i], quad), puts[i](landed[i], index(SELF)), local_sem.at[i]
        )

    for i in range(count):
        for j, f in enumerate(ALL_FLIPS):
            copy(i, j, f, index(SELF)).start()
        local(i).start()
    for i in range(count):
        local(i).wait()
        for j, f in enumerate(ALL_FLIPS):
            copy(i, j, f, index(f)).wait_recv()
    step = 16
    for (i, begin, end), out in zip(results, outs):

        def body(r, carry, i=i, begin=begin, end=end, out=out):
            at = pl.ds(pl.multiple_of(r * step, step), step)
            out[at, :] = landed[i][at, begin:end].astype(F32)
            return carry

        lax.fori_loop(0, out.shape[0] // step, body, 0)
    for i in range(count):
        for j, f in enumerate(ALL_FLIPS):
            copy(i, j, f, index(SELF)).wait_send()


def settle(arrays, takes, puts, shapes, results, ident, name):
    count = len(arrays)
    moved = sum(s[0] * s[1] for s in shapes)
    return pl.pallas_call(
        functools.partial(settle_kernel, count, takes, puts, results),
        out_shape=[jax.ShapeDtypeStruct((shapes[i][0], e - b), F32) for i, b, e in results],
        in_specs=[pl.BlockSpec(memory_space=pl.ANY)] * count,
        out_specs=[pl.BlockSpec(memory_space=pltpu.VMEM)] * len(results),
        scratch_shapes=[pltpu.VMEM(s, BF) for s in shapes]
        + [
            pltpu.SemaphoreType.DMA((count,)),
            pltpu.SemaphoreType.DMA((count, len(ALL_FLIPS))),
            pltpu.SemaphoreType.DMA((count, len(ALL_FLIPS))),
        ],
        compiler_params=pltpu.CompilerParams(
            collective_id=ident, has_side_effects=True, vmem_limit_bytes=24 * 2**20
        ),
        cost_estimate=pl.CostEstimate(flops=0, bytes_accessed=64 * moved, transcendentals=0),
        name=name,
    )(*arrays)


def rows_of(begin, count):
    return lambda ref, q: ref.at[pl.ds(pl.multiple_of(begin + q * count, 16), count)]


def join_kernel(widths, blocks_ref, *outs):
    total = sum(widths)
    for i, out in enumerate(outs):
        for q in range(QUAD):
            begin, source = q * total, 0
            for width in widths:
                at = source + i * width
                out[:, begin : begin + width] = blocks_ref[q, :, at : at + width].astype(F32)
                begin += width
                source += 3 * width


def join(blocks, widths):
    rows, columns = blocks.shape[1], QUAD * sum(widths)
    strip = min(rows, 32)
    return pl.pallas_call(
        functools.partial(join_kernel, widths),
        grid=(rows // strip,),
        in_specs=[pl.BlockSpec((QUAD, strip, blocks.shape[2]), lambda i: (0, i, 0))],
        out_specs=[pl.BlockSpec((strip, columns), lambda i: (i, 0))] * 3,
        out_shape=[jax.ShapeDtypeStruct((rows, columns), F32)] * 3,
        cost_estimate=pl.CostEstimate(
            flops=0, bytes_accessed=18 * rows * columns, transcendentals=0
        ),
        name="join_feed",
    )(blocks)


def columns_of(width):
    return lambda ref, i: ref.at[:, pl.ds(pl.multiple_of(i * width, width), width)]


def quad_of(ref, i):
    return ref.at[i // PAIR]


def layer_groups(layers):
    return [[z * QUAD + q for z in range(layers)] for q in range(QUAD)]


def gather_layers(unit, layers):
    return lax.all_gather(
        unit, "batch", axis=0, tiled=True, axis_index_groups=layer_groups(layers)
    )


def reduce_layers(blocks, layers):
    return lax.psum_scatter(
        blocks,
        "batch",
        scatter_dimension=0,
        tiled=True,
        axis_index_groups=layer_groups(layers),
    )


def per_device(
    layers,
    tokens,
    lengths,
    attention_gain,
    query_down,
    query_gain,
    query_up,
    key_value,
    output_weight,
    feed_gain,
    gate_weight,
    up_weight,
    down_weight,
    cotangent,
):
    count_rows, model = tokens.shape
    part, rank = query_down.shape
    rank_part = query_up.shape[0]
    half = part // PAIR
    wide = rank + key_value.shape[1]
    all_rows = GROUP * count_rows
    heads = HEADS // GROUP
    head_columns = heads * HEAD_DIM
    units = gate_weight.shape[1] // QUAD
    cut = -(-units // 256) * 128
    chunks = [(0, cut), (cut, units)]
    scale = HEAD_DIM ** (-0.5)
    base, quad, hid = place()
    layer = base // QUAD
    me = quad * PAIR + hid
    span = QUAD * part
    rank_span = QUAD * rank_part

    first_pack = jnp.concatenate(
        [
            lax.dynamic_slice_in_dim(
                jnp.concatenate([query_down, key_value], axis=1), hid * half, half, axis=0
            ),
            jnp.pad(
                jnp.concatenate([attention_gain, query_gain, feed_gain, lengths[0].astype(BF)])[None],
                ((0, EXTRA - 1), (0, wide - 2 * part - rank_part - lengths.shape[1])),
            ),
        ],
        axis=0,
    )
    first_slots = gather_layers(first_pack, layers).reshape(layers, half + EXTRA, wide)
    packs = [
        jnp.concatenate(
            [
                w.reshape(part, QUAD, units)[:, :, low:high]
                for w in (gate_weight, up_weight, down_weight)
            ],
            axis=2,
        ).transpose(1, 0, 2)
        for low, high in chunks
    ]
    folds = part // rank_part
    thin = head_columns // folds
    feed_end = head_columns + packs[0].shape[2]

    def fold_of(fold):
        def take(ref, i):
            begin = pl.multiple_of(i * head_columns, head_columns) + fold * thin
            return ref.at[:, pl.ds(begin, thin)]

        def put(ref, i):
            rows = pl.ds(fold * rank_part, rank_part)
            return ref.at[i // PAIR, rows, pl.ds(feed_end, thin)]

        return take, put

    fold_ways = [fold_of(fold) for fold in range(folds)]
    [head_unit] = swap(
        [output_weight, packs[0]] + [query_up] * folds,
        [columns_of(head_columns), quad_of] + [take for take, put in fold_ways],
        [
            lambda ref, i: ref.at[i // PAIR, :, pl.ds(0, head_columns)],
            lambda ref, i: ref.at[i // PAIR, :, pl.ds(head_columns, feed_end - head_columns)],
        ]
        + [put for take, put in fold_ways],
        [(QUAD, part, feed_end + thin)],
        QUAD_FLIPS,
        1,
        "swap_heads",
        [0] * (2 + folds),
    )
    head_all = gather_layers(head_unit.reshape(span, -1), layers)
    out_slice = head_all[:, :head_columns]
    feed_weights = [head_all[:, head_columns:feed_end]]
    query_slice = (
        head_all[:, feed_end:]
        .reshape(layers * QUAD, folds, rank_part, thin)
        .transpose(0, 2, 1, 3)
        .reshape(rank, head_columns)
    )
    [feed_unit] = swap(
        [after(packs[1], head_unit)],
        [quad_of],
        [quad_of],
        [packs[1].shape],
        QUAD_FLIPS,
        2,
        "swap_feed",
    )

    small_width = -(-(2 * part + rank_part + lengths.shape[1]) // 128) * 128
    first_weight, small = gather_layer(
        [first_slots[:, :half], first_slots[:, half : half + 16, :small_width]],
        3,
        "gather_first",
        [inside, stacked],
    )
    feed_weights.append(gather_layers(after(feed_unit, first_weight).reshape(span, -1), layers))
    first_weight = first_weight.reshape(model, wide)
    small = small[:, :, 0].transpose(1, 0, 2)
    first_gain = small[:, ::PAIR, :part].reshape(model).astype(F32)
    second_gain = small[:, ::PAIR, part : part + rank_part].reshape(rank).astype(F32)
    third_gain = (
        small[:, ::PAIR, part + rank_part : 2 * part + rank_part].reshape(model).astype(F32)
    )
    begin = 2 * part + rank_part
    all_lengths = small[:, :, begin : begin + lengths.shape[1]].astype(jnp.int32)
    all_lengths = lax.dynamic_index_in_dim(all_lengths, layer, 0, keepdims=False)

    inputs = tokens.astype(F32)
    upstream = cotangent.astype(F32)
    position, valid, allowed_own = layout(lengths[0], count_rows)
    cosine, sine = angles_of(position, HEAD_DIM)
    normed = norm_rows(inputs, first_gain).astype(BF)
    first = matmul("rd,de->re", normed, first_weight)
    latent = first[:, :rank]
    keyvals = first[:, rank:]
    latent_normed = norm_rows(latent, second_gain).astype(BF)
    key_rot = rotate(keyvals[:, :HEAD_DIM], cosine, sine).astype(BF)
    value_rows = keyvals[:, HEAD_DIM:].astype(BF)
    latent_all, key_all, value_all = gather_layer(
        [latent_normed, key_rot, value_rows], 4, "gather_latent"
    )
    kept = jnp.where(valid[:, None], upstream, 0.0)
    grad_rows, normed_rows = gather_layer(
        [after(kept.astype(BF), latent_all), normed], 15, "gather_upstream"
    )
    grad_rows = grad_rows.reshape(all_rows, model)
    query_slice = after(query_slice, grad_rows)
    latent_all = latent_all.reshape(all_rows, rank)

    positions, valids, allowed = jax.vmap(lambda one: layout(one, count_rows))(all_lengths)
    cosines, sines = angles_of(positions, HEAD_DIM)
    queries = matmul("rc,cf->rf", latent_all, query_slice).reshape(
        GROUP, count_rows, heads, HEAD_DIM
    )
    query_rot = rotate(queries, cosines[:, :, None, :], sines[:, :, None, :]).astype(BF)

    def masked_scores():
        raw = matmul("gqhd,gkd->ghqk", query_rot, key_all) * scale
        return jnp.where(allowed[:, None], raw, NEGATIVE)

    scores = masked_scores()
    highest = jnp.max(scores, axis=-1, keepdims=True)
    raised = jnp.exp(scores - highest)
    totals = jnp.sum(raised, axis=-1, keepdims=True)
    probs = (raised / totals).astype(BF)
    logsum = highest + jnp.log(totals)
    mixed = matmul("ghqk,gkd->gqhd", probs, value_all).reshape(all_rows, head_columns).astype(BF)
    branch_terms = matmul("rf,df->rd", mixed, out_slice).astype(BF)
    branch = reduce_layer(branch_terms.reshape(GROUP, count_rows, model), 5, "reduce_branch")
    middle = inputs + branch
    normed_ffn = norm_rows(middle, third_gain).astype(BF)
    [feed_rows] = gather_layer([normed_ffn], 6, "gather_feed")
    feed_rows = feed_rows.reshape(all_rows, model)

    hiddens = []
    ffn_terms = jnp.zeros((all_rows, model), F32)
    grad_packs = []
    for weights, (low, high) in zip(feed_weights, chunks):
        width = high - low
        gate_up, down = weights[:, : 2 * width], weights[:, 2 * width :]
        both = matmul("rd,df->rf", feed_rows, gate_up)
        gate, up = both[:, :width], both[:, width:]
        hidden_grad = matmul("rd,df->rf", grad_rows, down)
        sigma = jax.nn.sigmoid(gate)
        activated = gate * sigma
        slope = sigma * (1.0 + gate * (1.0 - sigma))
        hidden = (activated * up).astype(BF)
        both_grad = jnp.concatenate(
            [hidden_grad * up * slope, hidden_grad * activated], axis=1
        ).astype(BF)
        grad_both = matmul("rd,rf->df", feed_rows, both_grad).astype(BF)
        grad_down = matmul("rd,rf->df", grad_rows, hidden).astype(BF)
        grad_pack = jnp.concatenate([grad_both, grad_down], axis=1)
        grad_packs.append(grad_pack)
        feed_rows = after(feed_rows, grad_pack)
        both_grad = after(both_grad, grad_pack)
        ffn_terms = ffn_terms + matmul("rf,df->rd", both_grad, gate_up)
        hiddens.append((hidden, down))
    ffn_grad = reduce_layer(
        ffn_terms.astype(BF).reshape(GROUP, count_rows, model), 7, "reduce_ffn_grad"
    )
    unused_third, third_pull = jax.vjp(norm_rows, middle, third_gain)
    middle_norm_grad, feed_gain_grad = third_pull(ffn_grad)
    middle_grad = kept + middle_norm_grad
    [branch_rows] = gather_layer([middle_grad.astype(BF)], 8, "gather_branch")
    feed_sums = [reduce_layers(grad_packs[0], layers)]
    branch_rows = branch_rows.reshape(all_rows, model)

    mixed_grad = (
        matmul("rd,df->rf", branch_rows, out_slice)
        .astype(BF)
        .reshape(GROUP, count_rows, heads, HEAD_DIM)
    )
    probs_back = jnp.exp(masked_scores() - logsum)
    prob_grad = matmul("gqhd,gkd->ghqk", mixed_grad, value_all)
    score_grad = (
        probs_back * (prob_grad - jnp.sum(probs_back * prob_grad, axis=-1, keepdims=True))
    ).astype(BF)
    value_terms = matmul("ghqk,gqhd->gkd", probs, mixed_grad)
    query_rot_grad = matmul("ghqk,gkd->gqhd", score_grad, key_all) * scale
    key_terms = matmul("ghqk,gqhd->gkd", score_grad, query_rot) * scale
    query_grad = (
        rotate(query_rot_grad, cosines[:, :, None, :], -sines[:, :, None, :])
        .reshape(all_rows, head_columns)
        .astype(BF)
    )
    latent_terms = matmul("rf,cf->rc", query_grad, query_slice)
    back_terms = jnp.concatenate(
        [latent_terms.reshape(GROUP, count_rows, rank), key_terms, value_terms], axis=2
    ).astype(BF)
    second_pack = after(grad_packs[1], feed_sums[0], score_grad)
    feed_sums.append(reduce_layers(second_pack, layers))
    back = reduce_layer(after(back_terms, second_pack), 9, "reduce_latent")
    grad_query = matmul("rc,rf->cf", latent_all, after(query_grad, back)).astype(BF)
    grad_out = matmul("rd,rf->df", after(branch_rows, back), mixed).astype(BF)
    head_pack = jnp.concatenate(
        [
            grad_query.reshape(layers, QUAD, rank_part, head_columns),
            grad_out.reshape(layers, QUAD, part, head_columns),
        ],
        axis=2,
    ).reshape(rank + model, head_columns)

    latent_normed_grad = back[:, :rank]
    keyval_grad = jnp.concatenate(
        [rotate(back[:, rank : rank + HEAD_DIM], cosine, -sine), back[:, rank + HEAD_DIM :]], axis=1
    ).astype(BF)
    unused_second, second_pull = jax.vjp(norm_rows, latent, second_gain)
    latent_back, latent_gain_grad = second_pull(latent_normed_grad)
    first_grad = jnp.concatenate([latent_back.astype(BF), keyval_grad], axis=1)
    normed_grad = matmul("re,de->rd", first_grad, first_weight)
    unused_first, first_pull = jax.vjp(norm_rows, inputs, first_gain)
    input_norm_grad, norm_gain_grad = first_pull(normed_grad)
    grad_tokens = (
        middle_grad + input_norm_grad + jnp.where(valid[:, None], 0.0, upstream)
    ).astype(BF)
    first_grad = after(first_grad, head_pack)
    gains = jnp.concatenate([norm_gain_grad, feed_gain_grad, latent_gain_grad])
    gains = jnp.pad(gains.reshape(-1, rank), ((0, 32 - gains.size // rank), (0, 0)))
    grad_all, gains_all = gather_layer([first_grad, gains.astype(BF)], 10, "gather_last")
    feed_terms = sum(
        matmul("rf,df->rd", after(hidden, grad_all), down) for hidden, down in hiddens
    ).astype(BF)
    feed = reduce_layer(
        feed_terms.reshape(GROUP, count_rows, model), 11, "reduce_feed"
    )
    output = jnp.where(valid[:, None], middle + feed, inputs).astype(BF)

    head_pack = after(head_pack, grad_all)
    head_sum = reduce_layers(after(head_pack, *feed_sums), layers)
    normed_rows = normed_rows.reshape(all_rows, model)
    gain_sums = jnp.sum(gains_all.astype(F32), axis=0)
    lines = model // rank
    columns = wide // QUAD
    grad_slice = lax.dynamic_slice_in_dim(
        grad_all.reshape(all_rows, wide), quad * columns, columns, axis=1
    )
    grad_first = matmul("rd,re->de", normed_rows, grad_slice).astype(BF)
    grad_first = lax.dynamic_index_in_dim(
        grad_first.reshape(layers * QUAD, PAIR, half, columns), hid, 1, keepdims=False
    )
    small_sums = jnp.concatenate(
        [
            gain_sums[:lines].reshape(layers, span),
            gain_sums[lines : 2 * lines].reshape(layers, span),
            gain_sums[2 * lines].reshape(layers, rank_span),
        ],
        axis=1,
    )
    flat = 16 * columns
    small_sums = jnp.pad(small_sums, ((0, 0), (0, flat - small_sums.shape[1])))
    quads = [[z * QUAD + q for q in range(QUAD)] for z in range(layers)]
    feed_own = lax.all_to_all(
        after(jnp.concatenate(feed_sums, axis=1), grad_all).reshape(QUAD, part, -1),
        "batch",
        0,
        0,
        axis_index_groups=quads,
        tiled=True,
    )
    last_pack = jnp.concatenate(
        [
            grad_first.reshape(layers, QUAD * half, columns),
            small_sums.reshape(layers, 16, columns).astype(BF),
        ],
        axis=1,
    ).reshape(layers * (QUAD * half + 16), columns)
    grads = join(feed_own, [high - low for low, high in chunks])
    last_pack = after(after(last_pack, feed), head_sum)
    last_sum = reduce_layers(last_pack, layers)
    small_sum = last_sum[QUAD * half :].astype(F32).reshape(-1)

    groups = [[z * GROUP + i for i in range(GROUP)] for z in range(layers)]
    head_own = lax.all_to_all(
        jnp.repeat(
            head_sum.reshape(QUAD, rank_part + part, head_columns),
            PAIR,
            axis=0,
        ),
        ("batch", "hid"),
        0,
        0,
        axis_index_groups=groups,
        tiled=True,
    )
    down_own, pair_own = settle(
        [last_sum],
        [rows_of(0, half)],
        [
            lambda ref, i: ref.at[
                pl.ds(pl.multiple_of(lax.rem(i, PAIR) * half, half), half),
                pl.ds(pl.multiple_of(i // PAIR * columns, columns), columns),
            ],
        ],
        [(part, wide)],
        [(0, 0, rank), (0, rank, wide)],
        14,
        "settle_last",
    )
    query_own, out_own = spread(after(head_own, down_own), rank_part)
    return (
        output,
        grad_tokens,
        lax.dynamic_slice_in_dim(small_sum, quad * part, part),
        down_own,
        lax.dynamic_slice_in_dim(small_sum, 2 * span + quad * rank_part, rank_part),
        query_own,
        pair_own,
        out_own,
        lax.dynamic_slice_in_dim(small_sum, span + quad * part, part),
        *grads,
    )


def solution(mesh):
    placed = (
        P(("batch", "hid"), None),
        P(("batch", "hid"), None),
        P("batch"),
        P("batch", None),
        P("batch"),
        P("batch", None),
        P("batch", None),
        P("batch", None),
        P("batch"),
        P("batch", "hid"),
        P("batch", "hid"),
        P("batch", "hid"),
        P(("batch", "hid"), None),
    )
    return jax.shard_map(
        functools.partial(per_device, mesh.shape["batch"] // QUAD),
        mesh=mesh,
        in_specs=placed,
        out_specs=(
            P(("batch", "hid"), None),
            P(("batch", "hid"), None),
            P("batch"),
            P("batch", None),
            P("batch"),
            P("batch", None),
            P("batch", None),
            P("batch", None),
            P("batch"),
            P("batch", "hid"),
            P("batch", "hid"),
            P("batch", "hid"),
        ),
        check_vma=False,
    )
```
